32 devices in a mesh: seq: 2 (over x), clips: 16 (over z, y, core).
Axes of the slice: x: 2, y: 2, z: 4, core: 2. Of those that a mesh axis runs over, the one named last changes fastest.
Arguments:
- tokens: bfloat16 [2, 16384, 768], P('seq', 'clips'), may hold values from -6 to 6
- clip_class: int32 [16], P('clips'), may hold values from 0 to 1
- w_qkv: bfloat16 [768, 2304], P(('seq', 'clips')), may hold values from -0.21875 to 0.21875
- w_out: bfloat16 [768, 768], P(('seq', 'clips')), may hold values from -3.5 to 3.5
- w_up: bfloat16 [768, 3072], P(('seq', 'clips')), may hold values from -0.21875 to 0.21875
- w_down: bfloat16 [3072, 768], P(('seq', 'clips')), may hold values from -0.109375 to 0.109375
- norm_gains: bfloat16 [768, 2], P(('seq', 'clips')), may hold values from 0.5 to 1.5
- cotangent: bfloat16 [2, 16384, 768], P('seq', 'clips'), may hold values from -6 to 6
Outputs:
- output_tokens: bfloat16 [2, 16384, 768], P('seq', 'clips')
- grad_tokens: bfloat16 [2, 16384, 768], P('seq', 'clips')
- grad_w_qkv: float32 [768, 2304], P(('seq', 'clips'))
- grad_w_out: float32 [768, 768], P(('seq', 'clips'))
- grad_w_up: float32 [768, 3072], P(('seq', 'clips'))
- grad_w_down: float32 [3072, 768], P(('seq', 'clips'))
- grad_norm_gains: float32 [768, 2], P(('seq', 'clips'))
The draws below stay inside these ranges and needn't reach their ends.
Inputs may be any that keep to these rules, and one draw needn't show every extreme that they name: `clip_class`: 0 means the group holds clips of 512 patches, 1 clips of half as many; each clip's patches are split evenly in time over the seq axis.
All inputs are finite; a program needn't handle non-finite values.
Results may differ from the reference program's by a relative error of at most 0.014.
Values may be sent and summed in bfloat16 or wider, within the bound.
No kernel may reach another device: no remote copies, remote signals or barrier semaphores. Data moves between devices by JAX's collectives and lax.ppermute only.
A program may use at most 192 MiB of HBM per device.

```python
import jax
import jax.numpy as jnp
from jax import lax

D = 768
HEAD_DIM = 64
FF = 3072
CLIP = 512
TOK_DEV = 1024
SPLIT = 2
GROUPS = 16
TOKENS = 16384


def with_ends(values, stream_key, low, top_value):
    longest = values.shape.index(max(values.shape))
    spots = []
    for shift in (0, 1):
        where = [jax.random.randint(jax.random.fold_in(stream_key, axis), (), 0, length) for axis, length in enumerate(values.shape)]
        where[longest] = (where[longest] + shift) % values.shape[longest]
        spots.append(tuple(where))
    return values.at[spots[0]].set(low).at[spots[1]].set(top_value)


def strengthened(values, own_key, source, target, blocks, factor):
    owner, partner = [(jnp.arange(values.shape[dim]) // (values.shape[dim] // blocks)).reshape([-1 if axis == dim else 1 for axis in range(values.ndim)]) for dim in (source, target)]
    chosen = jax.random.permutation(own_key, blocks)[partner]
    strong = (owner == chosen) | (owner == (partner + blocks // 2) % blocks)
    return jnp.where(strong, factor * values, values)


def level_of(key, extent, cuts, least, largest):
    level = 1.0
    for dim, parts in cuts:
        draws = jax.random.uniform(jax.random.fold_in(jax.random.fold_in(key, 6), dim), (parts,), jnp.float32, least / len(cuts), largest / len(cuts))
        level = level * jnp.repeat(jnp.exp(draws), extent[dim] // parts).reshape((-1,) + (1,) * (len(extent) - 1 - dim))
    return level


def bell_draw(rng, dims, scale, most, cuts=(), held_as=jnp.bfloat16):
    level = level_of(rng, dims, cuts, -0.22, 0.18) if cuts else 1.0
    entries = jax.random.normal(rng, dims, jnp.float32) * scale * level
    return jnp.minimum(jnp.maximum(entries, -most), most).astype(held_as)


def bell_draw_with(rng, dims, width, reach, cuts, heavy, kind=jnp.bfloat16):
    values = width * jax.random.normal(rng, dims, jnp.float32)
    if cuts:
        values = values * level_of(rng, dims, cuts, -0.22, 0.18)
    return jnp.clip(strengthened(values, jax.random.fold_in(rng, 3), *heavy), -reach, reach).astype(kind)


def setup_inputs(seed: int = 0) -> dict:
    keys = jax.random.split(jax.random.key(seed), 9)
    return {
        "tokens": bell_draw(keys[0], (SPLIT, TOKENS, D), 1.0, 6.0, ((0, 2), (1, 16))),
        "clip_class": with_ends(jax.random.randint(keys[1], (GROUPS,), 0, 2), jax.random.fold_in(keys[1], 1), 0, 1).astype(jnp.int32),
        "w_qkv": bell_draw(keys[2], (D, 3 * D), D ** -0.5, 0.21875, ((0, 32),)),
        "w_out": bell_draw(keys[3], (D, D), (2 * D // CLIP) ** -0.5, 3.5, ((0, 32),)),
        "w_up": bell_draw(keys[4], (D, FF), D ** -0.5, 0.21875, ((0, 32),)),
        "w_down": bell_draw(keys[5], (FF, D), FF ** -0.5, 0.109375, ((0, 32),)),
        "norm_gains": jnp.clip(0.5 + 1.0 * jax.random.uniform(keys[6], (D, 2), jnp.float32) ** level_of(keys[6], (D, 2), ((0, 32),), -0.2, 0.2), 0.5, 1.5).astype(jnp.bfloat16),
        "cotangent": bell_draw_with(keys[7], (SPLIT, TOKENS, D), 1.0, 6.0, ((0, 2), (1, 16)), (1, 2, 16, 2.0)),
    }


@jax.custom_vjp
def low(v):
    return lax.optimization_barrier(v.astype(jnp.bfloat16)).astype(jnp.float32)

@jax.custom_vjp
def low_back(v):
    return v

def low_keep(v):
    return (low(v), None)

def low_pass(kept, grad):
    return (grad,)

def back_keep(v):
    return (v, None)

def back_low(kept, grad):
    return (low(grad),)
low.defvjp(low_keep, low_pass)
low_back.defvjp(back_keep, back_low)
EPSILON = 1e-05
NEG_LARGE = -1e+30

def dense_dot(left, right):
    return jnp.dot(left, right, precision=lax.Precision.HIGHEST)

def norm_apply(values, scales):
    average = lax.optimization_barrier(jnp.mean(values, axis=-1, keepdims=True))
    centered = values - average
    spread = lax.optimization_barrier(jnp.mean(centered * centered, axis=-1, keepdims=True))
    return centered * lax.rsqrt(spread + EPSILON) * scales

def group_forward(inputs, classes, w_qkv, w_out, w_up, w_down, norm_gains):
    row_count, model_width = inputs.shape
    head_count = model_width // HEAD_DIM
    score_scale = HEAD_DIM ** (-0.5)
    shard_rows = CLIP // SPLIT // (1 + classes)
    clip_numbers = jnp.arange(row_count, dtype=jnp.int32) % TOK_DEV // shard_rows
    normed_first = low(norm_apply(inputs, norm_gains[:, 0]))
    packed = low_back(low(dense_dot(normed_first, w_qkv)))
    queries = packed[:, :model_width].reshape(row_count, head_count, HEAD_DIM)
    key_heads = packed[:, model_width:2 * model_width].reshape(row_count, head_count, HEAD_DIM)
    value_heads = packed[:, 2 * model_width:].reshape(row_count, head_count, HEAD_DIM)
    block_rows = min(512, row_count)
    block_count = row_count // block_rows

    def attend(pieces):
        query_block, clip_block = pieces
        scores = low_back(jnp.einsum('qhe,khe->hqk', query_block, key_heads, precision=lax.Precision.HIGHEST) * score_scale)
        allowed = (clip_block[:, None] == clip_numbers[None, :])[None]
        scores = jnp.where(allowed, scores, NEG_LARGE)
        top_score = lax.optimization_barrier(jnp.max(scores, axis=-1, keepdims=True))
        raised = jnp.exp(scores - top_score)
        soft_weights = low(raised / lax.optimization_barrier(jnp.sum(raised, axis=-1, keepdims=True)))
        mixed_heads = jnp.einsum('hqk,khe->qhe', soft_weights, value_heads, precision=lax.Precision.HIGHEST)
        return mixed_heads.reshape(block_rows, model_width)
    mixed_blocks = lax.map(jax.checkpoint(attend), (queries.reshape(block_count, block_rows, head_count, HEAD_DIM), clip_numbers.reshape(block_count, block_rows)))
    attended = low_back(low(mixed_blocks.reshape(row_count, model_width)))
    hidden = inputs + low_back(dense_dot(attended, w_out))
    normed_second = low(norm_apply(hidden, norm_gains[:, 1]))
    up_values = low_back(dense_dot(normed_second, w_up))
    active = low(jax.nn.gelu(up_values, approximate=False))
    return hidden + low_back(dense_dot(active, w_down))

def reference(tokens, clip_class, w_qkv, w_out, w_up, w_down, norm_gains, cotangent):

    def regroup(array):
        shaped = array.astype(jnp.float32).reshape(SPLIT, GROUPS, TOK_DEV, D)
        return shaped.transpose(1, 0, 2, 3).reshape(GROUPS, SPLIT * TOK_DEV, D)

    def ungroup(array):
        shaped = array.reshape(GROUPS, SPLIT, TOK_DEV, D)
        return shaped.transpose(1, 0, 2, 3).reshape(SPLIT, GROUPS * TOK_DEV, D)
    weights_float = tuple((member.astype(jnp.float32) for member in (w_qkv, w_out, w_up, w_down, norm_gains)))

    def forward(inputs, float_qkv, float_out, float_up, float_down, float_gains):

        def one_group(pieces):
            return group_forward(pieces[0], pieces[1], float_qkv, float_out, float_up, float_down, float_gains)
        return lax.map(jax.checkpoint(one_group), (inputs, clip_class))
    result, pullback = jax.vjp(forward, regroup(tokens), *weights_float)
    gradients = pullback(regroup(cotangent))
    return (ungroup(result).astype(jnp.bfloat16), ungroup(gradients[0]).astype(jnp.bfloat16), gradients[1], gradients[2], gradients[3], gradients[4], gradients[5])
```

```python
import functools

import jax
import jax.numpy as jnp
from jax import lax
from jax.experimental import pallas as pl
from jax.experimental.pallas import tpu as pltpu
from jax.sharding import PartitionSpec as P

HEAD_DIM = 64
CLIP = 512
EPSILON = 1e-05
AXES = ("seq", "clips")
LOG2E = 1.4426950408889634
SCORE_SCALE = HEAD_DIM ** (-0.5)
BF16 = jnp.bfloat16
F32 = jnp.float32
VMEM_BYTES = 58 * 1024 * 1024


class Grid:
    def __init__(self, seq, clips):
        self.nx = seq
        self.clips = clips
        pairs = clips // 2
        bits = pairs.bit_length() - 1
        self.ny = 2 ** (bits // 3)
        self.nz = pairs // self.ny
        self.sizes = {"x": self.nx, "y": self.ny, "z": self.nz}
        self.chips = self.nx * self.ny * self.nz

    def index(self, x, z, y, c):
        return x * self.clips + (z * self.ny + y) * 2 + c

    def shift(self, axis, k):
        pairs = []
        for x in range(self.nx):
            for z in range(self.nz):
                for y in range(self.ny):
                    for c in range(2):
                        t = {"x": x, "y": y, "z": z}
                        t[axis] = (t[axis] + k) % self.sizes[axis]
                        pairs.append((self.index(x, z, y, c), self.index(t["x"], t["z"], t["y"], c)))
        return pairs

    def core_swap(self):
        return [(i, i ^ 1) for i in range(self.nx * self.clips)]

    def here(self):
        x = lax.axis_index("seq")
        rest = lax.axis_index("clips")
        return {"x": x, "z": rest // (2 * self.ny), "y": (rest // 2) % self.ny, "c": rest % 2}


def rel_of(grid, coords):
    return (coords["x"] * grid.ny + coords["y"]) * grid.nz + coords["z"]


def after(value, *earlier):
    return lax.optimization_barrier((value,) + earlier)[0]


def exchange(grid, parts, axis):
    moved = []
    for k in range(1, grid.sizes[axis]):
        for array, spots in parts:
            moved.append((lax.ppermute(array, AXES, grid.shift(axis, k)), [{**s, axis: k} for s in spots]))
    return moved


def joined_parts(parts):
    if len(parts) == 1:
        return parts[0]
    return (jnp.concatenate([a for a, _ in parts], axis=0), [s for _, spots in parts for s in spots])


def gather_along_z(grid, piece):
    parts = [(piece[None], [{"x": 0, "y": 0, "z": 0}])]
    parts = parts + exchange(grid, parts, "z")
    cut = max(1, (3 * len(parts)) // 4)
    return joined_parts(parts[:cut]), joined_parts(parts[cut:])


def scatter_sum(grid, mine, other):
    got = lax.ppermute(other, AXES, grid.core_swap())
    shape = (grid.ny, grid.nx, grid.nz) + mine.shape[1:]
    mine, got = mine.reshape(shape), got.reshape(shape)
    cut = max(1, (3 * grid.nz) // 4)
    kept = []
    for lo, hi, first in ((0, cut, "y"), (cut, grid.nz, "x")):
        second = "x" if first == "y" else "y"
        current = [mine[:, :, lo:hi], got[:, :, lo:hi]]
        for axis in (first, second):
            dim = 0 if axis == "y" else 1 - (first == "y")
            pieces = [
                [lax.index_in_dim(c, k, dim, keepdims=False) for c in current] for k in range(grid.sizes[axis])
            ]
            received = [
                lax.ppermute(add_all(pieces[k]).astype(BF16), AXES, grid.shift(axis, k))
                for k in range(1, grid.sizes[axis])
            ]
            current = pieces[0] + received
        kept.append(current)
    final = []
    for k in range(grid.nz):
        group = kept[0] if k < cut else kept[1]
        at = k if k < cut else k - cut
        total = add_all([c[at] for c in group])
        final.append(total if k == 0 else lax.ppermute(total.astype(BF16), AXES, grid.shift("z", k)))
    return add_all(final)


def add_all(items):
    total = items[0].astype(F32)
    for item in items[1:]:
        total = total + item.astype(F32)
    return total


def nn(a, b):
    return lax.dot_general(a, b, (((1,), (0,)), ((), ())), preferred_element_type=F32)


def nt(a, b):
    return lax.dot_general(a, b, (((1,), (1,)), ((), ())), preferred_element_type=F32)


def tn(a, b):
    return lax.dot_general(a, b, (((0,), (0,)), ((), ())), preferred_element_type=F32)


def normalized(values):
    centered = values - jnp.mean(values, axis=-1, keepdims=True)
    spread = jnp.mean(centered * centered, axis=-1, keepdims=True)
    root = lax.rsqrt(spread + EPSILON)
    return centered * root, root


def norm_back(z, root, scaled):
    return root * (
        scaled
        - jnp.mean(scaled, axis=-1, keepdims=True)
        - z * jnp.mean(scaled * z, axis=-1, keepdims=True)
    )


class Pieces:
    def __init__(self, chips, mine, theirs, fields):
        self.chips = chips
        self.arrays = [a for a, _ in mine] + [a for a, _ in theirs]
        self.spots = [s for _, s in mine] + [s for _, s in theirs]
        self.count_mine = len(mine)
        self.rows = self.arrays[0].shape[1]
        self.fields = fields

    def copies(self, wanted):
        total = 0
        for n, spots in enumerate(self.spots):
            for name, column, width, gain in self.fields:
                if name in wanted and not (gain and n >= self.count_mine):
                    total += len(spots)
        return total

    def start(self, refs, tab, wanted, sems, first):
        core = tab[2 * self.chips]
        started = {name: [] for name in wanted}
        n_sem = first
        for n, spots in enumerate(self.spots):
            for name, column, width, gain in self.fields:
                if name not in wanted or (gain and n >= self.count_mine):
                    continue
                for k, r in enumerate(spots):
                    row = pl.multiple_of(tab[r] * self.rows, 16)
                    if gain:
                        place = wanted[name].at[pl.ds(row, self.rows), :]
                    else:
                        side = core if n < self.count_mine else 1 - core
                        col = pl.multiple_of(side * width, 128)
                        place = wanted[name].at[pl.ds(row, self.rows), pl.ds(col, width)]
                    copy = pltpu.make_async_copy(
                        refs[n].at[k, :, column : column + width], place, sems.at[n_sem]
                    )
                    copy.start()
                    started[name].append(copy)
                    n_sem += 1
        return started


def wait_all(copies):
    for copy in copies:
        copy.wait()


def emit(value, side, first_chip, rows, mine, other, columns, tab, chips):
    rel = side ^ tab[2 * chips]
    height = value.shape[0]
    low = value.astype(BF16)

    def put(ref):
        if rows >= height:
            ref[0, pl.ds(first_chip, height), columns] = low
        else:
            for a in range(height // rows):
                ref[tab[chips + first_chip + a], :, columns] = low[a * rows : (a + 1) * rows]

    @pl.when(rel == 0)
    def _():
        put(mine)

    @pl.when(rel != 0)
    def _():
        put(other)


def place_of(row, rows, chips):
    return row if chips == 1 else row // rows


def input_kernel(pieces, n_refs, chips, tab, own, got, *refs):
    sources, refs = refs[:n_refs], refs[n_refs:]
    packed, normed, gains, w_qkv, gain_cols, sems = refs
    i = pl.program_id(0)
    steps = pl.num_programs(0)
    width = own.shape[1]

    @pl.when(i == 0)
    def _():
        started = pieces.start(sources, tab, {"gain": gain_cols, "qkv": w_qkv}, sems, 0)
        wait_all(started["gain"])
        pick = (
            lax.broadcasted_iota(jnp.int32, (8, 128), 0) == lax.broadcasted_iota(jnp.int32, (8, 128), 1)
        ).astype(BF16)
        gains[...] = nt(pick, gain_cols[...])
        wait_all(started["qkv"])

    x = jnp.where(i < steps // 2, own[...], got[...]).astype(F32)
    z, _ = normalized(x)
    low = (z * gains[0:1, :]).astype(BF16)
    normed[...] = low
    for c in range(3):
        cols = slice(c * width, (c + 1) * width)
        packed[:, cols] = nn(low, w_qkv[:, cols]).astype(BF16)


def pair_of(ref, n):
    return ref[:, 0, :, 128 * n : 128 * (n + 1)].reshape(512, 128)


def fill_bias(bias, short):
    row_clip = (lax.broadcasted_iota(jnp.int32, (512, 512), 0) // 128) % 2
    col_clip = (lax.broadcasted_iota(jnp.int32, (512, 512), 1) // 128) % 2
    apart = jnp.logical_and(row_clip != col_clip, short != 0)
    bias[...] = jnp.where(apart, -1e30, 0.0)


def attend_kernel(chips, tab, q_ref, k_ref, v_ref, attended, log_totals, bias):
    @pl.when(jnp.logical_and(pl.program_id(0) == 0, pl.program_id(1) == 0))
    def _():
        fill_bias(bias, tab[2 * chips + 1])

    lane = lax.broadcasted_iota(jnp.int32, (512, 128), 1)
    for n in range(2):
        q, k, v = pair_of(q_ref, n), pair_of(k_ref, n), pair_of(v_ref, n)
        v_t = v.T
        mixed = []
        for h in range(2):
            k_h = jnp.where((lane // 64) == h, k, jnp.zeros_like(k))
            s = nt(k_h, q) * (SCORE_SCALE * LOG2E) + bias[...]
            top_score = jnp.max(s, axis=0, keepdims=True)
            p = jnp.exp2(s - top_score)
            total = jnp.sum(p, axis=0, keepdims=True)
            mixed.append(nn(v_t[64 * h : 64 * h + 64, :], p.astype(BF16)) * (1.0 / total))
            log_totals[2 * n + h] = top_score + jnp.log2(total)
        out = jnp.concatenate(mixed, axis=0).T.astype(BF16)
        attended[:, 0, :, 128 * n : 128 * (n + 1)] = out.reshape(2, 256, 128)


ERF_P = 0.3275911 * (0.5**0.5)
ERF_A = (0.254829592 * 0.5, -0.284496736 * 0.5, 1.421413741 * 0.5, -1.453152027 * 0.5, 1.061405429 * 0.5)


def gelu_both(u):
    t = 1.0 / (1.0 + ERF_P * jnp.abs(u))
    bell = jnp.exp2(u * u * (-0.5 * LOG2E))
    poly = t * (ERF_A[0] + t * (ERF_A[1] + t * (ERF_A[2] + t * (ERF_A[3] + t * ERF_A[4]))))
    tail = poly * bell
    below = jnp.where(u < 0, tail, 1.0 - tail)
    return u * below, below + u * (bell * 0.3989422804014327)


def middle_kernel(pieces, n_refs, chips, tab, attended, own, got, gains, *refs):
    sources, refs = refs[:n_refs], refs[n_refs:]
    hidden, normed, w_out, sems = refs
    i = pl.program_id(0)

    @pl.when(i == 0)
    def _():
        wait_all(pieces.start(sources, tab, {"out": w_out}, sems, 0)["out"])

    x = jnp.where(i < pl.num_programs(0) // 2, own[...], got[...]).astype(F32)
    h = x + nn(attended[...], w_out[...])
    hidden[...] = h
    z, _ = normalized(h)
    normed[...] = (z * gains[1:2, :]).astype(BF16)


def up_kernel(pieces, n_refs, chips, rows_down, tab, normed, cot_own, cot_got, *refs):
    sources, refs = refs[:n_refs], refs[n_refs:]
    active, slope, down_mine, down_other, w_up, sems = refs
    half, width = cot_own.shape
    j = pl.program_id(0)

    @pl.when(j == 0)
    def _():
        wait_all(pieces.start(sources, tab, {"up": w_up}, sems, 0)["up"])

    cols = pl.ds(pl.multiple_of(j * width, 128), width)

    @pl.loop(0, 2 * half // 256)
    def _(i):
        rows = pl.ds(pl.multiple_of(i * 256, 256), 256)
        a, s = gelu_both(nn(normed[rows, :], w_up[:, cols]))
        active[rows, :] = a.astype(BF16)
        slope[rows, :] = s.astype(BF16)

    for m in range(2):
        piece = slice(384 * m, 384 * (m + 1))
        grad = tn(active[:half, piece], cot_own[...]) + tn(active[half:, piece], cot_got[...])
        start = place_of(width * j + 384 * m, rows_down, chips)
        emit(grad[:, : width // 2], 0, start, rows_down, down_mine, down_other, slice(None), tab, chips)
        emit(grad[:, width // 2 :], 1, start, rows_down, down_mine, down_other, slice(None), tab, chips)


def down_back_kernel(pieces, n_refs, chips, rows_up, tab, cot_own, cot_got, normed, slope, *refs):
    sources, refs = refs[:n_refs], refs[n_refs:]
    grad_up, up_mine, up_other, w_down, sems = refs
    half, width = cot_own.shape
    j = pl.program_id(0)
    steps = pl.num_programs(0)

    @pl.when(j == 0)
    def _():
        wait_all(pieces.start(sources, tab, {"down": w_down}, sems, 0)["down"])

    w_rows = pl.ds(pl.multiple_of(j * width, 256), width)
    for part, cot in enumerate((cot_own, cot_got)):
        @pl.loop(0, half // 256)
        def _(i):
            inner = pl.ds(pl.multiple_of(i * 256, 256), 256)
            rows = pl.ds(pl.multiple_of(part * half + i * 256, 256), 256)
            grad_up[rows, :] = (nt(cot[inner, :], w_down[w_rows, :]) * slope[rows, :].astype(F32)).astype(BF16)

    side = j // (steps // 2)
    offset = lax.rem(j, steps // 2) * width
    for m in range(2):
        grad = tn(normed[:, 384 * m : 384 * (m + 1)], grad_up[...])
        start = place_of(384 * m, rows_up, chips)
        emit(grad, side, start, rows_up, up_mine, up_other, pl.ds(pl.multiple_of(offset, 128), width), tab, chips)


def up_back_kernel(pieces, n_refs, chips, rows_up, tab, grad_up, attended, gains, cot_own, cot_got, hidden, *refs):
    sources, refs = refs[:n_refs], refs[n_refs:]
    grad_hidden, grad_att, out_mine, out_other, w_up, w_out, total_out, sems = refs
    i = pl.program_id(0)
    steps = pl.num_programs(0)
    width = hidden.shape[1]

    @pl.when(i == 0)
    def _():
        started = pieces.start(sources, tab, {"up": w_up, "out": w_out}, sems, 0)
        total_out[...] = jnp.zeros_like(total_out)
        wait_all(started["up"])
        wait_all(started["out"])

    cot = jnp.where(i < steps // 2, cot_own[...], cot_got[...]).astype(F32)
    e = nt(grad_up[...], w_up[...])
    z, root = normalized(hidden[...])
    total = cot + norm_back(z, root, e * gains[1:2, :])
    grad_hidden[...] = total
    low = total.astype(BF16)
    grad_att[...] = nt(low, w_out[...]).astype(BF16)
    total_out[...] += tn(attended[...], low)

    @pl.when(i == steps - 1)
    def _():
        for m in range(2):
            start = place_of(384 * m, rows_up, chips)
            for side in range(2):
                value = total_out[384 * m : 384 * (m + 1), side * (width // 2) : (side + 1) * (width // 2)]
                emit(value, side, start, rows_up, out_mine, out_other, slice(None), tab, chips)


def output_kernel(pieces, n_refs, chips, tab, active, hidden, *refs):
    sources, refs = refs[:n_refs], refs[n_refs:]
    out, w_down, sems = refs

    @pl.when(pl.program_id(0) == 0)
    def _():
        wait_all(pieces.start(sources, tab, {"down": w_down}, sems, 0)["down"])

    out[...] = (hidden[...] + nn(active[...], w_down[...])).astype(BF16)


def attend_back_kernel(chips, tab, q_ref, k_ref, v_ref, o_ref, d_ref, log_totals, grad_q_ref, grad_k_ref, grad_v_ref, bias):
    @pl.when(jnp.logical_and(pl.program_id(0) == 0, pl.program_id(1) == 0))
    def _():
        fill_bias(bias, tab[2 * chips + 1])

    lane = lax.broadcasted_iota(jnp.int32, (512, 128), 1)
    for n in range(2):
        q, k, v, o, d = [pair_of(r, n) for r in (q_ref, k_ref, v_ref, o_ref, d_ref)]
        k_t = k.T
        dots = (o.astype(F32) * d.astype(F32)).T
        grad_q, grad_k, grad_v = [], [], []
        for h in range(2):
            here = (lane // 64) == h
            zero = jnp.zeros_like(k)
            s = nt(jnp.where(here, k, zero), q) * (SCORE_SCALE * LOG2E) + bias[...]
            p = jnp.exp2(s - log_totals[2 * n + h])
            grad_v.append(nn(p.astype(BF16), jnp.where(here, d, zero)))
            grad_p = nt(jnp.where(here, v, zero), d)
            delta = jnp.sum(dots[64 * h : 64 * h + 64, :], axis=0, keepdims=True)
            grad_s = (p * (grad_p - delta)).astype(BF16)
            grad_k.append(nn(grad_s, jnp.where(here, q, zero)))
            grad_q.append(nn(k_t[64 * h : 64 * h + 64, :], grad_s))

        def put(ref, value):
            ref[:, 0, :, 128 * n : 128 * (n + 1)] = value.astype(BF16).reshape(2, 256, 128)

        put(grad_q_ref, jnp.concatenate(grad_q, axis=0).T * SCORE_SCALE)
        put(grad_k_ref, (grad_k[0] + grad_k[1]) * SCORE_SCALE)
        put(grad_v_ref, grad_v[0] + grad_v[1])


def qkv_grad_kernel(chips, rows_qkv, tab, normed, grad_q, grad_k, grad_v, mine, other):
    width = normed.shape[1]
    near = width // 2
    for n, ref in enumerate((grad_q, grad_k, grad_v)):
        for m in range(2):
            grad = tn(normed[:, 384 * m : 384 * (m + 1)], ref[...])
            start = place_of(384 * m, rows_qkv, chips)
            for part in range(2):
                at = n * width + part * near
                side, column = at // (3 * near), at % (3 * near)
                value = grad[:, part * near : (part + 1) * near]
                emit(value, side, start, rows_qkv, mine, other, slice(column, column + near), tab, chips)


def first_kernel(pieces, n_refs, chips, tab, own, got, gains, grad_q, grad_k, grad_v, grad_hidden, *refs):
    sources, refs = refs[:n_refs], refs[n_refs:]
    out, w_qkv, sems = refs
    i = pl.program_id(0)
    width = own.shape[1]

    @pl.when(i == 0)
    def _():
        wait_all(pieces.start(sources, tab, {"qkv": w_qkv}, sems, 0)["qkv"])

    x = jnp.where(i < pl.num_programs(0) // 2, own[...], got[...]).astype(F32)
    e = nt(grad_q[...], w_qkv[:, :width])
    e += nt(grad_k[...], w_qkv[:, width : 2 * width])
    e += nt(grad_v[...], w_qkv[:, 2 * width :])
    z, root = normalized(x)
    out[...] = (grad_hidden[...] + norm_back(z, root, e * gains[0:1, :])).astype(BF16)


def whole(shape):
    return pl.BlockSpec(shape, lambda *_: (0,) * len(shape))


def call(kernel, tab, inputs, piece_arrays, outs, scratch, grid=(1,), cost=0):
    specs = [spec or whole(a.shape) for a, spec in inputs]
    specs = specs + [pl.BlockSpec(memory_space=pl.ANY) for _ in piece_arrays]
    moved = sum(a.size * a.dtype.itemsize for a, _ in inputs) + sum(a.size * a.dtype.itemsize for a in piece_arrays)
    moved += sum(o.size * o.dtype.itemsize for o, _ in outs)
    return pl.pallas_call(
        kernel,
        out_shape=[o for o, _ in outs],
        grid_spec=pltpu.PrefetchScalarGridSpec(
            num_scalar_prefetch=1,
            grid=grid,
            in_specs=specs,
            out_specs=[spec or whole(o.shape) for o, spec in outs],
            scratch_shapes=scratch,
        ),
        compiler_params=pltpu.CompilerParams(
            dimension_semantics=("arbitrary",) * len(grid), vmem_limit_bytes=VMEM_BYTES
        ),
        cost_estimate=pl.CostEstimate(flops=cost, bytes_accessed=moved, transcendentals=0),
    )(tab, *[a for a, _ in inputs], *piece_arrays)


def body(grid, tokens, clip_class, w_qkv, w_out, w_up, w_down, norm_gains, cotangent):
    rows, width = tokens.shape[1:]
    half = rows // 2
    ff = w_up.shape[1]
    here = grid.here()
    mx = here["x"]
    fast = (2 * w_qkv.shape[0]) % 16 == 0 and (2 * w_down.shape[0]) % 16 == 0
    chips = grid.chips if fast else 1

    def split(array):
        own = lax.dynamic_slice(array[0], (mx * half, 0), (half, width))
        away = lax.dynamic_slice(array[0], ((1 - mx) * half, 0), (half, width))
        return own, away

    swap_x = [(0, 1), (1, 0)]
    tok_own, tok_away = split(tokens)
    cot_own, cot_away = split(cotangent)

    if fast:
        spots = [(x, y, z) for x in range(grid.nx) for y in range(grid.ny) for z in range(grid.nz)]
        chip_at = [
            (((mx - x) % grid.nx) * grid.nz + ((here["z"] - z) % grid.nz)) * grid.ny + ((here["y"] - y) % grid.ny)
            for x, y, z in spots
        ]
        place_at = []
        for a in range(chips):
            x, z, y = a // (grid.nz * grid.ny), (a // grid.ny) % grid.nz, a % grid.ny
            rx, rz, ry = (x - mx) % grid.nx, (z - here["z"]) % grid.nz, (y - here["y"]) % grid.ny
            place_at.append((ry * grid.nx + rx) * grid.nz + rz)
        core = here["c"]
    else:
        chip_at, place_at, core = [jnp.int32(0)], [jnp.int32(0)], jnp.int32(0)
    tab = jnp.stack([jnp.asarray(v, jnp.int32) for v in chip_at + place_at + [core, clip_class[0]]])

    def side_of(weight, side):
        wide = weight.shape[1] // 2
        return lax.dynamic_slice(weight, (0, side * wide), (weight.shape[0], wide))

    gain_block = jnp.pad(norm_gains, ((0, 0), (0, 126)))
    fields_a = [("qkv", 0, 3 * width // 2, False), ("gain", 3 * width // 2, 128, True)]
    fields_b = [("up", 0, ff // 2, False), ("out", ff // 2, width // 2, False)]
    fields_c = [("down", 0, width // 2, False)]
    swap_core = functools.partial(lax.ppermute, axis_name=AXES, perm=grid.core_swap())
    tok_got = lax.ppermute(tok_away, "seq", swap_x)

    if fast:
        def sides(side):
            return (
                jnp.concatenate([side_of(w_qkv, side), gain_block], axis=1),
                jnp.concatenate([side_of(w_up, side), side_of(w_out, side)], axis=1),
                side_of(w_down, side),
            )

        def with_partner(keep, give):
            other = swap_core(give)
            return jnp.concatenate(
                [jnp.where(core == 0, keep, other), jnp.where(core == 0, other, keep)], axis=0
            )

        pieces = [with_partner(k, g) for k, g in zip(sides(core), sides(1 - core))]
        pieces_a, pieces_b, pieces_c = pieces

        def plane(x_first, y_first):
            near = exchange(grid, [x_first], "x"), exchange(grid, [y_first], "y")
            straight = exchange(grid, [x_first], "y"), exchange(grid, [y_first], "x")
            return near, straight

        def corners(near):
            return exchange(grid, near[0], "y") + exchange(grid, near[1], "x")

        def finish(mine, fields):
            mine = [(a, [rel_of(grid, s) for s in spots]) for a, spots in mine]
            theirs = [(swap_core(a), s) for a, s in mine]
            return Pieces(chips, mine, theirs, fields)

        z_a = gather_along_z(grid, pieces_a)
        near_a, straight_a = plane(*z_a)
        far_a = corners(near_a)
        z_b = gather_along_z(grid, after(pieces_b, z_a[0][0], z_a[1][0]))
        z_c = gather_along_z(grid, after(pieces_c, z_b[0][0], z_b[1][0]))
        group_a = finish(list(z_a) + near_a[0] + near_a[1] + straight_a[0] + straight_a[1] + far_a, fields_a)

        def held(parts, *earlier):
            arrays = lax.optimization_barrier(tuple(a for a, _ in parts) + earlier)
            return [(a, s) for a, (_, s) in zip(arrays, parts)]

        near_b, straight_b = plane(*held(z_b, *[a for a, _ in far_a]))
        cot_away = after(cot_away, *[a for a, _ in far_a])
        cot_got = lax.ppermute(cot_away, "seq", swap_x)
    else:
        full = [lax.all_gather(w, AXES, axis=0, tiled=True) for w in (w_qkv, w_out, w_up, w_down, gain_block)]

        def natural(parts, fields):
            sides = []
            for side in range(2):
                cut = [p if p.shape[1] == 128 else p[:, side * (p.shape[1] // 2) : (side + 1) * (p.shape[1] // 2)] for p in parts]
                sides.append([(jnp.concatenate(cut, axis=1)[None], [0])])
            return Pieces(1, sides[0], sides[1], fields)

        group_a = natural([full[0], full[4]], fields_a)
        group_b = natural([full[2], full[1]], fields_b)
        group_c = natural([full[3]], fields_c)
        cot_got = lax.ppermute(cot_away, "seq", swap_x)

    sds = jax.ShapeDtypeStruct
    heads = width // HEAD_DIM
    rows_a, rows_c = (2 * w_qkv.shape[0], 2 * w_down.shape[0]) if fast else (width, ff)
    dma = pltpu.SemaphoreType.DMA
    vmem = pltpu.VMEM
    tiles = rows // 256
    tile = lambda columns: pl.BlockSpec((256, columns), lambda i, t: (i, 0))
    own_tile = pl.BlockSpec((256, width), lambda i, t: (jnp.minimum(i, tiles // 2 - 1), 0))
    got_tile = pl.BlockSpec((256, width), lambda i, t: (jnp.maximum(i - tiles // 2, 0), 0))
    chunk = pl.BlockSpec((rows, width), lambda j, t: (0, j))
    low = lambda *shape: sds(shape, BF16)

    packed, normed_first, gains = call(
        functools.partial(input_kernel, group_a, len(group_a.arrays), chips),
        tab,
        [(tok_own, own_tile), (tok_got, got_tile)],
        group_a.arrays,
        [(low(rows, 3 * width), tile(3 * width)), (low(rows, width), tile(width)), (sds((8, width), F32), None)],
        [vmem((width, 3 * width), BF16), vmem((width, 128), BF16), dma((group_a.copies(("qkv", "gain")),))],
        grid=(tiles,),
        cost=2 * rows * width * 3 * width,
    )

    clip_blocks = half // 256
    by_clip = lambda a: a.reshape(2, clip_blocks, 256, a.shape[1])
    heads_at = lambda base: pl.BlockSpec((2, 1, 256, 256), lambda b, g, t: (0, b, 0, base + g))
    totals_at = pl.BlockSpec((4, 1, 512), lambda b, g, t: (b * (heads // 4) + g, 0, 0))
    clip_shape = low(2, clip_blocks, 256, width)
    step = width // 256
    qkv_in = [(by_clip(packed), heads_at(0)), (by_clip(packed), heads_at(step)), (by_clip(packed), heads_at(2 * step))]
    if fast:
        qkv_in = [(after(a, *[x for x, _ in near_b[0] + near_b[1]]), s) for a, s in qkv_in[:1]] + qkv_in[1:]
        far_b = corners(near_b)
    attended, log_totals = call(
        functools.partial(attend_kernel, chips),
        tab,
        qkv_in,
        [],
        [(clip_shape, heads_at(0)), (sds((clip_blocks * heads, 1, 512), F32), totals_at)],
        [vmem((512, 512), F32)],
        grid=(clip_blocks, heads // 4),
        cost=8 * rows * 512 * width,
    )
    attended = attended.reshape(rows, width)

    if fast:
        parts_b = list(z_b) + near_b[0] + near_b[1] + straight_b[0] + straight_b[1] + far_b
        group_b = finish(parts_b, fields_b)
        near_c, straight_c = plane(*held(z_c, *[a for a, _ in far_b]))

    hidden, normed_second = call(
        functools.partial(middle_kernel, group_b, len(group_b.arrays), chips),
        tab,
        [(attended, tile(width)), (tok_own, own_tile), (tok_got, got_tile), (gains, None)],
        group_b.arrays,
        [(sds((rows, width), F32), tile(width)), (low(rows, width), tile(width))],
        [vmem((width, width), BF16), dma((group_b.copies(("out",)),))],
        grid=(tiles,),
        cost=2 * rows * width * width,
    )

    if fast:
        normed_up = after(normed_second, *[x for x, _ in near_c[0] + near_c[1]])
        far_c = corners(near_c)
    else:
        normed_up = normed_second
    steps = ff // width
    down_out = low(chips, rows_c, width // 2)
    active, slope, down_mine, down_other = call(
        functools.partial(up_kernel, group_b, len(group_b.arrays), chips, rows_c),
        tab,
        [(normed_up, None), (cot_own, None), (cot_got, None)],
        group_b.arrays,
        [(low(rows, ff), chunk), (low(rows, ff), chunk), (down_out, None), (down_out, None)],
        [vmem((width, ff), BF16), dma((group_b.copies(("up",)),))],
        grid=(steps,),
        cost=4 * rows * width * ff,
    )

    def sums(mine, other):
        if fast:
            total = scatter_sum(grid, mine, other)
            height = total.shape[0] // 2
            keep = lax.dynamic_slice(total, (core * height, 0), (height, total.shape[1]))
            away = lax.dynamic_slice(total, ((1 - core) * height, 0), (height, total.shape[1]))
            got = swap_core(away.astype(BF16)).astype(F32)
            return jnp.where(core == 0, keep, got), jnp.where(core == 0, got, keep)
        whole_sum = jnp.concatenate([mine[0], other[0]], axis=1)
        total = lax.psum_scatter(whole_sum, AXES, scatter_dimension=0, tiled=True).astype(F32)
        return total[:, : total.shape[1] // 2], total[:, total.shape[1] // 2 :]

    left, right = sums(down_mine, down_other)
    owned_down = jnp.concatenate([left, right], axis=1)

    if fast:
        group_c = finish(list(z_c) + near_c[0] + near_c[1] + straight_c[0] + straight_c[1] + far_c, fields_c)
    up_out = low(chips, rows_a, ff // 2)
    grad_up, up_mine, up_other = call(
        functools.partial(down_back_kernel, group_c, len(group_c.arrays), chips, rows_a),
        tab,
        [(cot_own, None), (cot_got, None), (normed_second, None), (slope, chunk)],
        group_c.arrays,
        [(low(rows, ff), chunk), (up_out, None), (up_out, None)],
        [vmem((ff, width), BF16), dma((group_c.copies(("down",)),))],
        grid=(steps,),
        cost=4 * rows * width * ff,
    )
    small_out = low(chips, rows_a, width // 2)
    grad_hidden, grad_att, out_mine, out_other = call(
        functools.partial(up_back_kernel, group_b, len(group_b.arrays), chips, rows_a),
        tab,
        [
            (grad_up, tile(ff)), (attended, tile(width)), (gains, None), (cot_own, own_tile), (cot_got, got_tile),
            (hidden, tile(width)),
        ],
        group_b.arrays,
        [(sds((rows, width), F32), tile(width)), (low(rows, width), tile(width)), (small_out, None), (small_out, None)],
        [vmem((width, ff), BF16), vmem((width, width), BF16), vmem((width, width), F32), dma((group_b.copies(("up", "out")),))],
        grid=(tiles,),
        cost=2 * rows * width * ff + 4 * rows * width * width,
    )
    left, right = sums(
        jnp.concatenate([up_mine, out_mine], axis=2), jnp.concatenate([up_other, out_other], axis=2)
    )
    owned_up = jnp.concatenate([left[:, : ff // 2], right[:, : ff // 2]], axis=1)
    owned_out = jnp.concatenate([left[:, ff // 2 :], right[:, ff // 2 :]], axis=1)

    def joined(both):
        own, away = both[:half], both[half:]
        back = lax.ppermute(away, "seq", swap_x)
        first = mx == 0
        return jnp.concatenate([jnp.where(first, own, back), jnp.where(first, back, own)], axis=0)[None]

    (outputs,) = call(
        functools.partial(output_kernel, group_c, len(group_c.arrays), chips),
        tab,
        [(active, tile(ff)), (hidden, tile(width))],
        group_c.arrays,
        [(low(rows, width), tile(width))],
        [vmem((ff, width), BF16), dma((group_c.copies(("down",)),))],
        grid=(tiles,),
        cost=2 * rows * width * ff,
    )
    output_tokens = joined(outputs)

    grads = call(
        functools.partial(attend_back_kernel, chips),
        tab,
        [
            (by_clip(packed), heads_at(0)), (by_clip(packed), heads_at(step)), (by_clip(packed), heads_at(2 * step)),
            (by_clip(attended), heads_at(0)), (by_clip(grad_att), heads_at(0)), (log_totals, totals_at),
        ],
        [],
        [(clip_shape, heads_at(0))] * 3,
        [vmem((512, 512), F32)],
        grid=(clip_blocks, heads // 4),
        cost=30 * rows * 512 * width,
    )
    grads = [g.reshape(rows, width) for g in grads]
    qkv_out = low(chips, rows_a, 3 * width // 2)
    qkv_mine, qkv_other = call(
        functools.partial(qkv_grad_kernel, chips, rows_a),
        tab,
        [(normed_first, None)] + [(g, None) for g in grads],
        [],
        [(qkv_out, None), (qkv_out, None)],
        [],
        cost=2 * rows * width * 3 * width,
    )
    left, right = sums(qkv_mine, qkv_other)
    owned_qkv = jnp.concatenate([left, right], axis=1)

    (grad_rows,) = call(
        functools.partial(first_kernel, group_a, len(group_a.arrays), chips),
        tab,
        [(tok_own, own_tile), (tok_got, got_tile), (gains, None)] + [(g, tile(width)) for g in grads] + [(grad_hidden, tile(width))],
        group_a.arrays,
        [(low(rows, width), tile(width))],
        [vmem((width, 3 * width), BF16), dma((group_a.copies(("qkv",)),))],
        grid=(tiles,),
        cost=2 * rows * width * 3 * width,
    )
    grad_tokens = joined(grad_rows)

    scale = norm_gains.astype(F32)
    first_gain = jnp.sum(w_qkv.astype(F32) * owned_qkv, axis=1) / scale[:, 0]
    second_gain = jnp.sum(w_up.astype(F32) * owned_up, axis=1) / scale[:, 1]
    owned_gains = jnp.stack([first_gain, second_gain], axis=1)
    return (output_tokens, grad_tokens, owned_qkv, owned_out, owned_up, owned_down, owned_gains)


def solution(mesh):
    grid = Grid(mesh.shape["seq"], mesh.shape["clips"])
    shard = P(AXES, None)
    return jax.shard_map(
        functools.partial(body, grid),
        mesh=mesh,
        in_specs=(P("seq", "clips", None), P("clips"), shard, shard, shard, shard, shard, P("seq", "clips", None)),
        out_specs=(P("seq", "clips", None), P("seq", "clips", None), shard, shard, shard, shard, shard),
        check_vma=False,
    )
```

```python
import functools
import math

import jax
import jax.numpy as jnp
from jax import lax
from jax.experimental import pallas as pl
from jax.experimental.pallas import tpu as pltpu
from jax.sharding import PartitionSpec as P

HEAD_DIM = 64
CLIP = 512
EPSILON = 1e-05
AXES = ("seq", "clips")
LOG2E = 1.4426950408889634
SCORE_SCALE = HEAD_DIM ** (-0.5)
BF16 = jnp.bfloat16
F32 = jnp.float32
VMEM_BYTES = 58 * 1024 * 1024
SPARE_BYTES = 10 * 1024 * 1024


class Grid:
    def __init__(self, seq, clips):
        self.nx = seq
        self.clips = clips
        pairs = clips // 2
        bits = pairs.bit_length() - 1
        self.ny = 2 ** (bits // 3)
        self.nz = pairs // self.ny
        self.sizes = {"x": self.nx, "y": self.ny, "z": self.nz}
        self.chips = self.nx * self.ny * self.nz

    def index(self, x, z, y, c):
        return x * self.clips + (z * self.ny + y) * 2 + c

    def shift(self, axis, k):
        pairs = []
        for x in range(self.nx):
            for z in range(self.nz):
                for y in range(self.ny):
                    for c in range(2):
                        t = {"x": x, "y": y, "z": z}
                        t[axis] = (t[axis] + k) % self.sizes[axis]
                        pairs.append((self.index(x, z, y, c), self.index(t["x"], t["z"], t["y"], c)))
        return pairs

    def core_swap(self):
        return [(i, i ^ 1) for i in range(self.nx * self.clips)]

    def here(self):
        x = lax.axis_index("seq")
        rest = lax.axis_index("clips")
        return {"x": x, "z": rest // (2 * self.ny), "y": (rest // 2) % self.ny, "c": rest % 2}


def rel_of(grid, coords):
    return (coords["x"] * grid.ny + coords["y"]) * grid.nz + coords["z"]


def together(*values):
    return lax.optimization_barrier(values)


def exchange(grid, parts, axis):
    moved = []
    for k in range(1, grid.sizes[axis]):
        for array, spots in parts:
            moved.append((lax.ppermute(array, AXES, grid.shift(axis, k)), [{**s, axis: k} for s in spots]))
    return moved


def joined_parts(parts):
    if len(parts) == 1:
        return parts[0]
    return (jnp.concatenate([a for a, _ in parts], axis=0), [s for _, spots in parts for s in spots])


def gather_along_z(grid, piece):
    parts = [(piece[None], [{"x": 0, "y": 0, "z": 0}])]
    return parts + exchange(grid, parts, "z")


def lots_of(parts, cut):
    cut = min(cut, len(parts))
    return [joined_parts(p) for p in (parts[:cut], parts[cut:]) if p]


def arrays_of(parts):
    return [a for a, _ in parts]


def with_arrays(parts, arrays):
    return [(a, s) for a, (_, s) in zip(arrays, parts)]


def scatter_steps(grid, mine, other, cut):
    got = lax.ppermute(other, AXES, grid.core_swap())
    (got,) = yield [got]
    shape = (grid.ny, grid.nx, grid.nz) + mine.shape[1:]
    mine, got = mine.reshape(shape), got.reshape(shape)
    cut = min(cut, grid.nz)
    lots = [(lo, hi, axes) for lo, hi, axes in ((0, cut, "yx"), (cut, grid.nz, "xy")) if hi > lo]
    current = [[mine[:, :, lo:hi], got[:, :, lo:hi]] for lo, hi, _ in lots]
    for step in range(2):
        waiting = []
        for n, (_, _, axes) in enumerate(lots):
            axis = axes[step]
            dim = 1 if axis == "x" and step == 0 else 0
            pieces = [
                [lax.index_in_dim(c, k, dim, keepdims=False) for c in current[n]] for k in range(grid.sizes[axis])
            ]
            received = [
                lax.ppermute(add_all(pieces[k]).astype(BF16), AXES, grid.shift(axis, k))
                for k in range(1, grid.sizes[axis])
            ]
            waiting.append(received)
            current[n] = pieces[0]
        flat = yield [a for received in waiting for a in received]
        flat = list(flat)
        for n, received in enumerate(waiting):
            current[n] = current[n] + flat[: len(received)]
            flat = flat[len(received) :]
    final = []
    for k in range(grid.nz):
        n = 0 if k < lots[0][1] else 1
        total = add_all([c[k - lots[n][0]] for c in current[n]])
        final.append(total if k == 0 else lax.ppermute(total.astype(BF16), AXES, grid.shift("z", k)))
    final[1:] = yield final[1:]
    yield add_all(final)


def add_all(items):
    total = items[0].astype(F32)
    for item in items[1:]:
        total = total + item.astype(F32)
    return total


def nn(a, b):
    return lax.dot_general(a, b, (((1,), (0,)), ((), ())), preferred_element_type=F32)


def nt(a, b):
    return lax.dot_general(a, b, (((1,), (1,)), ((), ())), preferred_element_type=F32)


def tn(a, b):
    return lax.dot_general(a, b, (((0,), (0,)), ((), ())), preferred_element_type=F32)


def normalized(values):
    centered = values - jnp.mean(values, axis=-1, keepdims=True)
    spread = jnp.mean(centered * centered, axis=-1, keepdims=True)
    root = lax.rsqrt(spread + EPSILON)
    return centered * root, root


def norm_back(z, root, scaled):
    return root * (
        scaled
        - jnp.mean(scaled, axis=-1, keepdims=True)
        - z * jnp.mean(scaled * z, axis=-1, keepdims=True)
    )


class Pieces:
    def __init__(self, chips, mine, theirs, fields):
        self.chips = chips
        self.arrays = [a for a, _ in mine] + [a for a, _ in theirs]
        self.spots = [s for _, s in mine] + [s for _, s in theirs]
        self.count_mine = len(mine)
        self.rows = self.arrays[0].shape[1]
        self.fields = fields

    def copies(self, wanted):
        total = 0
        for n, spots in enumerate(self.spots):
            for name, column, width, gain in self.fields:
                if name in wanted and not (gain and n >= self.count_mine):
                    total += len(spots)
        return total

    def start(self, refs, tab, wanted, sems, first):
        core = tab[2 * self.chips]
        started = {name: [] for name in wanted}
        n_sem = first
        for n, spots in enumerate(self.spots):
            for name, column, width, gain in self.fields:
                if name not in wanted or (gain and n >= self.count_mine):
                    continue
                for k, r in enumerate(spots):
                    row = pl.multiple_of(tab[r] * self.rows, 16)
                    if gain:
                        place = wanted[name].at[pl.ds(row, self.rows), :]
                    else:
                        side = core if n < self.count_mine else 1 - core
                        col = pl.multiple_of(side * width, 128)
                        place = wanted[name].at[pl.ds(row, self.rows), pl.ds(col, width)]
                    copy = pltpu.make_async_copy(
                        refs[n].at[k, :, column : column + width], place, sems.at[n_sem]
                    )
                    copy.start()
                    started[name].append(copy)
                    n_sem += 1
        return started


def wait_all(copies):
    for copy in copies:
        copy.wait()


def emit(value, side, first_chip, rows, mine, other, columns, tab, chips):
    rel = side ^ tab[2 * chips]
    height = value.shape[0]
    low = value.astype(BF16)

    def put(ref):
        if rows >= height:
            ref[0, pl.ds(first_chip, height), columns] = low
        else:
            for a in range(height // rows):
                ref[tab[chips + first_chip + a], :, columns] = low[a * rows : (a + 1) * rows]

    @pl.when(rel == 0)
    def _():
        put(mine)

    @pl.when(rel != 0)
    def _():
        put(other)


def place_of(row, rows, chips):
    return row if chips == 1 else row // rows


def input_kernel(pieces, n_refs, chips, tab, own, got, *refs):
    sources, refs = refs[:n_refs], refs[n_refs:]
    packed, normed, gains, w_qkv, gain_cols, sems = refs
    i = pl.program_id(0)
    steps = pl.num_programs(0)
    width = own.shape[1]

    @pl.when(i == 0)
    def _():
        started = pieces.start(sources, tab, {"gain": gain_cols, "qkv": w_qkv}, sems, 0)
        wait_all(started["gain"])
        pick = (
            lax.broadcasted_iota(jnp.int32, (8, 128), 0) == lax.broadcasted_iota(jnp.int32, (8, 128), 1)
        ).astype(BF16)
        gains[...] = nt(pick, gain_cols[...])
        wait_all(started["qkv"])

    x = jnp.where(i < steps // 2, own[...], got[...]).astype(F32)
    z, _ = normalized(x)
    low = (z * gains[0:1, :]).astype(BF16)
    normed[...] = low
    for c in range(3):
        cols = slice(c * width, (c + 1) * width)
        packed[:, cols] = nn(low, w_qkv[:, cols]).astype(BF16)


def pair_of(ref, n):
    return ref[:, 0, :, 128 * n : 128 * (n + 1)].reshape(512, 128)


def fill_bias(bias, short):
    row_clip = (lax.broadcasted_iota(jnp.int32, (512, 512), 0) // 128) % 2
    col_clip = (lax.broadcasted_iota(jnp.int32, (512, 512), 1) // 128) % 2
    apart = jnp.logical_and(row_clip != col_clip, short != 0)
    bias[...] = jnp.where(apart, -1e30, 0.0)


def attend_kernel(chips, tab, q_ref, k_ref, v_ref, attended, log_totals, bias):
    @pl.when(jnp.logical_and(pl.program_id(0) == 0, pl.program_id(1) == 0))
    def _():
        fill_bias(bias, tab[2 * chips + 1])

    lane = lax.broadcasted_iota(jnp.int32, (512, 128), 1)
    for n in range(2):
        q, k, v = pair_of(q_ref, n), pair_of(k_ref, n), pair_of(v_ref, n)
        v_t = v.T
        mixed = []
        for h in range(2):
            k_h = jnp.where((lane // 64) == h, k, jnp.zeros_like(k))
            s = nt(k_h, q) * (SCORE_SCALE * LOG2E) + bias[...]
            top_score = jnp.max(s, axis=0, keepdims=True)
            p = jnp.exp2(s - top_score)
            total = jnp.sum(p, axis=0, keepdims=True)
            mixed.append(nn(v_t[64 * h : 64 * h + 64, :], p.astype(BF16)) * (1.0 / total))
            log_totals[2 * n + h] = top_score + jnp.log2(total)
        out = jnp.concatenate(mixed, axis=0).T.astype(BF16)
        attended[:, 0, :, 128 * n : 128 * (n + 1)] = out.reshape(2, 256, 128)


ERF_P = 0.3275911 * (0.5**0.5)
ERF_A = (0.254829592 * 0.5, -0.284496736 * 0.5, 1.421413741 * 0.5, -1.453152027 * 0.5, 1.061405429 * 0.5)


def gelu_both(u):
    t = 1.0 / (1.0 + ERF_P * jnp.abs(u))
    bell = jnp.exp2(u * u * (-0.5 * LOG2E))
    poly = t * (ERF_A[0] + t * (ERF_A[1] + t * (ERF_A[2] + t * (ERF_A[3] + t * ERF_A[4]))))
    tail = poly * bell
    below = jnp.where(u < 0, tail, 1.0 - tail)
    return u * below, below + u * (bell * 0.3989422804014327)


def middle_kernel(pieces, n_refs, chips, tab, attended, own, got, gains, *refs):
    sources, refs = refs[:n_refs], refs[n_refs:]
    hidden, normed, w_out, sems = refs
    i = pl.program_id(0)

    @pl.when(i == 0)
    def _():
        wait_all(pieces.start(sources, tab, {"out": w_out}, sems, 0)["out"])

    x = jnp.where(i < pl.num_programs(0) // 2, own[...], got[...]).astype(F32)
    h = x + nn(attended[...], w_out[...])
    hidden[...] = h
    z, _ = normalized(h)
    normed[...] = (z * gains[1:2, :]).astype(BF16)


def up_kernel(pieces, n_refs, chips, first, tab, normed, *refs):
    sources, refs = refs[-n_refs - 4 : -4], refs[-4:]
    active, slope, w_up, sems = refs
    rows, width = normed.shape
    j = pl.program_id(0)

    @pl.when(j == 0)
    def _():
        wait_all(pieces.start(sources, tab, {"up": w_up}, sems, 0)["up"])

    cols = pl.ds(pl.multiple_of((first + j) * width, 128), width)
    for i in range(rows // 256):
        rows = slice(256 * i, 256 * (i + 1))
        a, s = gelu_both(nn(normed[rows, :], w_up[:, cols]))
        active[rows, :] = a.astype(BF16)
        slope[rows, :] = s.astype(BF16)


def down_grad_kernel(chips, rows_down, tab, active, cot_own, cot_got, down_mine, down_other):
    half, width = cot_own.shape
    j = pl.program_id(0)
    for m in range(2):
        piece = slice(384 * m, 384 * (m + 1))
        grad = tn(active[:half, piece], cot_own[...]) + tn(active[half:, piece], cot_got[...])
        start = place_of(width * j + 384 * m, rows_down, chips)
        emit(grad[:, : width // 2], 0, start, rows_down, down_mine, down_other, slice(None), tab, chips)
        emit(grad[:, width // 2 :], 1, start, rows_down, down_mine, down_other, slice(None), tab, chips)


def down_back_kernel(pieces, n_refs, chips, rows_up, tab, cot_own, cot_got, normed, slope, *refs):
    sources, refs = refs[:n_refs], refs[n_refs:]
    grad_up, up_mine, up_other, w_down, sems = refs
    half, width = cot_own.shape
    j = pl.program_id(0)
    steps = pl.num_programs(0)

    @pl.when(j == 0)
    def _():
        wait_all(pieces.start(sources, tab, {"down": w_down}, sems, 0)["down"])

    w_rows = pl.ds(pl.multiple_of(j * width, 256), width)
    for part, cot in enumerate((cot_own, cot_got)):
        for i in range(half // 256):
            inner = slice(256 * i, 256 * (i + 1))
            rows = slice(part * half + 256 * i, part * half + 256 * (i + 1))
            grad_up[rows, :] = (nt(cot[inner, :], w_down[w_rows, :]) * slope[rows, :].astype(F32)).astype(BF16)

    side = j // (steps // 2)
    offset = lax.rem(j, steps // 2) * width
    for m in range(2):
        grad = tn(normed[:, 384 * m : 384 * (m + 1)], grad_up[...])
        start = place_of(384 * m, rows_up, chips)
        emit(grad, side, start, rows_up, up_mine, up_other, pl.ds(pl.multiple_of(offset, 128), width), tab, chips)


def up_back_kernel(pieces, n_refs, chips, rows_up, tab, grad_up, attended, gains, cot_own, cot_got, hidden, _mine, _other, *refs):
    sources, refs = refs[:n_refs], refs[n_refs:]
    grad_hidden, grad_att, out_mine, out_other, w_up, w_out, total_out, sems = refs
    i = pl.program_id(0)
    steps = pl.num_programs(0)
    width = hidden.shape[1]

    @pl.when(i == 0)
    def _():
        started = pieces.start(sources, tab, {"up": w_up, "out": w_out}, sems, 0)
        total_out[...] = jnp.zeros_like(total_out)
        wait_all(started["up"])
        wait_all(started["out"])

    cot = jnp.where(i < steps // 2, cot_own[...], cot_got[...]).astype(F32)
    e = nt(grad_up[...], w_up[...])
    z, root = normalized(hidden[...])
    total = cot + norm_back(z, root, e * gains[1:2, :])
    grad_hidden[...] = total
    low = total.astype(BF16)
    grad_att[...] = nt(low, w_out[...]).astype(BF16)
    total_out[...] += tn(attended[...], low)

    @pl.when(i == steps - 1)
    def _():
        for m in range(2):
            start = place_of(384 * m, rows_up, chips)
            for side in range(2):
                value = total_out[384 * m : 384 * (m + 1), side * (width // 2) : (side + 1) * (width // 2)]
                emit(value, side, start, rows_up, out_mine, out_other, slice(None), tab, chips)


def output_kernel(pieces, n_refs, chips, tab, active, hidden, *refs):
    sources, refs = refs[:n_refs], refs[n_refs:]
    out, w_down, sems = refs

    @pl.when(pl.program_id(0) == 0)
    def _():
        wait_all(pieces.start(sources, tab, {"down": w_down}, sems, 0)["down"])

    out[...] = (hidden[...] + nn(active[...], w_down[...])).astype(BF16)


def attend_back_kernel(chips, tab, q_ref, k_ref, v_ref, o_ref, d_ref, log_totals, grad_q_ref, grad_k_ref, grad_v_ref, bias):
    @pl.when(jnp.logical_and(pl.program_id(0) == 0, pl.program_id(1) == 0))
    def _():
        fill_bias(bias, tab[2 * chips + 1])

    lane = lax.broadcasted_iota(jnp.int32, (512, 128), 1)
    for n in range(2):
        q, k, v, o, d = [pair_of(r, n) for r in (q_ref, k_ref, v_ref, o_ref, d_ref)]
        k_t = k.T
        dots = (o.astype(F32) * d.astype(F32)).T
        grad_q, grad_k, grad_v = [], [], []
        for h in range(2):
            here = (lane // 64) == h
            zero = jnp.zeros_like(k)
            s = nt(jnp.where(here, k, zero), q) * (SCORE_SCALE * LOG2E) + bias[...]
            p = jnp.exp2(s - log_totals[2 * n + h])
            grad_v.append(nn(p.astype(BF16), jnp.where(here, d, zero)))
            grad_p = nt(jnp.where(here, v, zero), d)
            delta = jnp.sum(dots[64 * h : 64 * h + 64, :], axis=0, keepdims=True)
            grad_s = (p * (grad_p - delta)).astype(BF16)
            grad_k.append(nn(grad_s, jnp.where(here, q, zero)))
            grad_q.append(nn(k_t[64 * h : 64 * h + 64, :], grad_s))

        def put(ref, value):
            ref[:, 0, :, 128 * n : 128 * (n + 1)] = value.astype(BF16).reshape(2, 256, 128)

        put(grad_q_ref, jnp.concatenate(grad_q, axis=0).T * SCORE_SCALE)
        put(grad_k_ref, (grad_k[0] + grad_k[1]) * SCORE_SCALE)
        put(grad_v_ref, grad_v[0] + grad_v[1])


def qkv_grad_kernel(chips, rows_qkv, cuts, tab, normed, *refs):
    grads, mine, other = refs[:-2], refs[-2], refs[-1]
    width = normed.shape[1]
    wide = 3 * width // 2
    for n, ref in enumerate(grads):
        base = (n % 3) * width + cuts[n // 3]
        size = ref.shape[1]
        for m in range(2):
            grad = tn(normed[:, 384 * m : 384 * (m + 1)], ref[...])
            start = place_of(384 * m, rows_qkv, chips)
            at = base
            while at < base + size:
                side = at // wide
                end = min(base + size, (side + 1) * wide)
                columns = slice(at - side * wide, end - side * wide)
                emit(grad[:, at - base : end - base], side, start, rows_qkv, mine, other, columns, tab, chips)
                at = end


def first_kernel(pieces, n_refs, chips, cuts, tab, source, gains, grad_hidden, *refs):
    n_grads = 3 * (len(cuts) - 1)
    grads, sources, refs = refs[:n_grads], refs[n_grads : n_grads + n_refs], refs[n_grads + n_refs :]
    out, w_qkv, sems = refs
    width = source.shape[1]

    @pl.when(pl.program_id(0) == 0)
    def _():
        wait_all(pieces.start(sources, tab, {"qkv": w_qkv}, sems, 0)["qkv"])

    e = 0.0
    for n, grad in enumerate(grads):
        base, lot = (n % 3) * width, n // 3
        e = e + nt(grad[...], w_qkv[:, base + cuts[lot] : base + cuts[lot + 1]])
    z, root = normalized(source[...].astype(F32))
    out[...] = (grad_hidden[...] + norm_back(z, root, e * gains[0:1, :])).astype(BF16)


def whole(shape):
    return pl.BlockSpec(shape, lambda *_: (0,) * len(shape))


anywhere = pl.BlockSpec(memory_space=pl.ANY)


def call(kernel, tab, inputs, piece_arrays, outs, scratch, grid=(1,), cost=0, aliases=None):
    specs = [spec or whole(a.shape) for a, spec in inputs]
    specs = specs + [pl.BlockSpec(memory_space=pl.ANY) for _ in piece_arrays]
    blocks = [(a, spec) for a, spec in inputs] + [(o, spec) for o, spec in outs]
    need = SPARE_BYTES
    for array, spec in blocks:
        if spec is anywhere:
            continue
        size = jnp.dtype(array.dtype).itemsize
        for extent in spec.block_shape if spec else array.shape:
            size *= extent
        need += 2 * size
    for buffer in scratch:
        if hasattr(buffer, "shape") and buffer.dtype in (BF16, F32):
            size = buffer.dtype.itemsize if hasattr(buffer.dtype, "itemsize") else jnp.dtype(buffer.dtype).itemsize
            for extent in buffer.shape:
                size *= extent
            need += size
    moved = sum(a.size * a.dtype.itemsize for a, _ in inputs) + sum(a.size * a.dtype.itemsize for a in piece_arrays)
    moved += sum(math.prod(o.shape) * jnp.dtype(o.dtype).itemsize for o, _ in outs)
    inputs = [
        (pltpu.with_memory_space_constraint(a, pltpu.HBM) if a.size > 2**21 and spec is not None else a, spec)
        for a, spec in inputs
    ]
    return pl.pallas_call(
        kernel,
        out_shape=[o for o, _ in outs],
        input_output_aliases=aliases or {},
        grid_spec=pltpu.PrefetchScalarGridSpec(
            num_scalar_prefetch=1,
            grid=grid,
            in_specs=specs,
            out_specs=[spec or whole(o.shape) for o, spec in outs],
            scratch_shapes=scratch,
        ),
        compiler_params=pltpu.CompilerParams(
            dimension_semantics=("arbitrary",) * len(grid), vmem_limit_bytes=min(need, VMEM_BYTES)
        ),
        cost_estimate=pl.CostEstimate(flops=cost, bytes_accessed=moved, transcendentals=0),
    )(tab, *[a for a, _ in inputs], *piece_arrays)


def body(grid, tokens, clip_class, w_qkv, w_out, w_up, w_down, norm_gains, cotangent):
    rows, width = tokens.shape[1:]
    half = rows // 2
    ff = w_up.shape[1]
    here = grid.here()
    mx = here["x"]
    fast = (2 * w_qkv.shape[0]) % 16 == 0 and (2 * w_down.shape[0]) % 16 == 0
    chips = grid.chips if fast else 1

    def split(array):
        own = lax.dynamic_slice(array[0], (mx * half, 0), (half, width))
        away = lax.dynamic_slice(array[0], ((1 - mx) * half, 0), (half, width))
        return own, away

    swap_x = [(0, 1), (1, 0)]
    tok_own, tok_away = split(tokens)
    cot_own, cot_away = split(cotangent)

    if fast:
        spots = [(x, y, z) for x in range(grid.nx) for y in range(grid.ny) for z in range(grid.nz)]
        chip_at = [
            (((mx - x) % grid.nx) * grid.nz + ((here["z"] - z) % grid.nz)) * grid.ny + ((here["y"] - y) % grid.ny)
            for x, y, z in spots
        ]
        place_at = []
        for a in range(chips):
            x, z, y = a // (grid.nz * grid.ny), (a // grid.ny) % grid.nz, a % grid.ny
            rx, rz, ry = (x - mx) % grid.nx, (z - here["z"]) % grid.nz, (y - here["y"]) % grid.ny
            place_at.append((ry * grid.nx + rx) * grid.nz + rz)
        core = here["c"]
    else:
        chip_at, place_at, core = [jnp.int32(0)], [jnp.int32(0)], jnp.int32(0)
    tab = jnp.stack([jnp.asarray(v, jnp.int32) for v in chip_at + place_at + [core, clip_class[0]]])

    def side_of(weight, side):
        wide = weight.shape[1] // 2
        return lax.dynamic_slice(weight, (0, side * wide), (weight.shape[0], wide))

    gain_block = jnp.pad(norm_gains, ((0, 0), (0, 126)))
    fields_a = [("qkv", 0, 3 * width // 2, False), ("gain", 3 * width // 2, 128, True)]
    fields_b = [("up", 0, ff // 2, False), ("out", ff // 2, width // 2, False)]
    fields_c = [("down", 0, width // 2, False)]
    swap_core = functools.partial(lax.ppermute, axis_name=AXES, perm=grid.core_swap())
    if fast:
        def sides(side, group):
            if group == 0:
                return jnp.concatenate([side_of(w_qkv, side), gain_block], axis=1)
            if group == 1:
                return jnp.concatenate([side_of(w_up, side), side_of(w_out, side)], axis=1)
            return side_of(w_down, side)

        def with_partner(group):
            keep, other = sides(core, group), swap_core(sides(1 - core, group))
            return jnp.concatenate(
                [jnp.where(core == 0, keep, other), jnp.where(core == 0, other, keep)], axis=0
            )

        tok_away, w_qkv = together(tok_away, w_qkv)
        tok_first = lax.ppermute(tok_away[: half // 2], "seq", swap_x)
        piece_a = with_partner(0)
        piece_a, w_up, w_out, w_down = together(piece_a, w_up, w_out, w_down)
        piece_b, piece_c = with_partner(1), with_partner(2)

        def near_of(lots):
            return [exchange(grid, [lot], axis) for lot, axis in zip(lots, "xy")]

        def widened(lots, near):
            return [joined_parts([lot] + moved) for lot, moved in zip(lots, near)]

        def far_of(wide):
            far = []
            for lot, axis in zip(wide, "yx"):
                far += exchange(grid, [lot], axis)
            return far

        def flat(groups):
            return [part for group in groups for part in group]

        def finish(mine, fields):
            mine = [(a, [rel_of(grid, s) for s in spots]) for a, spots in mine]
            theirs = [(swap_core(a), s) for a, s in mine]
            return Pieces(chips, mine, theirs, fields)

        z_a = gather_along_z(grid, piece_a)
        arrays, tok_first, piece_b, tok_next = together(arrays_of(z_a), tok_first, piece_b, tok_away[half // 2 :])
        tok_second = lax.ppermute(tok_next, "seq", swap_x)
        z_a = lots_of(with_arrays(z_a, arrays), 2)
        near_a = near_of(z_a)
        z_b = gather_along_z(grid, piece_b)
        arrays, tok_second = together(arrays_of(flat(near_a)), tok_second)
        tok_got = jnp.concatenate([tok_first, tok_second], axis=0)
        wide_a = widened(z_a, [[part] for part in with_arrays(flat(near_a), arrays)])
        far_a = far_of(wide_a)
        all_a = wide_a + far_a
        arrays_a, z_own, piece_c = together(arrays_of(all_a), z_b[0][0], piece_c)
        z_b = with_arrays(z_b, [z_own] + arrays_of(z_b[1:]))
        group_a = finish(with_arrays(all_a, arrays_a), fields_a)
        arrays_b = lax.optimization_barrier(arrays_of(z_b))
        z_b = lots_of(with_arrays(z_b, arrays_b), 2)
        near_b = near_of(z_b)
    else:
        full = [lax.all_gather(w, AXES, axis=0, tiled=True) for w in (w_qkv, w_out, w_up, w_down, gain_block)]

        def natural(parts, fields):
            sides = []
            for side in range(2):
                cut = [p if p.shape[1] == 128 else p[:, side * (p.shape[1] // 2) : (side + 1) * (p.shape[1] // 2)] for p in parts]
                sides.append([(jnp.concatenate(cut, axis=1)[None], [0])])
            return Pieces(1, sides[0], sides[1], fields)

        group_a = natural([full[0], full[4]], fields_a)
        group_b = natural([full[2], full[1]], fields_b)
        group_c = natural([full[3]], fields_c)
        tok_got = lax.ppermute(tok_away, "seq", swap_x)
        cot_got = lax.ppermute(cot_away, "seq", swap_x)

    sds = jax.ShapeDtypeStruct
    heads = width // HEAD_DIM
    rows_a, rows_c = (2 * w_qkv.shape[0], 2 * w_down.shape[0]) if fast else (width, ff)
    dma = pltpu.SemaphoreType.DMA
    vmem = pltpu.VMEM
    tiles = rows // 256
    tile = lambda columns: pl.BlockSpec((256, columns), lambda i, t: (i, 0))
    own_tile = pl.BlockSpec((256, width), lambda i, t: (jnp.minimum(i, tiles // 2 - 1), 0))
    got_tile = pl.BlockSpec((256, width), lambda i, t: (jnp.maximum(i - tiles // 2, 0), 0))
    chunk = pl.BlockSpec((rows, width), lambda j, t: (0, j))
    low = lambda *shape: sds(shape, BF16)

    packed, normed_first, gains = call(
        functools.partial(input_kernel, group_a, len(group_a.arrays), chips),
        tab,
        [(tok_own, own_tile), (tok_got, got_tile)],
        group_a.arrays,
        [(low(rows, 3 * width), tile(3 * width)), (low(rows, width), tile(width)), (sds((8, width), F32), None)],
        [vmem((width, 3 * width), BF16), vmem((width, 128), BF16), dma((group_a.copies(("qkv", "gain")),))],
        grid=(tiles,),
        cost=2 * rows * width * 3 * width,
    )

    if fast:
        packed, arrays_b, piece_c = together(packed, arrays_of(flat(near_b)), piece_c)
        wide_b = widened(z_b, [[part] for part in with_arrays(flat(near_b), arrays_b)])
        far_b = far_of(wide_b)
        z_c = gather_along_z(grid, piece_c)

    clip_blocks = half // 256
    by_clip = lambda a: a.reshape(2, clip_blocks, 256, a.shape[1])
    heads_at = lambda base: pl.BlockSpec((2, 1, 256, 256), lambda b, g, t: (0, b, 0, base + g))
    totals_at = pl.BlockSpec((4, 1, 512), lambda b, g, t: (b * (heads // 4) + g, 0, 0))
    clip_shape = low(2, clip_blocks, 256, width)
    step = width // 256
    qkv_in = [(by_clip(packed), heads_at(0)), (by_clip(packed), heads_at(step)), (by_clip(packed), heads_at(2 * step))]
    attended, log_totals = call(
        functools.partial(attend_kernel, chips),
        tab,
        qkv_in,
        [],
        [(clip_shape, heads_at(0)), (sds((clip_blocks * heads, 1, 512), F32), totals_at)],
        [vmem((512, 512), F32)],
        grid=(clip_blocks, heads // 4),
        cost=8 * rows * 512 * width,
    )
    attended = attended.reshape(rows, width)

    if fast:
        all_b = wide_b + far_b
        attended, arrays_b, arrays_c = together(attended, arrays_of(all_b), arrays_of(z_c))
        group_b = finish(with_arrays(all_b, arrays_b), fields_b)
        z_c = lots_of(with_arrays(z_c, arrays_c), grid.nz)
        near_c = exchange(grid, z_c, "x")
        straight_c = exchange(grid, z_c, "y")

    hidden, normed_second = call(
        functools.partial(middle_kernel, group_b, len(group_b.arrays), chips),
        tab,
        [(attended, tile(width)), (tok_own, own_tile), (tok_got, got_tile), (gains, None)],
        group_b.arrays,
        [(sds((rows, width), F32), tile(width)), (low(rows, width), tile(width))],
        [vmem((width, width), BF16), dma((group_b.copies(("out",)),))],
        grid=(tiles,),
        cost=2 * rows * width * width,
    )

    steps = ff // width

    def up_part_of(first, count, normed, earlier):
        to = pl.BlockSpec((rows, width), lambda j, t: (0, first + j))
        return call(
            functools.partial(up_kernel, group_b, len(group_b.arrays), chips, first),
            tab,
            [(normed, None)] + [(a, anywhere) for a in earlier],
            group_b.arrays,
            [(pltpu.HBM((rows, ff), BF16), to), (pltpu.HBM((rows, ff), BF16), to)],
            [vmem((width, ff), BF16), dma((group_b.copies(("up",)),))],
            grid=(count,),
            cost=2 * rows * width * width * count,
            aliases={2: 0, 3: 1} if earlier else None,
        )

    active, slope = up_part_of(0, steps // 2, normed_second, [])
    if fast:
        active, slope, normed_second, arrays_c, cot_away = together(active, slope, normed_second, arrays_of(near_c), cot_away)
        near_c = with_arrays(near_c, arrays_c)
        far_c = exchange(grid, near_c, "y")
        cot_got = lax.ppermute(cot_away, "seq", swap_x)
    active, slope = up_part_of(steps // 2, steps - steps // 2, normed_second, [active, slope])
    if fast:
        all_c = z_c + near_c + straight_c + far_c
        active, slope, arrays_c, cot_got = together(active, slope, arrays_of(all_c), cot_got)
        group_c = finish(with_arrays(all_c, arrays_c), fields_c)
    (outputs,) = call(
        functools.partial(output_kernel, group_c, len(group_c.arrays), chips),
        tab,
        [(active, tile(ff)), (hidden, tile(width))],
        group_c.arrays,
        [(low(rows, width), tile(width))],
        [vmem((ff, width), BF16), dma((group_c.copies(("down",)),))],
        grid=(tiles,),
        cost=2 * rows * width * ff,
    )
    outputs, active = together(outputs, active)
    out_back = lax.ppermute(outputs[half:], "seq", swap_x)
    down_out = low(chips, rows_c, width // 2)
    down_mine, down_other = call(
        functools.partial(down_grad_kernel, chips, rows_c),
        tab,
        [(active, chunk), (cot_own, None), (cot_got, None)],
        [],
        [(down_out, None), (down_out, None)],
        [],
        grid=(steps,),
        cost=2 * rows * width * ff,
    )

    def steps_of(mine, other, cut):
        if fast:
            return scatter_steps(grid, mine, other, cut)

        def plain():
            whole_sum = jnp.concatenate([mine[0], other[0]], axis=1)
            for _ in range(4):
                yield []
            yield lax.psum_scatter(whole_sum, AXES, scatter_dimension=0, tiled=True).astype(F32)

        return plain()

    def owned(total):
        if not fast:
            return total[:, : total.shape[1] // 2], total[:, total.shape[1] // 2 :]
        height = total.shape[0] // 2
        keep = lax.dynamic_slice(total, (core * height, 0), (height, total.shape[1]))
        away = lax.dynamic_slice(total, ((1 - core) * height, 0), (height, total.shape[1]))
        got = swap_core(away.astype(BF16)).astype(F32)
        return jnp.where(core == 0, keep, got), jnp.where(core == 0, got, keep)

    down_sum = steps_of(down_mine, down_other, 3)
    arrived = next(down_sum)
    def joined(own, back):
        first = mx == 0
        return jnp.concatenate([jnp.where(first, own, back), jnp.where(first, back, own)], axis=0)[None]

    up_part = pl.BlockSpec((chips, rows_a, ff // 2), lambda *_: (0, 0, 0))
    out_part = pl.BlockSpec((chips, rows_a, width // 2), lambda *_: (0, 0, ff // width))
    up_out = low(chips, rows_a, ff // 2 + width // 2)
    grad_up, up_mine, up_other = call(
        functools.partial(down_back_kernel, group_c, len(group_c.arrays), chips, rows_a),
        tab,
        [(cot_own, None), (cot_got, None), (normed_second, None), (slope, chunk)],
        group_c.arrays,
        [(pltpu.HBM((rows, ff), BF16), chunk), (up_out, up_part), (up_out, up_part)],
        [vmem((ff, width), BF16), dma((group_c.copies(("down",)),))],
        grid=(steps,),
        cost=4 * rows * width * ff,
    )
    grad_up, up_mine, up_other, out_back, arrived = together(grad_up, up_mine, up_other, out_back, arrived)
    arrived = down_sum.send(arrived)
    grad_hidden, grad_att, up_mine, up_other = call(
        functools.partial(up_back_kernel, group_b, len(group_b.arrays), chips, rows_a),
        tab,
        [
            (grad_up, tile(ff)), (attended, tile(width)), (gains, None), (cot_own, own_tile), (cot_got, got_tile),
            (hidden, tile(width)), (up_mine, anywhere), (up_other, anywhere),
        ],
        group_b.arrays,
        [(sds((rows, width), F32), tile(width)), (low(rows, width), tile(width)), (up_out, out_part), (up_out, out_part)],
        [vmem((width, ff), BF16), vmem((width, width), BF16), vmem((width, width), F32), dma((group_b.copies(("up", "out")),))],
        grid=(tiles,),
        cost=2 * rows * width * ff + 4 * rows * width * width,
        aliases={7: 2, 8: 3},
    )
    grad_att, grad_hidden, up_mine, up_other, arrived = together(grad_att, grad_hidden, up_mine, up_other, arrived)
    arrived = down_sum.send(arrived)
    up_sum = steps_of(up_mine, up_other, 2)
    arrived_up = next(up_sum)

    groups = heads // 4
    group_cut = max(1, groups // 3)
    cuts = [0, 256 * group_cut, width]

    def attend_back(first, last, grad_att):
        at = lambda base: pl.BlockSpec((2, 1, 256, 256), lambda b, g, t: (0, b, 0, base + first + g))
        to = pl.BlockSpec((2, 1, 256, 256), lambda b, g, t: (0, b, 0, g))
        totals = pl.BlockSpec((4, 1, 512), lambda b, g, t: (b * groups + first + g, 0, 0))
        shape = low(2, clip_blocks, 256, 256 * (last - first))
        grads = call(
            functools.partial(attend_back_kernel, chips),
            tab,
            [
                (by_clip(packed), at(0)), (by_clip(packed), at(step)), (by_clip(packed), at(2 * step)),
                (by_clip(attended), at(0)), (by_clip(grad_att), at(0)), (log_totals, totals),
            ],
            [],
            [(shape, to)] * 3,
            [vmem((512, 512), F32)],
            grid=(clip_blocks, last - first),
            cost=30 * rows * 512 * 256 * (last - first),
        )
        return [g.reshape(rows, 256 * (last - first)) for g in grads]

    grads_a = attend_back(0, group_cut, grad_att)
    grads_a, grad_att, arrived, arrived_up = together(grads_a, grad_att, arrived, arrived_up)
    arrived = down_sum.send(arrived)
    arrived_up = up_sum.send(arrived_up)
    grads_b = attend_back(group_cut, groups, grad_att)
    grads_b, arrived, arrived_up = together(grads_b, arrived, arrived_up)
    output_tokens = joined(outputs[:half], out_back)
    left, right = owned(down_sum.send(arrived))
    owned_down = jnp.concatenate([left, right], axis=1)
    arrived_up = up_sum.send(arrived_up)
    qkv_out = low(chips, rows_a, 3 * width // 2)
    qkv_mine, qkv_other = call(
        functools.partial(qkv_grad_kernel, chips, rows_a, cuts),
        tab,
        [(normed_first, None)] + [(g, None) for g in grads_a + grads_b],
        [],
        [(qkv_out, None), (qkv_out, None)],
        [],
        cost=2 * rows * width * 3 * width,
    )
    qkv_mine, qkv_other, grads_a, grads_b = together(qkv_mine, qkv_other, grads_a, grads_b)
    qkv_sum = steps_of(qkv_mine, qkv_other, 2)
    arrived = next(qkv_sum)

    def first_back(part, source, grad_hidden):
        here_tile = lambda columns: pl.BlockSpec((256, columns), lambda i, t: (part * (tiles // 2) + i, 0))
        return call(
            functools.partial(first_kernel, group_a, len(group_a.arrays), chips, cuts),
            tab,
            [(source, tile(width)), (gains, None), (grad_hidden, here_tile(width))]
            + [(g, here_tile(g.shape[1])) for g in grads_a + grads_b],
            group_a.arrays,
            [(low(half, width), tile(width))],
            [vmem((width, 3 * width), BF16), dma((group_a.copies(("qkv",)),))],
            grid=(tiles // 2,),
            cost=2 * half * width * 3 * width,
        )[0]

    grad_got = first_back(1, tok_got, grad_hidden)
    grad_back = lax.ppermute(grad_got, "seq", swap_x)
    grad_got, arrived, tok_own = together(grad_got, arrived, tok_own)
    arrived = qkv_sum.send(arrived)
    grad_own = first_back(0, tok_own, grad_hidden)
    grad_own, arrived_up = together(grad_own, arrived_up)
    arrived_up = up_sum.send(arrived_up)
    grad_own, arrived = together(grad_own, arrived)
    arrived = qkv_sum.send(arrived)
    arrived_up, arrived = together(arrived_up, arrived)
    arrived = qkv_sum.send(arrived)
    left, right = owned(up_sum.send(arrived_up))
    owned_up = jnp.concatenate([left[:, : ff // 2], right[:, : ff // 2]], axis=1)
    owned_out = jnp.concatenate([left[:, ff // 2 :], right[:, ff // 2 :]], axis=1)
    left, right = owned(qkv_sum.send(arrived))
    owned_qkv = jnp.concatenate([left, right], axis=1)
    grad_tokens = joined(grad_own, grad_back)

    scale = norm_gains.astype(F32)
    first_gain = jnp.sum(w_qkv.astype(F32) * owned_qkv, axis=1) / scale[:, 0]
    second_gain = jnp.sum(w_up.astype(F32) * owned_up, axis=1) / scale[:, 1]
    owned_gains = jnp.stack([first_gain, second_gain], axis=1)
    return (output_tokens, grad_tokens, owned_qkv, owned_out, owned_up, owned_down, owned_gains)


def solution(mesh):
    grid = Grid(mesh.shape["seq"], mesh.shape["clips"])
    shard = P(AXES, None)
    return jax.shard_map(
        functools.partial(body, grid),
        mesh=mesh,
        in_specs=(P("seq", "clips", None), P("clips"), shard, shard, shard, shard, shard, P("seq", "clips", None)),
        out_specs=(P("seq", "clips", None), P("seq", "clips", None), shard, shard, shard, shard, shard),
        check_vma=False,
    )
```

```python
import functools
import math

import jax
import jax.numpy as jnp
from jax import lax
from jax.experimental import pallas as pl
from jax.experimental.pallas import tpu as pltpu
from jax.sharding import PartitionSpec as P

HEAD_DIM = 64
CLIP = 512
EPSILON = 1e-05
AXES = ("seq", "clips")
LOG2E = 1.4426950408889634
SCORE_SCALE = HEAD_DIM ** (-0.5)
BF16 = jnp.bfloat16
F32 = jnp.float32
VMEM_BYTES = 58 * 1024 * 1024
SPARE_BYTES = 10 * 1024 * 1024


class Grid:
    def __init__(self, seq, clips):
        self.nx = seq
        self.clips = clips
        pairs = clips // 2
        bits = pairs.bit_length() - 1
        self.ny = 2 ** (bits // 3)
        self.nz = pairs // self.ny
        self.sizes = {"x": self.nx, "y": self.ny, "z": self.nz}
        self.chips = self.nx * self.ny * self.nz

    def index(self, x, z, y, c):
        return x * self.clips + (z * self.ny + y) * 2 + c

    def shift(self, axis, k):
        pairs = []
        for x in range(self.nx):
            for z in range(self.nz):
                for y in range(self.ny):
                    for c in range(2):
                        t = {"x": x, "y": y, "z": z}
                        t[axis] = (t[axis] + k) % self.sizes[axis]
                        pairs.append((self.index(x, z, y, c), self.index(t["x"], t["z"], t["y"], c)))
        return pairs

    def core_swap(self):
        return [(i, i ^ 1) for i in range(self.nx * self.clips)]

    def here(self):
        x = lax.axis_index("seq")
        rest = lax.axis_index("clips")
        return {"x": x, "z": rest // (2 * self.ny), "y": (rest // 2) % self.ny, "c": rest % 2}


def rel_of(grid, coords):
    return (coords["x"] * grid.ny + coords["y"]) * grid.nz + coords["z"]


def together(*values):
    return lax.optimization_barrier(values)


def exchange(grid, parts, axis):
    moved = []
    for k in range(1, grid.sizes[axis]):
        for array, spots in parts:
            moved.append((lax.ppermute(array, AXES, grid.shift(axis, k)), [{**s, axis: k} for s in spots]))
    return moved


def joined_parts(parts):
    if len(parts) == 1:
        return parts[0]
    return (jnp.concatenate([a for a, _ in parts], axis=0), [s for _, spots in parts for s in spots])


def gather_along_z(grid, piece):
    parts = [(piece[None], [{"x": 0, "y": 0, "z": 0}])]
    return parts + exchange(grid, parts, "z")


def lots_of(parts, cut):
    cut = min(cut, len(parts))
    return [joined_parts(p) for p in (parts[:cut], parts[cut:]) if p]


def arrays_of(parts):
    return [a for a, _ in parts]


def with_arrays(parts, arrays):
    return [(a, s) for a, (_, s) in zip(arrays, parts)]


def scatter_steps(grid, mine, other, cut):
    got = lax.ppermute(other, AXES, grid.core_swap())
    back = yield [got]
    (got,), held = (back[0], tuple(back[1:])) if isinstance(back, tuple) else (back, ())
    shape = (grid.ny, grid.nx, grid.nz) + mine.shape[1:]
    mine, got = mine.reshape(shape), got.reshape(shape)
    cut = min(cut, grid.nz)
    lots = [(lo, hi, axes) for lo, hi, axes in ((0, cut, "yx"), (cut, grid.nz, "xy")) if hi > lo]
    current = [[mine[:, :, lo:hi], got[:, :, lo:hi]] for lo, hi, _ in lots]
    for step in range(2):
        waiting = []
        for n, (_, _, axes) in enumerate(lots):
            axis = axes[step]
            dim = 1 if axis == "x" and step == 0 else 0
            pieces = [
                [lax.index_in_dim(c, k, dim, keepdims=False) for c in current[n]] for k in range(grid.sizes[axis])
            ]
            waiting.append([add_all(pieces[k]).astype(BF16) for k in range(1, grid.sizes[axis])])
            current[n] = pieces[0]
        if held:
            waiting, held = together(waiting, held)
        for n, (_, _, axes) in enumerate(lots):
            waiting[n] = [
                lax.ppermute(total, AXES, grid.shift(axes[step], k + 1)) for k, total in enumerate(waiting[n])
            ]
        flat = [a for received in waiting for a in received]
        back = yield (flat, *held) if held else flat
        flat, held = (back[0], tuple(back[1:])) if isinstance(back, tuple) else (list(back), ())
        for n, received in enumerate(waiting):
            current[n] = current[n] + flat[: len(received)]
            flat = flat[len(received) :]
    final = []
    for k in range(grid.nz):
        n = 0 if k < lots[0][1] else 1
        total = add_all([c[k - lots[n][0]] for c in current[n]])
        final.append(total if k == 0 else lax.ppermute(total.astype(BF16), AXES, grid.shift("z", k)))
    final[1:] = yield final[1:]
    yield add_all(final)


def add_all(items):
    total = items[0].astype(F32)
    for item in items[1:]:
        total = total + item.astype(F32)
    return total


def nn(a, b):
    return lax.dot_general(a, b, (((1,), (0,)), ((), ())), preferred_element_type=F32)


def nt(a, b):
    return lax.dot_general(a, b, (((1,), (1,)), ((), ())), preferred_element_type=F32)


def tn(a, b):
    return lax.dot_general(a, b, (((0,), (0,)), ((), ())), preferred_element_type=F32)


def normalized(values):
    centered = values - jnp.mean(values, axis=-1, keepdims=True)
    spread = jnp.mean(centered * centered, axis=-1, keepdims=True)
    root = lax.rsqrt(spread + EPSILON)
    return centered * root, root


def norm_back(z, root, scaled):
    return root * (
        scaled
        - jnp.mean(scaled, axis=-1, keepdims=True)
        - z * jnp.mean(scaled * z, axis=-1, keepdims=True)
    )


class Pieces:
    def __init__(self, chips, mine, theirs, fields):
        self.chips = chips
        self.arrays = [a for a, _ in mine] + [a for a, _ in theirs]
        self.spots = [s for _, s in mine] + [s for _, s in theirs]
        self.count_mine = len(mine)
        self.rows = self.arrays[0].shape[1]
        self.fields = fields

    def copies(self, wanted):
        total = 0
        for n, spots in enumerate(self.spots):
            for name, column, width, gain in self.fields:
                if name in wanted and not (gain and n >= self.count_mine):
                    total += len(spots)
        return total

    def start(self, refs, tab, wanted, sems, first):
        core = tab[2 * self.chips]
        started = {name: [] for name in wanted}
        n_sem = first
        for n, spots in enumerate(self.spots):
            for name, column, width, gain in self.fields:
                if name not in wanted or (gain and n >= self.count_mine):
                    continue
                for k, r in enumerate(spots):
                    row = pl.multiple_of(tab[r] * self.rows, 16)
                    if gain:
                        place = wanted[name].at[pl.ds(row, self.rows), :]
                    else:
                        side = core if n < self.count_mine else 1 - core
                        col = pl.multiple_of(side * width, 128)
                        place = wanted[name].at[pl.ds(row, self.rows), pl.ds(col, width)]
                    copy = pltpu.make_async_copy(
                        refs[n].at[k, :, column : column + width], place, sems.at[n_sem]
                    )
                    copy.start()
                    started[name].append(copy)
                    n_sem += 1
        return started


def hand_on(scratch, target, sem, step, steps):
    copy = pltpu.make_async_copy(scratch, target, sem.at[0])

    @pl.when(step == 0)
    def _():
        copy.start()

    @pl.when(step == steps - 1)
    def _():
        copy.wait()


def wait_all(copies):
    for copy in copies:
        copy.wait()


def emit(value, first_chip, rows, ref, columns, tab, chips):
    height = value.shape[0]
    low = value.astype(BF16)
    if rows >= height:
        ref[0, pl.ds(first_chip, height), columns] = low
    else:
        for a in range(height // rows):
            ref[tab[chips + first_chip + a], :, columns] = low[a * rows : (a + 1) * rows]


def by_side(core, mine, other, run):
    @pl.when(core == 0)
    def _():
        run(mine, other)

    @pl.when(core != 0)
    def _():
        run(other, mine)


def place_of(row, rows, chips):
    return row if chips == 1 else row // rows


def input_kernel(pieces, n_refs, chips, tab, own, got, *refs):
    sources, refs = refs[:n_refs], refs[n_refs:]
    packed, normed, gains, w_whole, w_qkv, gain_cols, sems, w_sem = refs
    i = pl.program_id(0)
    steps = pl.num_programs(0)
    width = own.shape[1]

    @pl.when(i == 0)
    def _():
        started = pieces.start(sources, tab, {"gain": gain_cols, "qkv": w_qkv}, sems, 0)
        wait_all(started["gain"])
        pick = (
            lax.broadcasted_iota(jnp.int32, (8, 128), 0) == lax.broadcasted_iota(jnp.int32, (8, 128), 1)
        ).astype(BF16)
        gains[...] = nt(pick, gain_cols[...])
        wait_all(started["qkv"])

    x = jnp.where(i < steps // 2, own[...], got[...]).astype(F32)
    z, _ = normalized(x)
    low = (z * gains[0:1, :]).astype(BF16)
    normed[...] = low
    for c in range(3):
        cols = slice(c * width, (c + 1) * width)
        packed[:, cols] = nn(low, w_qkv[:, cols]).astype(BF16)
    hand_on(w_qkv, w_whole, w_sem, i, steps)


def pair_of(ref, n):
    return ref[:, 0, :, 128 * n : 128 * (n + 1)].reshape(512, 128)


def fill_bias(bias, short):
    row_clip = (lax.broadcasted_iota(jnp.int32, (512, 512), 0) // 128) % 2
    col_clip = (lax.broadcasted_iota(jnp.int32, (512, 512), 1) // 128) % 2
    apart = jnp.logical_and(row_clip != col_clip, short != 0)
    bias[...] = jnp.where(apart, -1e30, 0.0)


def by_class(short, run):
    @pl.when(short == 0)
    def _():
        run(False)

    @pl.when(short != 0)
    def _():
        run(True)


def attend_kernel(chips, tab, q_ref, k_ref, v_ref, *refs):
    attended, log_totals, bias = refs[-3:]
    short = tab[2 * chips + 1]

    @pl.when(jnp.logical_and(pl.program_id(0) == 0, pl.program_id(1) == 0))
    def _():
        fill_bias(bias, short)

    def run(masked):
        lane = lax.broadcasted_iota(jnp.int32, (512, 128), 1)
        q, k, v = [[pair_of(ref, n) for n in range(2)] for ref in (q_ref, k_ref, v_ref)]

        def head_of(value, h):
            return jnp.where((lane // 64) == h, value, jnp.zeros_like(value))

        def scores(i):
            s = nt(head_of(q[i // 2], i % 2), k[i // 2])
            return s + bias[...] if masked else s

        logs = jnp.zeros((512, 128), F32)
        mixed = [0.0, 0.0]
        ahead = scores(0)
        for i in range(4):
            s, ahead = ahead, scores(i + 1) if i < 3 else None
            top_score = jnp.max(s, axis=1, keepdims=True) * (SCORE_SCALE * LOG2E)
            p = jnp.exp2(s * (SCORE_SCALE * LOG2E) - top_score)
            total = jnp.sum(p, axis=1, keepdims=True)
            logs = jnp.where(lane == i, top_score + jnp.log2(total), logs)
            mixed[i // 2] = mixed[i // 2] + nn(p.astype(BF16), head_of(v[i // 2], i % 2)) * (1.0 / total)
        for n in range(2):
            attended[:, 0, :, 128 * n : 128 * (n + 1)] = mixed[n].astype(BF16).reshape(2, 256, 128)
        turned = logs.T
        for i in range(4):
            log_totals[i] = turned[i : i + 1, :]

    by_class(short, run)


def gelu_both(u):
    below = 0.5 + 0.5 * lax.erf(u * (0.5**0.5))
    bell = jnp.exp2(u * u * (-0.5 * LOG2E)) * 0.3989422804014327
    return u * below, below + u * bell


def middle_kernel(pieces, n_refs, chips, tab, attended, own, got, gains, *refs):
    sources, refs = refs[:n_refs], refs[n_refs:]
    hidden, normed, w_whole, w_out, sems, w_sem = refs
    i = pl.program_id(0)

    @pl.when(i == 0)
    def _():
        wait_all(pieces.start(sources, tab, {"out": w_out}, sems, 0)["out"])

    x = jnp.where(i < pl.num_programs(0) // 2, own[...], got[...]).astype(F32)
    h = x + nn(attended[...], w_out[...])
    hidden[...] = h
    z, _ = normalized(h)
    normed[...] = (z * gains[1:2, :]).astype(BF16)
    hand_on(w_out, w_whole, w_sem, i, pl.num_programs(0))


def up_tiles(normed, weight, active, slope):
    for i in range(normed.shape[0] // 256):
        rows = slice(256 * i, 256 * (i + 1))
        a, s = gelu_both(nn(normed[rows, :], weight))
        active[rows, :] = a.astype(BF16)
        slope[rows, :] = s.astype(BF16)


def up_kernel(pieces, n_refs, chips, tab, normed, *refs):
    sources, refs = refs[:n_refs], refs[n_refs:]
    active, slope, w_whole, w_up, sems, w_sem = refs
    width = normed.shape[1]
    j = pl.program_id(0)

    @pl.when(j == 0)
    def _():
        wait_all(pieces.start(sources, tab, {"up": w_up}, sems, 0)["up"])

    up_tiles(normed, w_up[:, pl.ds(pl.multiple_of(j * width, 128), width)], active, slope)
    hand_on(w_up, w_whole, w_sem, j, pl.num_programs(0))


def up_rest_kernel(tab, normed, w_up, _active, _slope, active, slope):
    up_tiles(normed, w_up[...], active, slope)


def down_grad_kernel(chips, rows_down, tab, active, cot_own, cot_got, down_mine, down_other):
    half, width = cot_own.shape
    j = pl.program_id(0)

    def run(left, right):
        for m in range(2):
            piece = slice(384 * m, 384 * (m + 1))
            grad = tn(active[:half, piece], cot_own[...]) + tn(active[half:, piece], cot_got[...])
            start = place_of(width * j + 384 * m, rows_down, chips)
            emit(grad[:, : width // 2], start, rows_down, left, slice(None), tab, chips)
            emit(grad[:, width // 2 :], start, rows_down, right, slice(None), tab, chips)

    by_side(tab[2 * chips], down_mine, down_other, run)


def down_back_kernel(chips, rows_up, tab, cot_own, cot_got, normed, slope, w_down, grad_up, up_mine, up_other):
    half, width = cot_own.shape
    j = pl.program_id(0)
    steps = pl.num_programs(0)

    offset = pl.multiple_of(lax.rem(j, steps // 2) * width, 128)

    def run(target):
        for part, cot in enumerate((cot_own, cot_got)):
            for i in range(half // 256):
                inner = slice(256 * i, 256 * (i + 1))
                rows = slice(part * half + 256 * i, part * half + 256 * (i + 1))
                grad_up[rows, :] = (nt(cot[inner, :], w_down[...]) * slope[rows, :].astype(F32)).astype(BF16)
        for m in range(2):
            grad = tn(normed[:, 384 * m : 384 * (m + 1)], grad_up[...])
            emit(grad, place_of(384 * m, rows_up, chips), rows_up, target, pl.ds(offset, width), tab, chips)

    rel = (j // (steps // 2)) ^ tab[2 * chips]

    @pl.when(rel == 0)
    def _():
        run(up_mine)

    @pl.when(rel != 0)
    def _():
        run(up_other)


def up_back_kernel(
    chips, rows_up, tab, grad_up, attended, gains, cot_own, cot_got, hidden, _mine, _other, w_up, w_out, *refs
):
    grad_hidden, grad_att, out_mine, out_other, total_out = refs
    i = pl.program_id(0)
    steps = pl.num_programs(0)
    width = hidden.shape[1]

    @pl.when(i == 0)
    def _():
        total_out[...] = jnp.zeros_like(total_out)

    cot = jnp.where(i < steps // 2, cot_own[...], cot_got[...]).astype(F32)
    e = nt(grad_up[...], w_up[...])
    z, root = normalized(hidden[...])
    total = cot + norm_back(z, root, e * gains[1:2, :])
    grad_hidden[...] = total
    low = total.astype(BF16)
    grad_att[...] = nt(low, w_out[...]).astype(BF16)
    total_out[...] += tn(attended[...], low)

    @pl.when(i == steps - 1)
    def _():
        def run(left, right):
            for m in range(2):
                start = place_of(384 * m, rows_up, chips)
                for side, ref in enumerate((left, right)):
                    value = total_out[384 * m : 384 * (m + 1), side * (width // 2) : (side + 1) * (width // 2)]
                    emit(value, start, rows_up, ref, slice(None), tab, chips)

        by_side(tab[2 * chips], out_mine, out_other, run)


def output_kernel(pieces, n_refs, chips, tab, active, hidden, *refs):
    sources, refs = refs[:n_refs], refs[n_refs:]
    out, w_whole, w_down, sems, w_sem = refs

    @pl.when(pl.program_id(0) == 0)
    def _():
        wait_all(pieces.start(sources, tab, {"down": w_down}, sems, 0)["down"])

    out[...] = (hidden[...] + nn(active[...], w_down[...])).astype(BF16)
    hand_on(w_down, w_whole, w_sem, pl.program_id(0), pl.num_programs(0))


def attend_back_kernel(chips, tab, q_ref, k_ref, v_ref, o_ref, d_ref, log_totals, grad_q_ref, grad_k_ref, grad_v_ref, bias):
    short = tab[2 * chips + 1]

    @pl.when(jnp.logical_and(pl.program_id(0) == 0, pl.program_id(1) == 0))
    def _():
        fill_bias(bias, short)

    def put(ref, n, value):
        ref[:, 0, :, 128 * n : 128 * (n + 1)] = value.astype(BF16).reshape(2, 256, 128)

    def run(masked):
        lane = lax.broadcasted_iota(jnp.int32, (512, 128), 1)
        for n in range(2):
            q, k, v, o, d = [pair_of(r, n) for r in (q_ref, k_ref, v_ref, o_ref, d_ref)]
            k_t = k.T
            dots = (o.astype(F32) * d.astype(F32)).T
            grad_q, grad_k, grad_v = [], [], []
            for h in range(2):
                here = (lane // 64) == h
                zero = jnp.zeros_like(k)
                s = nt(jnp.where(here, k, zero), q)
                if masked:
                    s = s + bias[...]
                p = jnp.exp2(s * (SCORE_SCALE * LOG2E) - log_totals[2 * n + h])
                grad_v.append(nn(p.astype(BF16), jnp.where(here, d, zero)))
                grad_p = nt(jnp.where(here, v, zero), d)
                delta = jnp.sum(dots[64 * h : 64 * h + 64, :], axis=0, keepdims=True)
                grad_s = (p * (grad_p - delta)).astype(BF16)
                grad_k.append(nn(grad_s, jnp.where(here, q, zero)))
                grad_q.append(nn(k_t[64 * h : 64 * h + 64, :], grad_s))
            put(grad_q_ref, n, jnp.concatenate(grad_q, axis=0).T * SCORE_SCALE)
            put(grad_k_ref, n, (grad_k[0] + grad_k[1]) * SCORE_SCALE)
            put(grad_v_ref, n, grad_v[0] + grad_v[1])

    by_class(short, run)


def qkv_grad_kernel(chips, rows_qkv, cuts, tab, normed, *refs):
    grads, mine, other = refs[:-2], refs[-2], refs[-1]
    width = normed.shape[1]
    wide = 3 * width // 2

    def run(*sides):
        for n, ref in enumerate(grads):
            base = (n % 3) * width + cuts[n // 3]
            size = ref.shape[1]
            for m in range(2):
                grad = tn(normed[:, 384 * m : 384 * (m + 1)], ref[...])
                start = place_of(384 * m, rows_qkv, chips)
                at = base
                while at < base + size:
                    side = at // wide
                    end = min(base + size, (side + 1) * wide)
                    columns = slice(at - side * wide, end - side * wide)
                    emit(grad[:, at - base : end - base], start, rows_qkv, sides[side], columns, tab, chips)
                    at = end

    by_side(tab[2 * chips], mine, other, run)


def first_kernel(cuts, tab, own, got, gains, grad_hidden, w_qkv, *refs):
    grads, (out_own, out_got) = refs[:-2], refs[-2:]
    width = own.shape[1]
    here = pl.program_id(0) < pl.num_programs(0) // 2
    e = 0.0
    for n, grad in enumerate(grads):
        base, lot = (n % 3) * width, n // 3
        e = e + nt(grad[...], w_qkv[:, base + cuts[lot] : base + cuts[lot + 1]])
    z, root = normalized(jnp.where(here, own[...], got[...]).astype(F32))
    value = (grad_hidden[...] + norm_back(z, root, e * gains[0:1, :])).astype(BF16)

    @pl.when(here)
    def _():
        out_own[...] = value

    @pl.when(jnp.logical_not(here))
    def _():
        out_got[...] = value


def whole(shape):
    return pl.BlockSpec(shape, lambda *_: (0,) * len(shape))


anywhere = pl.BlockSpec(memory_space=pl.ANY)


def call(kernel, tab, inputs, piece_arrays, outs, scratch, grid=(1,), cost=0, aliases=None):
    specs = [spec or whole(a.shape) for a, spec in inputs]
    specs = specs + [pl.BlockSpec(memory_space=pltpu.HBM) for _ in piece_arrays]
    blocks = [(a, spec) for a, spec in inputs] + [(o, spec) for o, spec in outs]
    need = SPARE_BYTES
    for array, spec in blocks:
        if spec is anywhere:
            continue
        size = jnp.dtype(array.dtype).itemsize
        for extent in spec.block_shape if spec else array.shape:
            size *= extent
        need += 2 * size
    for buffer in scratch:
        if hasattr(buffer, "shape") and buffer.dtype in (BF16, F32):
            size = buffer.dtype.itemsize if hasattr(buffer.dtype, "itemsize") else jnp.dtype(buffer.dtype).itemsize
            for extent in buffer.shape:
                size *= extent
            need += size
    moved = sum(a.size * a.dtype.itemsize for a, _ in inputs) + sum(a.size * a.dtype.itemsize for a in piece_arrays)
    moved += sum(math.prod(o.shape) * jnp.dtype(o.dtype).itemsize for o, _ in outs)
    inputs = [
        (pltpu.with_memory_space_constraint(a, pltpu.HBM) if a.size > 2**21 and spec is not None else a, spec)
        for a, spec in inputs
    ]
    return pl.pallas_call(
        kernel,
        out_shape=[o for o, _ in outs],
        input_output_aliases=aliases or {},
        grid_spec=pltpu.PrefetchScalarGridSpec(
            num_scalar_prefetch=1,
            grid=grid,
            in_specs=specs,
            out_specs=[spec or whole(o.shape) for o, spec in outs],
            scratch_shapes=scratch,
        ),
        compiler_params=pltpu.CompilerParams(
            dimension_semantics=("arbitrary",) * len(grid), vmem_limit_bytes=min(need, VMEM_BYTES)
        ),
        cost_estimate=pl.CostEstimate(flops=cost, bytes_accessed=moved, transcendentals=0),
    )(tab, *[a for a, _ in inputs], *piece_arrays)


def body(grid, tokens, clip_class, w_qkv, w_out, w_up, w_down, norm_gains, cotangent):
    rows, width = tokens.shape[1:]
    half = rows // 2
    ff = w_up.shape[1]
    here = grid.here()
    mx = here["x"]
    fast = (2 * w_qkv.shape[0]) % 16 == 0 and (2 * w_down.shape[0]) % 16 == 0
    chips = grid.chips if fast else 1

    def split(array):
        own = lax.dynamic_slice(array[0], (mx * half, 0), (half, width))
        away = lax.dynamic_slice(array[0], ((1 - mx) * half, 0), (half, width))
        return own, away

    swap_x = [(0, 1), (1, 0)]
    tok_own, tok_away = split(tokens)
    cot_own, cot_away = split(cotangent)

    if fast:
        spots = [(x, y, z) for x in range(grid.nx) for y in range(grid.ny) for z in range(grid.nz)]
        chip_at = [
            (((mx - x) % grid.nx) * grid.nz + ((here["z"] - z) % grid.nz)) * grid.ny + ((here["y"] - y) % grid.ny)
            for x, y, z in spots
        ]
        place_at = []
        for a in range(chips):
            x, z, y = a // (grid.nz * grid.ny), (a // grid.ny) % grid.nz, a % grid.ny
            rx, rz, ry = (x - mx) % grid.nx, (z - here["z"]) % grid.nz, (y - here["y"]) % grid.ny
            place_at.append((ry * grid.nx + rx) * grid.nz + rz)
        core = here["c"]
    else:
        chip_at, place_at, core = [jnp.int32(0)], [jnp.int32(0)], jnp.int32(0)
    tab = jnp.stack([jnp.asarray(v, jnp.int32) for v in chip_at + place_at + [core, clip_class[0]]])

    def side_of(weight, side):
        wide = weight.shape[1] // 2
        return lax.dynamic_slice(weight, (0, side * wide), (weight.shape[0], wide))

    gain_block = jnp.pad(norm_gains, ((0, 0), (0, 126)))
    fields_a = [("qkv", 0, 3 * width // 2, False), ("gain", 3 * width // 2, 128, True)]
    fields_b = [("up", 0, ff // 2, False), ("out", ff // 2, width // 2, False)]
    fields_c = [("down", 0, width // 2, False)]
    swap_core = functools.partial(lax.ppermute, axis_name=AXES, perm=grid.core_swap())
    if fast:
        def sides(side, group):
            if group == 0:
                return jnp.concatenate([side_of(w_qkv, side), gain_block], axis=1)
            if group == 1:
                return jnp.concatenate([side_of(w_up, side), side_of(w_out, side)], axis=1)
            return side_of(w_down, side)

        def with_partner(group):
            keep, other = sides(core, group), swap_core(sides(1 - core, group))
            return jnp.concatenate(
                [jnp.where(core == 0, keep, other), jnp.where(core == 0, other, keep)], axis=0
            )

        tok_away, w_qkv = together(tok_away, w_qkv)
        tok_got = lax.ppermute(tok_away, "seq", swap_x)
        piece_a = with_partner(0)
        piece_a, w_up, w_out, w_down = together(piece_a, w_up, w_out, w_down)
        piece_b, piece_c = with_partner(1), with_partner(2)

        def near_of(lots):
            return [exchange(grid, [lot], axis) for lot, axis in zip(lots, "xy")]

        def widened(lots, near):
            return [joined_parts([lot] + moved) for lot, moved in zip(lots, near)]

        def far_of(wide):
            far = []
            for lot, axis in zip(wide, "yx"):
                far += exchange(grid, [lot], axis)
            return far

        def flat(groups):
            return [part for group in groups for part in group]

        def swapped(parts):
            return [(swap_core(a), s) for a, s in parts]

        def pieces_from(mine, theirs, fields):
            named = lambda parts: [(a, [rel_of(grid, s) for s in spots]) for a, spots in parts]
            return Pieces(chips, named(mine), named(theirs), fields)

        def finish(mine, fields):
            mine = [(a, [rel_of(grid, s) for s in spots]) for a, spots in mine]
            theirs = [(swap_core(a), s) for a, s in mine]
            return Pieces(chips, mine, theirs, fields)

        z_a = gather_along_z(grid, piece_a)
        arrays, tok_got, piece_b = together(arrays_of(z_a), tok_got, piece_b)
        z_a = lots_of(with_arrays(z_a, arrays), 2)
        near_a = near_of(z_a)
        z_b = gather_along_z(grid, piece_b)
        arrays = lax.optimization_barrier(arrays_of(flat(near_a)))
        wide_a = widened(z_a, [[part] for part in with_arrays(flat(near_a), arrays)])
        far_a = far_of(wide_a)
        all_a = wide_a + far_a
        arrays_a, z_own, piece_c = together(arrays_of(all_a), z_b[0][0], piece_c)
        z_b = with_arrays(z_b, [z_own] + arrays_of(z_b[1:]))
        group_a = finish(with_arrays(all_a, arrays_a), fields_a)
        z_b = lots_of(with_arrays(z_b, lax.optimization_barrier(arrays_of(z_b))), 2)
        near_b = near_of(z_b)
        z_c = gather_along_z(grid, piece_c)
    else:
        full = [lax.all_gather(w, AXES, axis=0, tiled=True) for w in (w_qkv, w_out, w_up, w_down, gain_block)]

        def natural(parts, fields):
            sides = []
            for side in range(2):
                cut = [p if p.shape[1] == 128 else p[:, side * (p.shape[1] // 2) : (side + 1) * (p.shape[1] // 2)] for p in parts]
                sides.append([(jnp.concatenate(cut, axis=1)[None], [0])])
            return Pieces(1, sides[0], sides[1], fields)

        group_a = natural([full[0], full[4]], fields_a)
        group_b = natural([full[2], full[1]], fields_b)
        group_c = natural([full[3]], fields_c)
        tok_got = lax.ppermute(tok_away, "seq", swap_x)
        cot_got = lax.ppermute(cot_away, "seq", swap_x)

    sds = jax.ShapeDtypeStruct
    heads = width // HEAD_DIM
    rows_a, rows_c = (2 * w_qkv.shape[0], 2 * w_down.shape[0]) if fast else (width, ff)
    dma = pltpu.SemaphoreType.DMA
    vmem = pltpu.VMEM
    tiles = rows // 256
    tile = lambda columns: pl.BlockSpec((256, columns), lambda i, t: (i, 0))
    own_tile = pl.BlockSpec((256, width), lambda i, t: (jnp.minimum(i, tiles // 2 - 1), 0))
    got_tile = pl.BlockSpec((256, width), lambda i, t: (jnp.maximum(i - tiles // 2, 0), 0))
    chunk = pl.BlockSpec((rows, width), lambda j, t: (0, j))
    low = lambda *shape: sds(shape, BF16)

    packed, normed_first, gains, whole_qkv = call(
        functools.partial(input_kernel, group_a, len(group_a.arrays), chips),
        tab,
        [(tok_own, own_tile), (tok_got, got_tile)],
        group_a.arrays,
        [(pltpu.HBM((rows, 3 * width), BF16), tile(3 * width)), (low(rows, width), tile(width)), (sds((8, width), F32), None),
         (pltpu.HBM((width, 3 * width), BF16), anywhere)],
        [vmem((width, 3 * width), BF16), vmem((width, 128), BF16), dma((group_a.copies(("qkv", "gain")),)), dma((1,))],
        grid=(tiles,),
        cost=2 * rows * width * 3 * width,
    )

    if fast:
        packed, arrays_b, arrays_c = together(packed, arrays_of(flat(near_b)), arrays_of(z_c))
        z_c = with_arrays(z_c, arrays_c)
        wide_b = widened(z_b, [[part] for part in with_arrays(flat(near_b), arrays_b)])
        far_b = far_of(wide_b)
        their_wide_b = swapped(wide_b)

    clip_blocks = half // 256
    by_clip = lambda a: a.reshape(2, clip_blocks, 256, a.shape[1])
    clip_shape = low(2, clip_blocks, 256, width)
    step = width // 256
    totals_shape = sds((clip_blocks * heads, 1, 512), F32)

    def attend(first, last, packed, earlier):
        at = lambda base: pl.BlockSpec((2, 1, 256, 256), lambda b, g, t: (0, first + b, 0, base + g))
        totals = pl.BlockSpec((4, 1, 512), lambda b, g, t: ((first + b) * (heads // 4) + g, 0, 0))
        return call(
            functools.partial(attend_kernel, chips),
            tab,
            [(by_clip(packed), at(0)), (by_clip(packed), at(step)), (by_clip(packed), at(2 * step))]
            + [(a, anywhere) for a in earlier],
            [],
            [(clip_shape, at(0)), (totals_shape, totals)],
            [vmem((512, 512), F32)],
            grid=(last - first, heads // 4),
            cost=8 * rows * 512 * width * (last - first) // clip_blocks,
            aliases={4: 0, 5: 1} if earlier else None,
        )

    attended, log_totals = attend(0, clip_blocks, packed, [])
    attended = attended.reshape(rows, width)

    if fast:
        attended, arrays_b, arrays_w, arrays_c = together(
            attended, arrays_of(far_b), arrays_of(their_wide_b), arrays_of(z_c)
        )
        far_b, their_wide_b = with_arrays(far_b, arrays_b), with_arrays(their_wide_b, arrays_w)
        group_b = pieces_from(wide_b + far_b, their_wide_b + swapped(far_b), fields_b)
        z_c = [joined_parts(with_arrays(z_c, arrays_c))]
        near_c = exchange(grid, z_c, "x")
        straight_c = exchange(grid, z_c, "y")

    hidden, normed_second, whole_out = call(
        functools.partial(middle_kernel, group_b, len(group_b.arrays), chips),
        tab,
        [(attended, tile(width)), (tok_own, own_tile), (tok_got, got_tile), (gains, None)],
        group_b.arrays,
        [
            (sds((rows, width), F32), tile(width)), (low(rows, width), tile(width)),
            (pltpu.HBM((width, width), BF16), anywhere),
        ],
        [vmem((width, width), BF16), dma((group_b.copies(("out",)),)), dma((1,))],
        grid=(tiles,),
        cost=2 * rows * width * width,
    )

    steps = ff // width

    split_up = steps // 2
    wide_hbm = pltpu.HBM((rows, ff), BF16)
    active, slope, whole_up = call(
        functools.partial(up_kernel, group_b, len(group_b.arrays), chips),
        tab,
        [(normed_second, None)],
        group_b.arrays,
        [(wide_hbm, chunk), (wide_hbm, chunk), (pltpu.HBM((width, ff), BF16), anywhere)],
        [vmem((width, ff), BF16), dma((group_b.copies(("up",)),)), dma((1,))],
        grid=(split_up,),
        cost=2 * rows * width * width * split_up,
    )
    if fast:
        active, slope, normed_second, arrays_c, arrays_s, cot_away = together(
            active, slope, normed_second, arrays_of(near_c), arrays_of(straight_c), cot_away
        )
        near_c, straight_c = with_arrays(near_c, arrays_c), with_arrays(straight_c, arrays_s)
        far_c = exchange(grid, near_c, "y")
        cot_got = lax.ppermute(cot_away, "seq", swap_x)
    rest = pl.BlockSpec((rows, width), lambda j, t: (0, split_up + j))
    active, slope = call(
        up_rest_kernel,
        tab,
        [
            (normed_second, None), (whole_up, pl.BlockSpec((width, width), lambda j, t: (0, split_up + j))),
            (active, anywhere), (slope, anywhere),
        ],
        [],
        [(wide_hbm, rest), (wide_hbm, rest)],
        [],
        grid=(steps - split_up,),
        cost=2 * rows * width * width * (steps - split_up),
        aliases={3: 0, 4: 1},
    )
    if fast:
        all_c = z_c + near_c + straight_c + far_c
        active, slope, arrays_c, cot_got = together(active, slope, arrays_of(all_c), cot_got)
        all_c = with_arrays(all_c, arrays_c)
        theirs_c = swapped(all_c)
    down_out = low(chips, rows_c, width // 2)
    down_mine, down_other = call(
        functools.partial(down_grad_kernel, chips, rows_c),
        tab,
        [(active, chunk), (cot_own, None), (cot_got, None)],
        [],
        [(down_out, None), (down_out, None)],
        [],
        grid=(steps,),
        cost=2 * rows * width * ff,
    )

    def steps_of(mine, other, cut):
        if fast:
            return scatter_steps(grid, mine, other, cut)

        def plain():
            whole_sum = jnp.concatenate([mine[0], other[0]], axis=1)
            back = yield []
            for _ in range(3):
                back = yield back
            yield lax.psum_scatter(whole_sum, AXES, scatter_dimension=0, tiled=True).astype(F32)

        return plain()

    def owned(total):
        if not fast:
            return total[:, : total.shape[1] // 2], total[:, total.shape[1] // 2 :]
        height = total.shape[0] // 2
        keep = lax.dynamic_slice(total, (core * height, 0), (height, total.shape[1]))
        away = lax.dynamic_slice(total, ((1 - core) * height, 0), (height, total.shape[1]))
        got = swap_core(away.astype(BF16)).astype(F32)
        return jnp.where(core == 0, keep, got), jnp.where(core == 0, got, keep)

    if fast:
        down_mine, down_other, active, arrays_c = together(down_mine, down_other, active, arrays_of(theirs_c))
        group_c = pieces_from(all_c, with_arrays(theirs_c, arrays_c), fields_c)
    outputs, whole_down = call(
        functools.partial(output_kernel, group_c, len(group_c.arrays), chips),
        tab,
        [(active, tile(ff)), (hidden, tile(width))],
        group_c.arrays,
        [(low(rows, width), tile(width)), (pltpu.HBM((ff, width), BF16), anywhere)],
        [vmem((ff, width), BF16), dma((group_c.copies(("down",)),)), dma((1,))],
        grid=(tiles,),
        cost=2 * rows * width * ff,
    )
    down_sum = steps_of(down_mine, down_other, 2)
    arrived = next(down_sum)
    outputs, arrived, slope = together(outputs, arrived, slope)
    arrived = down_sum.send(arrived)
    def joined(own, back):
        first = mx == 0
        return jnp.concatenate([jnp.where(first, own, back), jnp.where(first, back, own)], axis=0)[None]

    up_part = pl.BlockSpec((chips, rows_a, ff // 2), lambda *_: (0, 0, 0))
    out_part = pl.BlockSpec((chips, rows_a, width // 2), lambda *_: (0, 0, ff // width))
    up_out = low(chips, rows_a, ff // 2 + width // 2)
    grad_up, up_mine, up_other = call(
        functools.partial(down_back_kernel, chips, rows_a),
        tab,
        [
            (cot_own, None), (cot_got, None), (normed_second, None), (slope, chunk),
            (whole_down, pl.BlockSpec((width, width), lambda j, t: (j, 0))),
        ],
        [],
        [(pltpu.HBM((rows, ff), BF16), chunk), (up_out, up_part), (up_out, up_part)],
        [],
        grid=(steps,),
        cost=4 * rows * width * ff,
    )
    grad_up, up_mine, up_other, arrived = together(grad_up, up_mine, up_other, arrived)
    arrived = down_sum.send(arrived)
    quarter = half // 2
    out_first = lax.ppermute(outputs[half : half + quarter], "seq", swap_x)
    grad_hidden, grad_att, up_mine, up_other = call(
        functools.partial(up_back_kernel, chips, rows_a),
        tab,
        [
            (grad_up, tile(ff)), (attended, tile(width)), (gains, None), (cot_own, own_tile), (cot_got, got_tile),
            (hidden, tile(width)), (up_mine, anywhere), (up_other, anywhere),
            (whole_up, None), (whole_out, None),
        ],
        [],
        [(sds((rows, width), F32), tile(width)), (low(rows, width), tile(width)), (up_out, out_part), (up_out, out_part)],
        [vmem((width, width), F32)],
        grid=(tiles,),
        cost=2 * rows * width * ff + 4 * rows * width * width,
        aliases={7: 2, 8: 3},
    )
    grad_att, grad_hidden, up_mine, up_other, arrived, out_first, out_next = together(
        grad_att, grad_hidden, up_mine, up_other, arrived, out_first, outputs[half + quarter :]
    )
    out_second = lax.ppermute(out_next, "seq", swap_x)
    arrived = down_sum.send(arrived)
    up_sum = steps_of(up_mine, up_other, 2)
    arrived_up = next(up_sum)

    groups = heads // 4
    group_cut = max(1, groups // 3)
    cuts = [0, 256 * group_cut, width]

    def attend_back(first, last, grad_att):
        at = lambda base: pl.BlockSpec((2, 1, 256, 256), lambda b, g, t: (0, b, 0, base + first + g))
        to = pl.BlockSpec((2, 1, 256, 256), lambda b, g, t: (0, b, 0, g))
        totals = pl.BlockSpec((4, 1, 512), lambda b, g, t: (b * groups + first + g, 0, 0))
        shape = low(2, clip_blocks, 256, 256 * (last - first))
        grads = call(
            functools.partial(attend_back_kernel, chips),
            tab,
            [
                (by_clip(packed), at(0)), (by_clip(packed), at(step)), (by_clip(packed), at(2 * step)),
                (by_clip(attended), at(0)), (by_clip(grad_att), at(0)), (log_totals, totals),
            ],
            [],
            [(shape, to)] * 3,
            [vmem((512, 512), F32)],
            grid=(clip_blocks, last - first),
            cost=30 * rows * 512 * 256 * (last - first),
        )
        return [g.reshape(rows, 256 * (last - first)) for g in grads]

    grads_a = attend_back(0, group_cut, grad_att)
    grads_a, grad_att, arrived_up, out_second = together(grads_a, grad_att, arrived_up, out_second)
    arrived_up = up_sum.send(arrived_up)
    grads_b = attend_back(group_cut, groups, grad_att)
    grads_b, arrived_up, arrived = together(grads_b, arrived_up, arrived)
    left, right = owned(down_sum.send(arrived))
    owned_down = jnp.concatenate([left, right], axis=1)
    arrived_up, grads_b, normed_first = up_sum.send((arrived_up, grads_b, normed_first))
    qkv_out = low(chips, rows_a, 3 * width // 2)
    qkv_mine, qkv_other = call(
        functools.partial(qkv_grad_kernel, chips, rows_a, cuts),
        tab,
        [(normed_first, None)] + [(g, None) for g in grads_a + grads_b],
        [],
        [(qkv_out, None), (qkv_out, None)],
        [],
        cost=2 * rows * width * 3 * width,
    )
    qkv_mine, qkv_other, grads_a, grads_b = together(qkv_mine, qkv_other, grads_a, grads_b)
    qkv_sum = steps_of(qkv_mine, qkv_other, 2)
    arrived = next(qkv_sum)

    tok_own, arrived, arrived_up = together(tok_own, arrived, arrived_up)
    arrived_up = up_sum.send(arrived_up)
    arrived = qkv_sum.send(arrived)
    grad_own, grad_got = call(
        functools.partial(first_kernel, cuts),
        tab,
        [
            (tok_own, own_tile), (tok_got, got_tile), (gains, None), (grad_hidden, tile(width)), (whole_qkv, None),
        ]
        + [(g, tile(g.shape[1])) for g in grads_a + grads_b],
        [],
        [(low(half, width), own_tile), (low(half, width), got_tile)],
        [],
        grid=(tiles,),
        cost=2 * rows * width * 3 * width,
    )
    grad_got, grad_own, arrived = together(grad_got, grad_own, arrived)
    arrived = qkv_sum.send(arrived)
    grad_back = lax.ppermute(grad_got, "seq", swap_x)
    arrived_up, arrived, out_first, out_second = together(arrived_up, arrived, out_first, out_second)
    arrived = qkv_sum.send(arrived)
    left, right = owned(up_sum.send(arrived_up))
    owned_up = jnp.concatenate([left[:, : ff // 2], right[:, : ff // 2]], axis=1)
    owned_out = jnp.concatenate([left[:, ff // 2 :], right[:, ff // 2 :]], axis=1)
    output_tokens = joined(outputs[:half], jnp.concatenate([out_first, out_second], axis=0))
    left, right = owned(qkv_sum.send(arrived))
    owned_qkv = jnp.concatenate([left, right], axis=1)
    grad_tokens = joined(grad_own, grad_back)

    scale = norm_gains.astype(F32)
    first_gain = jnp.sum(w_qkv.astype(F32) * owned_qkv, axis=1) / scale[:, 0]
    second_gain = jnp.sum(w_up.astype(F32) * owned_up, axis=1) / scale[:, 1]
    owned_gains = jnp.stack([first_gain, second_gain], axis=1)
    return (output_tokens, grad_tokens, owned_qkv, owned_out, owned_up, owned_down, owned_gains)


def solution(mesh):
    grid = Grid(mesh.shape["seq"], mesh.shape["clips"])
    shard = P(AXES, None)
    return jax.shard_map(
        functools.partial(body, grid),
        mesh=mesh,
        in_specs=(P("seq", "clips", None), P("clips"), shard, shard, shard, shard, shard, P("seq", "clips", None)),
        out_specs=(P("seq", "clips", None), P("seq", "clips", None), shard, shard, shard, shard, shard),
        check_vma=False,
    )
```

```python
import functools
import math

import jax
import jax.numpy as jnp
from jax import lax
from jax.experimental import pallas as pl
from jax.experimental.pallas import tpu as pltpu
from jax.sharding import PartitionSpec as P

HEAD_DIM = 64
CLIP = 512
EPSILON = 1e-05
AXES = ("seq", "clips")
LOG2E = 1.4426950408889634
SCORE_SCALE = HEAD_DIM ** (-0.5)
BF16 = jnp.bfloat16
F32 = jnp.float32
VMEM_BYTES = 58 * 1024 * 1024
SPARE_BYTES = 10 * 1024 * 1024


class Grid:
    def __init__(self, seq, clips):
        self.nx = seq
        self.clips = clips
        pairs = clips // 2
        bits = pairs.bit_length() - 1
        self.ny = 2 ** (bits // 3)
        self.nz = pairs // self.ny
        self.sizes = {"x": self.nx, "y": self.ny, "z": self.nz}
        self.chips = self.nx * self.ny * self.nz

    def index(self, x, z, y, c):
        return x * self.clips + (z * self.ny + y) * 2 + c

    def shift(self, axis, k):
        pairs = []
        for x in range(self.nx):
            for z in range(self.nz):
                for y in range(self.ny):
                    for c in range(2):
                        t = {"x": x, "y": y, "z": z}
                        t[axis] = (t[axis] + k) % self.sizes[axis]
                        pairs.append((self.index(x, z, y, c), self.index(t["x"], t["z"], t["y"], c)))
        return pairs

    def core_swap(self):
        return [(i, i ^ 1) for i in range(self.nx * self.clips)]

    def here(self):
        x = lax.axis_index("seq")
        rest = lax.axis_index("clips")
        return {"x": x, "z": rest // (2 * self.ny), "y": (rest // 2) % self.ny, "c": rest % 2}


def rel_of(grid, coords):
    return (coords["x"] * grid.ny + coords["y"]) * grid.nz + coords["z"]


def together(*values):
    return lax.optimization_barrier(values)


def exchange(grid, parts, axis):
    moved = []
    for k in range(1, grid.sizes[axis]):
        for array, spots in parts:
            moved.append((lax.ppermute(array, AXES, grid.shift(axis, k)), [{**s, axis: k} for s in spots]))
    return moved


def joined_parts(parts):
    if len(parts) == 1:
        return parts[0]
    return (jnp.concatenate([a for a, _ in parts], axis=0), [s for _, spots in parts for s in spots])


def gather_along_z(grid, piece):
    parts = [(piece[None], [{"x": 0, "y": 0, "z": 0}])]
    return parts + exchange(grid, parts, "z")


def lots_of(parts, cut):
    cut = min(cut, len(parts))
    return [joined_parts(p) for p in (parts[:cut], parts[cut:]) if p]


def arrays_of(parts):
    return [a for a, _ in parts]


def with_arrays(parts, arrays):
    return [(a, s) for a, (_, s) in zip(arrays, parts)]


def scatter_steps(grid, mine, other, cut):
    got = lax.ppermute(other, AXES, grid.core_swap())
    back = yield [got]
    (got,), held = (back[0], tuple(back[1:])) if isinstance(back, tuple) else (back, ())
    shape = (grid.ny, grid.nx, grid.nz) + mine.shape[1:]
    mine, got = mine.reshape(shape), got.reshape(shape)
    cut = min(cut, grid.nz)
    lots = [(lo, hi, axes) for lo, hi, axes in ((0, cut, "yx"), (cut, grid.nz, "xy")) if hi > lo]
    current = [[mine[:, :, lo:hi], got[:, :, lo:hi]] for lo, hi, _ in lots]
    for step in range(2):
        waiting = []
        for n, (_, _, axes) in enumerate(lots):
            axis = axes[step]
            dim = 1 if axis == "x" and step == 0 else 0
            pieces = [
                [lax.index_in_dim(c, k, dim, keepdims=False) for c in current[n]] for k in range(grid.sizes[axis])
            ]
            waiting.append([add_all(pieces[k]).astype(BF16) for k in range(1, grid.sizes[axis])])
            current[n] = pieces[0]
        if held:
            waiting, held = together(waiting, held)
        for n, (_, _, axes) in enumerate(lots):
            waiting[n] = [
                lax.ppermute(total, AXES, grid.shift(axes[step], k + 1)) for k, total in enumerate(waiting[n])
            ]
        flat = [a for received in waiting for a in received]
        back = yield (flat, *held) if held else flat
        flat, held = (back[0], tuple(back[1:])) if isinstance(back, tuple) else (list(back), ())
        for n, received in enumerate(waiting):
            current[n] = current[n] + flat[: len(received)]
            flat = flat[len(received) :]
    final = []
    for k in range(grid.nz):
        n = 0 if k < lots[0][1] else 1
        final.append(add_all([c[k - lots[n][0]] for c in current[n]]))
    leaving = [total.astype(BF16) for total in final[1:]]
    if held:
        leaving, held = together(leaving, held)
    flat = [lax.ppermute(total, AXES, grid.shift("z", k + 1)) for k, total in enumerate(leaving)]
    back = yield (flat, *held) if held else flat
    final[1:] = back[0] if isinstance(back, tuple) else back
    yield add_all(final)


def add_all(items):
    total = items[0].astype(F32)
    for item in items[1:]:
        total = total + item.astype(F32)
    return total


def nn(a, b):
    return lax.dot_general(a, b, (((1,), (0,)), ((), ())), preferred_element_type=F32)


def nt(a, b):
    return lax.dot_general(a, b, (((1,), (1,)), ((), ())), preferred_element_type=F32)


def tn(a, b):
    return lax.dot_general(a, b, (((0,), (0,)), ((), ())), preferred_element_type=F32)


def normalized(values):
    centered = values - jnp.mean(values, axis=-1, keepdims=True)
    spread = jnp.mean(centered * centered, axis=-1, keepdims=True)
    root = lax.rsqrt(spread + EPSILON)
    return centered * root, root


def norm_back(z, root, scaled):
    return root * (
        scaled
        - jnp.mean(scaled, axis=-1, keepdims=True)
        - z * jnp.mean(scaled * z, axis=-1, keepdims=True)
    )


class Pieces:
    def __init__(self, chips, mine, theirs, fields):
        self.chips = chips
        self.arrays = [a for a, _ in mine] + [a for a, _ in theirs]
        self.spots = [s for _, s in mine] + [s for _, s in theirs]
        self.count_mine = len(mine)
        self.rows = self.arrays[0].shape[1]
        self.fields = fields

    def copies(self, wanted):
        total = 0
        for n, spots in enumerate(self.spots):
            for name, column, width, gain in self.fields:
                if name in wanted and not (gain and n >= self.count_mine):
                    total += len(spots)
        return total

    def start(self, refs, tab, wanted, sems, first):
        core = tab[2 * self.chips]
        started = {name: [] for name in wanted}
        n_sem = first
        for n, spots in enumerate(self.spots):
            for name, column, width, gain in self.fields:
                if name not in wanted or (gain and n >= self.count_mine):
                    continue
                for k, r in enumerate(spots):
                    row = pl.multiple_of(tab[r] * self.rows, 16)
                    if gain:
                        place = wanted[name].at[pl.ds(row, self.rows), :]
                    else:
                        side = core if n < self.count_mine else 1 - core
                        col = pl.multiple_of(side * width, 128)
                        place = wanted[name].at[pl.ds(row, self.rows), pl.ds(col, width)]
                    copy = pltpu.make_async_copy(
                        refs[n].at[k, :, column : column + width], place, sems.at[n_sem]
                    )
                    copy.start()
                    started[name].append(copy)
                    n_sem += 1
        return started


def hand_on(scratch, target, sem, step, steps):
    copy = pltpu.make_async_copy(scratch, target, sem.at[0])

    @pl.when(step == 0)
    def _():
        copy.start()

    @pl.when(step == steps - 1)
    def _():
        copy.wait()


def wait_all(copies):
    for copy in copies:
        copy.wait()


def emit(value, first_chip, rows, ref, columns, tab, chips):
    height = value.shape[0]
    low = value.astype(BF16)
    if rows >= height:
        ref[0, pl.ds(first_chip, height), columns] = low
    else:
        for a in range(height // rows):
            ref[tab[chips + first_chip + a], :, columns] = low[a * rows : (a + 1) * rows]


def by_side(core, mine, other, run):
    @pl.when(core == 0)
    def _():
        run(mine, other)

    @pl.when(core != 0)
    def _():
        run(other, mine)


def place_of(row, rows, chips):
    return row if chips == 1 else row // rows


def input_kernel(pieces, n_refs, chips, tab, own, got, *refs):
    sources, refs = refs[:n_refs], refs[n_refs:]
    packed, normed, gains, w_whole, w_qkv, gain_cols, sems, w_sem = refs
    i = pl.program_id(0)
    steps = pl.num_programs(0)
    width = own.shape[1]

    @pl.when(i == 0)
    def _():
        started = pieces.start(sources, tab, {"gain": gain_cols, "qkv": w_qkv}, sems, 0)
        wait_all(started["gain"])
        pick = (
            lax.broadcasted_iota(jnp.int32, (8, 128), 0) == lax.broadcasted_iota(jnp.int32, (8, 128), 1)
        ).astype(BF16)
        gains[...] = nt(pick, gain_cols[...])
        wait_all(started["qkv"])

    x = jnp.where(i < steps // 2, own[...], got[...]).astype(F32)
    z, _ = normalized(x)
    low = (z * gains[0:1, :]).astype(BF16)
    normed[...] = low
    for c in range(3):
        cols = slice(c * width, (c + 1) * width)
        packed[:, cols] = nn(low, w_qkv[:, cols]).astype(BF16)
    hand_on(w_qkv, w_whole, w_sem, i, steps)


def pair_of(ref, n):
    return ref[:, 0, :, 128 * n : 128 * (n + 1)].reshape(512, 128)


def fill_bias(bias, short):
    row_clip = (lax.broadcasted_iota(jnp.int32, (512, 512), 0) // 128) % 2
    col_clip = (lax.broadcasted_iota(jnp.int32, (512, 512), 1) // 128) % 2
    apart = jnp.logical_and(row_clip != col_clip, short != 0)
    bias[...] = jnp.where(apart, -1e30, 0.0)


def by_class(short, run):
    @pl.when(short == 0)
    def _():
        run(False)

    @pl.when(short != 0)
    def _():
        run(True)


def attend_kernel(chips, tab, q_ref, k_ref, v_ref, *refs):
    attended, log_totals, bias = refs[-3:]
    short = tab[2 * chips + 1]

    @pl.when(jnp.logical_and(pl.program_id(0) == 0, pl.program_id(1) == 0))
    def _():
        fill_bias(bias, short)

    def run(masked):
        lane = lax.broadcasted_iota(jnp.int32, (512, 128), 1)
        q, k, v = [[pair_of(ref, n) for n in range(2)] for ref in (q_ref, k_ref, v_ref)]

        def head_of(value, h):
            return jnp.where((lane // 64) == h, value, jnp.zeros_like(value))

        def scores(i):
            s = nt(head_of(q[i // 2], i % 2), k[i // 2])
            return s + bias[...] if masked else s

        logs = jnp.zeros((512, 128), F32)
        mixed = [0.0, 0.0]
        ahead = scores(0)
        for i in range(4):
            s, ahead = ahead, scores(i + 1) if i < 3 else None
            top_score = jnp.max(s, axis=1, keepdims=True) * (SCORE_SCALE * LOG2E)
            p = jnp.exp2(s * (SCORE_SCALE * LOG2E) - top_score)
            total = jnp.sum(p, axis=1, keepdims=True)
            logs = jnp.where(lane == i, top_score + jnp.log2(total), logs)
            mixed[i // 2] = mixed[i // 2] + nn(p.astype(BF16), head_of(v[i // 2], i % 2)) * (1.0 / total)
        for n in range(2):
            attended[:, 0, :, 128 * n : 128 * (n + 1)] = mixed[n].astype(BF16).reshape(2, 256, 128)
        turned = logs.T
        for i in range(4):
            log_totals[i] = turned[i : i + 1, :]

    by_class(short, run)


def gelu_both(u):
    below = 0.5 + 0.5 * lax.erf(u * (0.5**0.5))
    bell = jnp.exp2(u * u * (-0.5 * LOG2E)) * 0.3989422804014327
    return u * below, below + u * bell


def middle_kernel(pieces, n_refs, chips, tab, attended, own, got, gains, *refs):
    sources, refs = refs[:n_refs], refs[n_refs:]
    hidden, normed, w_whole, w_out, sems, w_sem = refs
    i = pl.program_id(0)

    @pl.when(i == 0)
    def _():
        wait_all(pieces.start(sources, tab, {"out": w_out}, sems, 0)["out"])

    x = jnp.where(i < pl.num_programs(0) // 2, own[...], got[...]).astype(F32)
    h = x + nn(attended[...], w_out[...])
    hidden[...] = h
    z, _ = normalized(h)
    normed[...] = (z * gains[1:2, :]).astype(BF16)
    hand_on(w_out, w_whole, w_sem, i, pl.num_programs(0))


def up_tiles(normed, weight, active, slope):
    for i in range(normed.shape[0] // 256):
        rows = slice(256 * i, 256 * (i + 1))
        a, s = gelu_both(nn(normed[rows, :], weight))
        active[rows, :] = a.astype(BF16)
        slope[rows, :] = s.astype(BF16)


def up_kernel(pieces, n_refs, chips, tab, normed, *refs):
    sources, refs = refs[:n_refs], refs[n_refs:]
    active, slope, w_whole, w_up, sems, w_sem = refs
    width = normed.shape[1]
    j = pl.program_id(0)

    @pl.when(j == 0)
    def _():
        wait_all(pieces.start(sources, tab, {"up": w_up}, sems, 0)["up"])

    up_tiles(normed, w_up[:, pl.ds(pl.multiple_of(j * width, 128), width)], active, slope)
    hand_on(w_up, w_whole, w_sem, j, pl.num_programs(0))


def up_rest_kernel(tab, normed, w_up, _active, _slope, active, slope):
    up_tiles(normed, w_up[...], active, slope)


def down_grad_kernel(chips, rows_down, tab, active, cot_own, cot_got, down_mine, down_other):
    half, width = cot_own.shape
    j = pl.program_id(0)

    def run(left, right):
        for m in range(2):
            piece = slice(384 * m, 384 * (m + 1))
            grad = tn(active[:half, piece], cot_own[...]) + tn(active[half:, piece], cot_got[...])
            start = place_of(width * j + 384 * m, rows_down, chips)
            emit(grad[:, : width // 2], start, rows_down, left, slice(None), tab, chips)
            emit(grad[:, width // 2 :], start, rows_down, right, slice(None), tab, chips)

    by_side(tab[2 * chips], down_mine, down_other, run)


def down_back_kernel(chips, rows_up, tab, cot_own, cot_got, normed, slope, w_down, grad_up, up_mine, up_other):
    half, width = cot_own.shape
    j = pl.program_id(0)
    steps = pl.num_programs(0)

    offset = pl.multiple_of(lax.rem(j, steps // 2) * width, 128)

    def run(target):
        for part, cot in enumerate((cot_own, cot_got)):
            for i in range(half // 256):
                inner = slice(256 * i, 256 * (i + 1))
                rows = slice(part * half + 256 * i, part * half + 256 * (i + 1))
                grad_up[rows, :] = (nt(cot[inner, :], w_down[...]) * slope[rows, :].astype(F32)).astype(BF16)
        for m in range(2):
            grad = tn(normed[:, 384 * m : 384 * (m + 1)], grad_up[...])
            emit(grad, place_of(384 * m, rows_up, chips), rows_up, target, pl.ds(offset, width), tab, chips)

    rel = (j // (steps // 2)) ^ tab[2 * chips]

    @pl.when(rel == 0)
    def _():
        run(up_mine)

    @pl.when(rel != 0)
    def _():
        run(up_other)


def up_back_kernel(
    chips, rows_up, tab, grad_up, attended, gains, cot_own, cot_got, hidden, _mine, _other, w_up, w_out, *refs
):
    grad_hidden, grad_att, out_mine, out_other, total_out = refs
    i = pl.program_id(0)
    steps = pl.num_programs(0)
    width = hidden.shape[1]

    @pl.when(i == 0)
    def _():
        total_out[...] = jnp.zeros_like(total_out)

    cot = jnp.where(i < steps // 2, cot_own[...], cot_got[...]).astype(F32)
    e = nt(grad_up[...], w_up[...])
    z, root = normalized(hidden[...])
    total = cot + norm_back(z, root, e * gains[1:2, :])
    grad_hidden[...] = total
    low = total.astype(BF16)
    grad_att[...] = nt(low, w_out[...]).astype(BF16)
    total_out[...] += tn(attended[...], low)

    @pl.when(i == steps - 1)
    def _():
        def run(left, right):
            for m in range(2):
                start = place_of(384 * m, rows_up, chips)
                for side, ref in enumerate((left, right)):
                    value = total_out[384 * m : 384 * (m + 1), side * (width // 2) : (side + 1) * (width // 2)]
                    emit(value, start, rows_up, ref, slice(None), tab, chips)

        by_side(tab[2 * chips], out_mine, out_other, run)


def output_kernel(pieces, n_refs, chips, tab, active, hidden, *refs):
    sources, refs = refs[:n_refs], refs[n_refs:]
    out, w_whole, w_down, sems, w_sem = refs

    @pl.when(pl.program_id(0) == 0)
    def _():
        wait_all(pieces.start(sources, tab, {"down": w_down}, sems, 0)["down"])

    out[...] = (hidden[...] + nn(active[...], w_down[...])).astype(BF16)
    hand_on(w_down, w_whole, w_sem, pl.program_id(0), pl.num_programs(0))


def attend_back_kernel(chips, tab, q_ref, k_ref, v_ref, o_ref, d_ref, log_totals, grad_q_ref, grad_k_ref, grad_v_ref, bias):
    short = tab[2 * chips + 1]

    @pl.when(jnp.logical_and(pl.program_id(0) == 0, pl.program_id(1) == 0))
    def _():
        fill_bias(bias, short)

    def put(ref, n, value):
        ref[:, 0, :, 128 * n : 128 * (n + 1)] = value.astype(BF16).reshape(2, 256, 128)

    def run(masked):
        lane = lax.broadcasted_iota(jnp.int32, (512, 128), 1)
        for n in range(2):
            q, k, v, o, d = [pair_of(r, n) for r in (q_ref, k_ref, v_ref, o_ref, d_ref)]
            k_t = k.T
            dots = (o.astype(F32) * d.astype(F32)).T
            grad_q, grad_k, grad_v = [], [], []
            for h in range(2):
                here = (lane // 64) == h
                zero = jnp.zeros_like(k)
                s = nt(jnp.where(here, k, zero), q)
                if masked:
                    s = s + bias[...]
                p = jnp.exp2(s * (SCORE_SCALE * LOG2E) - log_totals[2 * n + h])
                grad_v.append(nn(p.astype(BF16), jnp.where(here, d, zero)))
                grad_p = nt(jnp.where(here, v, zero), d)
                delta = jnp.sum(dots[64 * h : 64 * h + 64, :], axis=0, keepdims=True)
                grad_s = (p * (grad_p - delta)).astype(BF16)
                grad_k.append(nn(grad_s, jnp.where(here, q, zero)))
                grad_q.append(nn(k_t[64 * h : 64 * h + 64, :], grad_s))
            put(grad_q_ref, n, jnp.concatenate(grad_q, axis=0).T * SCORE_SCALE)
            put(grad_k_ref, n, (grad_k[0] + grad_k[1]) * SCORE_SCALE)
            put(grad_v_ref, n, grad_v[0] + grad_v[1])

    by_class(short, run)


def qkv_grad_kernel(chips, rows_qkv, cuts, tab, normed, *refs):
    grads, mine, other = refs[:-2], refs[-2], refs[-1]
    width = normed.shape[1]
    wide = 3 * width // 2

    def run(*sides):
        for n, ref in enumerate(grads):
            base = (n % 3) * width + cuts[n // 3]
            size = ref.shape[1]
            for m in range(2):
                grad = tn(normed[:, 384 * m : 384 * (m + 1)], ref[...])
                start = place_of(384 * m, rows_qkv, chips)
                at = base
                while at < base + size:
                    side = at // wide
                    end = min(base + size, (side + 1) * wide)
                    columns = slice(at - side * wide, end - side * wide)
                    emit(grad[:, at - base : end - base], start, rows_qkv, sides[side], columns, tab, chips)
                    at = end

    by_side(tab[2 * chips], mine, other, run)


def first_kernel(cuts, tab, own, got, gains, grad_hidden, w_qkv, *refs):
    grads, (out_own, out_got) = refs[:-2], refs[-2:]
    width = own.shape[1]
    here = pl.program_id(0) < pl.num_programs(0) // 2
    e = 0.0
    for n, grad in enumerate(grads):
        base, lot = (n % 3) * width, n // 3
        e = e + nt(grad[...], w_qkv[:, base + cuts[lot] : base + cuts[lot + 1]])
    z, root = normalized(jnp.where(here, own[...], got[...]).astype(F32))
    value = (grad_hidden[...] + norm_back(z, root, e * gains[0:1, :])).astype(BF16)

    @pl.when(here)
    def _():
        out_own[...] = value

    @pl.when(jnp.logical_not(here))
    def _():
        out_got[...] = value


def whole(shape):
    return pl.BlockSpec(shape, lambda *_: (0,) * len(shape))


anywhere = pl.BlockSpec(memory_space=pl.ANY)


def call(kernel, tab, inputs, piece_arrays, outs, scratch, grid=(1,), cost=0, aliases=None, stay=()):
    specs = [spec or whole(a.shape) for a, spec in inputs]
    specs = specs + [pl.BlockSpec(memory_space=pltpu.HBM) for _ in piece_arrays]
    blocks = [(a, spec) for a, spec in inputs] + [(o, spec) for o, spec in outs]
    need = SPARE_BYTES
    for array, spec in blocks:
        if spec is anywhere:
            continue
        size = jnp.dtype(array.dtype).itemsize
        for extent in spec.block_shape if spec else array.shape:
            size *= extent
        need += 2 * size
    for buffer in scratch:
        if hasattr(buffer, "shape") and buffer.dtype in (BF16, F32):
            size = buffer.dtype.itemsize if hasattr(buffer.dtype, "itemsize") else jnp.dtype(buffer.dtype).itemsize
            for extent in buffer.shape:
                size *= extent
            need += size
    moved = sum(a.size * a.dtype.itemsize for a, _ in inputs) + sum(a.size * a.dtype.itemsize for a in piece_arrays)
    moved += sum(math.prod(o.shape) * jnp.dtype(o.dtype).itemsize for o, _ in outs)
    inputs = [
        (pltpu.with_memory_space_constraint(a, pltpu.HBM) if n in stay or a.size > 2**21 and spec is not None else a, spec)
        for n, (a, spec) in enumerate(inputs)
    ]
    return pl.pallas_call(
        kernel,
        out_shape=[o for o, _ in outs],
        input_output_aliases=aliases or {},
        grid_spec=pltpu.PrefetchScalarGridSpec(
            num_scalar_prefetch=1,
            grid=grid,
            in_specs=specs,
            out_specs=[spec or whole(o.shape) for o, spec in outs],
            scratch_shapes=scratch,
        ),
        compiler_params=pltpu.CompilerParams(
            dimension_semantics=("arbitrary",) * len(grid), vmem_limit_bytes=min(need, VMEM_BYTES)
        ),
        cost_estimate=pl.CostEstimate(flops=cost, bytes_accessed=moved, transcendentals=0),
    )(tab, *[a for a, _ in inputs], *piece_arrays)


def body(grid, tokens, clip_class, w_qkv, w_out, w_up, w_down, norm_gains, cotangent):
    rows, width = tokens.shape[1:]
    half = rows // 2
    ff = w_up.shape[1]
    here = grid.here()
    mx = here["x"]
    fast = (2 * w_qkv.shape[0]) % 16 == 0 and (2 * w_down.shape[0]) % 16 == 0
    chips = grid.chips if fast else 1

    def split(array):
        own = lax.dynamic_slice(array[0], (mx * half, 0), (half, width))
        away = lax.dynamic_slice(array[0], ((1 - mx) * half, 0), (half, width))
        return own, away

    swap_x = [(0, 1), (1, 0)]
    tok_own, tok_away = split(tokens)
    cot_own, cot_away = split(cotangent)

    if fast:
        spots = [(x, y, z) for x in range(grid.nx) for y in range(grid.ny) for z in range(grid.nz)]
        chip_at = [
            (((mx - x) % grid.nx) * grid.nz + ((here["z"] - z) % grid.nz)) * grid.ny + ((here["y"] - y) % grid.ny)
            for x, y, z in spots
        ]
        place_at = []
        for a in range(chips):
            x, z, y = a // (grid.nz * grid.ny), (a // grid.ny) % grid.nz, a % grid.ny
            rx, rz, ry = (x - mx) % grid.nx, (z - here["z"]) % grid.nz, (y - here["y"]) % grid.ny
            place_at.append((ry * grid.nx + rx) * grid.nz + rz)
        core = here["c"]
    else:
        chip_at, place_at, core = [jnp.int32(0)], [jnp.int32(0)], jnp.int32(0)
    tab = jnp.stack([jnp.asarray(v, jnp.int32) for v in chip_at + place_at + [core, clip_class[0]]])

    def side_of(weight, side):
        wide = weight.shape[1] // 2
        return lax.dynamic_slice(weight, (0, side * wide), (weight.shape[0], wide))

    gain_block = jnp.pad(norm_gains, ((0, 0), (0, 126)))
    fields_a = [("qkv", 0, 3 * width // 2, False), ("gain", 3 * width // 2, 128, True)]
    fields_b = [("up", 0, ff // 2, False), ("out", ff // 2, width // 2, False)]
    fields_c = [("down", 0, width // 2, False)]
    swap_core = functools.partial(lax.ppermute, axis_name=AXES, perm=grid.core_swap())
    if fast:
        def sides(side, group):
            if group == 0:
                return jnp.concatenate([side_of(w_qkv, side), gain_block], axis=1)
            if group == 1:
                return jnp.concatenate([side_of(w_up, side), side_of(w_out, side)], axis=1)
            return side_of(w_down, side)

        def with_partner(group):
            keep, other = sides(core, group), swap_core(sides(1 - core, group))
            return jnp.concatenate(
                [jnp.where(core == 0, keep, other), jnp.where(core == 0, other, keep)], axis=0
            )

        tok_away, w_qkv = together(tok_away, w_qkv)
        most = 3 * half // 4
        tok_first = lax.ppermute(tok_away[:most], "seq", swap_x)
        piece_a = with_partner(0)
        piece_a, w_up, w_out, w_down = together(piece_a, w_up, w_out, w_down)
        piece_b, piece_c = with_partner(1), with_partner(2)

        def near_of(lots):
            return [exchange(grid, [lot], axis) for lot, axis in zip(lots, "xy")]

        def widened(lots, near):
            return [joined_parts([lot] + moved) for lot, moved in zip(lots, near)]

        def far_of(wide):
            far = []
            for lot, axis in zip(wide, "yx"):
                far += exchange(grid, [lot], axis)
            return far

        def flat(groups):
            return [part for group in groups for part in group]

        def swapped(parts):
            return [(swap_core(a), s) for a, s in parts]

        def pieces_from(mine, theirs, fields):
            named = lambda parts: [(a, [rel_of(grid, s) for s in spots]) for a, spots in parts]
            return Pieces(chips, named(mine), named(theirs), fields)

        def finish(mine, fields):
            mine = [(a, [rel_of(grid, s) for s in spots]) for a, spots in mine]
            theirs = [(swap_core(a), s) for a, s in mine]
            return Pieces(chips, mine, theirs, fields)

        z_a = gather_along_z(grid, piece_a)
        arrays, tok_first, tok_next, piece_b = together(arrays_of(z_a), tok_first, tok_away[most:], piece_b)
        tok_second = lax.ppermute(tok_next, "seq", swap_x)
        z_a = lots_of(with_arrays(z_a, arrays), 2)
        near_a = near_of(z_a)
        z_b = gather_along_z(grid, piece_b)
        arrays = lax.optimization_barrier(arrays_of(flat(near_a)))
        wide_a = widened(z_a, [[part] for part in with_arrays(flat(near_a), arrays)])
        far_a = far_of(wide_a)
        all_a = wide_a + far_a
        arrays_a, z_own, piece_c = together(arrays_of(all_a), z_b[0][0], piece_c)
        tok_got = jnp.concatenate([tok_first, tok_second], axis=0)
        z_b = with_arrays(z_b, [z_own] + arrays_of(z_b[1:]))
        group_a = finish(with_arrays(all_a, arrays_a), fields_a)
        z_b = lots_of(with_arrays(z_b, lax.optimization_barrier(arrays_of(z_b))), 2)
        near_b = near_of(z_b)
        z_c = gather_along_z(grid, piece_c)
    else:
        full = [lax.all_gather(w, AXES, axis=0, tiled=True) for w in (w_qkv, w_out, w_up, w_down, gain_block)]

        def natural(parts, fields):
            sides = []
            for side in range(2):
                cut = [p if p.shape[1] == 128 else p[:, side * (p.shape[1] // 2) : (side + 1) * (p.shape[1] // 2)] for p in parts]
                sides.append([(jnp.concatenate(cut, axis=1)[None], [0])])
            return Pieces(1, sides[0], sides[1], fields)

        group_a = natural([full[0], full[4]], fields_a)
        group_b = natural([full[2], full[1]], fields_b)
        group_c = natural([full[3]], fields_c)
        tok_got = lax.ppermute(tok_away, "seq", swap_x)
        cot_got = lax.ppermute(cot_away, "seq", swap_x)

    sds = jax.ShapeDtypeStruct
    heads = width // HEAD_DIM
    rows_a, rows_c = (2 * w_qkv.shape[0], 2 * w_down.shape[0]) if fast else (width, ff)
    dma = pltpu.SemaphoreType.DMA
    vmem = pltpu.VMEM
    tiles = rows // 256
    tile = lambda columns: pl.BlockSpec((256, columns), lambda i, t: (i, 0))
    own_tile = pl.BlockSpec((256, width), lambda i, t: (jnp.minimum(i, tiles // 2 - 1), 0))
    got_tile = pl.BlockSpec((256, width), lambda i, t: (jnp.maximum(i - tiles // 2, 0), 0))
    chunk = pl.BlockSpec((rows, width), lambda j, t: (0, j))
    low = lambda *shape: sds(shape, BF16)

    packed, normed_first, gains, whole_qkv = call(
        functools.partial(input_kernel, group_a, len(group_a.arrays), chips),
        tab,
        [(tok_own, own_tile), (tok_got, got_tile)],
        group_a.arrays,
        [(pltpu.HBM((rows, 3 * width), BF16), tile(3 * width)), (low(rows, width), tile(width)), (sds((8, width), F32), None),
         (pltpu.HBM((width, 3 * width), BF16), anywhere)],
        [vmem((width, 3 * width), BF16), vmem((width, 128), BF16), dma((group_a.copies(("qkv", "gain")),)), dma((1,))],
        grid=(tiles,),
        cost=2 * rows * width * 3 * width,
    )

    if fast:
        packed, arrays_b, arrays_c = together(packed, arrays_of(flat(near_b)), arrays_of(z_c))
        z_c = with_arrays(z_c, arrays_c)
        wide_b = widened(z_b, [[part] for part in with_arrays(flat(near_b), arrays_b)])
        far_b = far_of(wide_b)
        their_wide_b = swapped(wide_b)

    clip_blocks = half // 256
    by_clip = lambda a: a.reshape(2, clip_blocks, 256, a.shape[1])
    clip_shape = low(2, clip_blocks, 256, width)
    step = width // 256
    totals_shape = sds((clip_blocks * heads, 1, 512), F32)

    def attend(first, last, packed, earlier):
        at = lambda base: pl.BlockSpec((2, 1, 256, 256), lambda b, g, t: (0, first + b, 0, base + g))
        totals = pl.BlockSpec((4, 1, 512), lambda b, g, t: ((first + b) * (heads // 4) + g, 0, 0))
        return call(
            functools.partial(attend_kernel, chips),
            tab,
            [(by_clip(packed), at(0)), (by_clip(packed), at(step)), (by_clip(packed), at(2 * step))]
            + [(a, anywhere) for a in earlier],
            [],
            [(clip_shape, at(0)), (totals_shape, totals)],
            [vmem((512, 512), F32)],
            grid=(last - first, heads // 4),
            cost=8 * rows * 512 * width * (last - first) // clip_blocks,
            aliases={4: 0, 5: 1} if earlier else None,
        )

    attended, log_totals = attend(0, clip_blocks, packed, [])
    attended = attended.reshape(rows, width)

    if fast:
        attended, arrays_b, arrays_w, arrays_c = together(
            attended, arrays_of(far_b), arrays_of(their_wide_b), arrays_of(z_c)
        )
        far_b, their_wide_b = with_arrays(far_b, arrays_b), with_arrays(their_wide_b, arrays_w)
        group_b = pieces_from(wide_b + far_b, their_wide_b + swapped(far_b), fields_b)
        z_c = [joined_parts(with_arrays(z_c, arrays_c))]
        near_c = exchange(grid, z_c, "x")
        straight_c = exchange(grid, z_c, "y")

    hidden, normed_second, whole_out = call(
        functools.partial(middle_kernel, group_b, len(group_b.arrays), chips),
        tab,
        [(attended, tile(width)), (tok_own, own_tile), (tok_got, got_tile), (gains, None)],
        group_b.arrays,
        [
            (sds((rows, width), F32), tile(width)), (low(rows, width), tile(width)),
            (pltpu.HBM((width, width), BF16), anywhere),
        ],
        [vmem((width, width), BF16), dma((group_b.copies(("out",)),)), dma((1,))],
        grid=(tiles,),
        cost=2 * rows * width * width,
    )

    steps = ff // width

    split_up = steps // 2
    wide_hbm = pltpu.HBM((rows, ff), BF16)
    active, slope, whole_up = call(
        functools.partial(up_kernel, group_b, len(group_b.arrays), chips),
        tab,
        [(normed_second, None)],
        group_b.arrays,
        [(wide_hbm, chunk), (wide_hbm, chunk), (pltpu.HBM((width, ff), BF16), anywhere)],
        [vmem((width, ff), BF16), dma((group_b.copies(("up",)),)), dma((1,))],
        grid=(split_up,),
        cost=2 * rows * width * width * split_up,
    )
    if fast:
        active, slope, normed_second, arrays_c, arrays_s, cot_away = together(
            active, slope, normed_second, arrays_of(near_c), arrays_of(straight_c), cot_away
        )
        near_c, straight_c = with_arrays(near_c, arrays_c), with_arrays(straight_c, arrays_s)
        far_c = exchange(grid, near_c, "y")
        cot_got = lax.ppermute(cot_away, "seq", swap_x)
    rest = pl.BlockSpec((rows, width), lambda j, t: (0, split_up + j))
    active, slope = call(
        up_rest_kernel,
        tab,
        [
            (normed_second, None), (whole_up, pl.BlockSpec((width, width), lambda j, t: (0, split_up + j))),
            (active, anywhere), (slope, anywhere),
        ],
        [],
        [(wide_hbm, rest), (wide_hbm, rest)],
        [],
        grid=(steps - split_up,),
        cost=2 * rows * width * width * (steps - split_up),
        aliases={3: 0, 4: 1},
    )
    if fast:
        all_c = z_c + near_c + straight_c + far_c
        active, slope, arrays_c, cot_got = together(active, slope, arrays_of(all_c), cot_got)
        all_c = with_arrays(all_c, arrays_c)
        theirs_c = swapped(all_c)
    down_out = low(chips, rows_c, width // 2)
    down_mine, down_other = call(
        functools.partial(down_grad_kernel, chips, rows_c),
        tab,
        [(active, chunk), (cot_own, None), (cot_got, None)],
        [],
        [(down_out, None), (down_out, None)],
        [],
        grid=(steps,),
        cost=2 * rows * width * ff,
    )

    def steps_of(mine, other, cut):
        if fast:
            return scatter_steps(grid, mine, other, cut)

        def plain():
            whole_sum = jnp.concatenate([mine[0], other[0]], axis=1)
            back = yield []
            for _ in range(3):
                back = yield back
            yield lax.psum_scatter(whole_sum, AXES, scatter_dimension=0, tiled=True).astype(F32)

        return plain()

    def owned(total):
        if not fast:
            return total[:, : total.shape[1] // 2], total[:, total.shape[1] // 2 :]
        height = total.shape[0] // 2
        keep = lax.dynamic_slice(total, (core * height, 0), (height, total.shape[1]))
        away = lax.dynamic_slice(total, ((1 - core) * height, 0), (height, total.shape[1]))
        got = swap_core(away.astype(BF16)).astype(F32)
        return jnp.where(core == 0, keep, got), jnp.where(core == 0, got, keep)

    if fast:
        down_mine, down_other, active, arrays_c = together(down_mine, down_other, active, arrays_of(theirs_c))
        group_c = pieces_from(all_c, with_arrays(theirs_c, arrays_c), fields_c)
    outputs, whole_down = call(
        functools.partial(output_kernel, group_c, len(group_c.arrays), chips),
        tab,
        [(active, tile(ff)), (hidden, tile(width))],
        group_c.arrays,
        [(low(rows, width), tile(width)), (pltpu.HBM((ff, width), BF16), anywhere)],
        [vmem((ff, width), BF16), dma((group_c.copies(("down",)),)), dma((1,))],
        grid=(tiles,),
        cost=2 * rows * width * ff,
    )
    down_sum = steps_of(down_mine, down_other, 2)
    arrived = next(down_sum)
    outputs, arrived, slope = together(outputs, arrived, slope)
    arrived = down_sum.send(arrived)
    def joined(own, back):
        first = mx == 0
        return jnp.concatenate([jnp.where(first, own, back), jnp.where(first, back, own)], axis=0)[None]

    up_part = pl.BlockSpec((chips, rows_a, ff // 2), lambda *_: (0, 0, 0))
    out_part = pl.BlockSpec((chips, rows_a, width // 2), lambda *_: (0, 0, ff // width))
    up_out = low(chips, rows_a, ff // 2 + width // 2)
    grad_up, up_mine, up_other = call(
        functools.partial(down_back_kernel, chips, rows_a),
        tab,
        [
            (cot_own, None), (cot_got, None), (normed_second, None), (slope, chunk),
            (whole_down, pl.BlockSpec((width, width), lambda j, t: (j, 0))),
        ],
        [],
        [(pltpu.HBM((rows, ff), BF16), chunk), (up_out, up_part), (up_out, up_part)],
        [],
        grid=(steps,),
        cost=4 * rows * width * ff,
    )
    grad_up, up_mine, up_other, arrived = together(grad_up, up_mine, up_other, arrived)
    arrived = down_sum.send(arrived)
    quarter = half // 2
    out_first = lax.ppermute(outputs[half : half + quarter], "seq", swap_x)
    grad_hidden, grad_att, up_mine, up_other = call(
        functools.partial(up_back_kernel, chips, rows_a),
        tab,
        [
            (grad_up, tile(ff)), (attended, tile(width)), (gains, None), (cot_own, own_tile), (cot_got, got_tile),
            (hidden, tile(width)), (up_mine, anywhere), (up_other, anywhere),
            (whole_up, None), (whole_out, None),
        ],
        [],
        [(pltpu.HBM((rows, width), F32), tile(width)), (low(rows, width), tile(width)), (up_out, out_part), (up_out, out_part)],
        [vmem((width, width), F32)],
        grid=(tiles,),
        cost=2 * rows * width * ff + 4 * rows * width * width,
        aliases={7: 2, 8: 3},
    )
    grad_att, grad_hidden, up_mine, up_other, arrived, out_first, out_next = together(
        grad_att, grad_hidden, up_mine, up_other, arrived, out_first, outputs[half + quarter :]
    )
    out_second = lax.ppermute(out_next, "seq", swap_x)
    arrived = down_sum.send(arrived)
    up_sum = steps_of(up_mine, up_other, 2)
    arrived_up = next(up_sum)

    groups = heads // 4
    group_cut = max(1, groups // 3)
    cuts = [0, 256 * group_cut, width]

    def attend_back(first, last, grad_att):
        at = lambda base: pl.BlockSpec((2, 1, 256, 256), lambda b, g, t: (0, b, 0, base + first + g))
        to = pl.BlockSpec((2, 1, 256, 256), lambda b, g, t: (0, b, 0, g))
        totals = pl.BlockSpec((4, 1, 512), lambda b, g, t: (b * groups + first + g, 0, 0))
        shape = pltpu.HBM((2, clip_blocks, 256, 256 * (last - first)), BF16)
        grads = call(
            functools.partial(attend_back_kernel, chips),
            tab,
            [
                (by_clip(packed), at(0)), (by_clip(packed), at(step)), (by_clip(packed), at(2 * step)),
                (by_clip(attended), at(0)), (by_clip(grad_att), at(0)), (log_totals, totals),
            ],
            [],
            [(shape, to)] * 3,
            [vmem((512, 512), F32)],
            grid=(clip_blocks, last - first),
            cost=30 * rows * 512 * 256 * (last - first),
        )
        return [g.reshape(rows, 256 * (last - first)) for g in grads]

    grads_a = attend_back(0, group_cut, grad_att)
    grads_a, grad_att, arrived_up, out_second = together(grads_a, grad_att, arrived_up, out_second)
    arrived_up = up_sum.send(arrived_up)
    grads_b = attend_back(group_cut, groups, grad_att)
    grads_b, arrived_up, arrived = together(grads_b, arrived_up, arrived)
    arrived_down = arrived
    arrived_up, grads_b, normed_first = up_sum.send((arrived_up, grads_b, normed_first))
    qkv_out = low(chips, rows_a, 3 * width // 2)
    qkv_mine, qkv_other = call(
        functools.partial(qkv_grad_kernel, chips, rows_a, cuts),
        tab,
        [(normed_first, None)] + [(g, None) for g in grads_a + grads_b],
        [],
        [(qkv_out, None), (qkv_out, None)],
        [],
        cost=2 * rows * width * 3 * width,
        stay=tuple(range(1, 7)),
    )
    qkv_mine, qkv_other, grads_a, grads_b, tok_own, arrived_up = together(
        qkv_mine, qkv_other, grads_a, grads_b, tok_own, arrived_up
    )
    arrived_up, tok_got = up_sum.send((arrived_up, tok_got))
    qkv_sum = steps_of(qkv_mine, qkv_other, 2)
    arrived = next(qkv_sum)
    arrived, tok_own = qkv_sum.send((arrived, tok_own))

    grad_own, grad_got = call(
        functools.partial(first_kernel, cuts),
        tab,
        [
            (tok_own, own_tile), (tok_got, got_tile), (gains, None), (grad_hidden, tile(width)), (whole_qkv, None),
        ]
        + [(g, tile(g.shape[1])) for g in grads_a + grads_b],
        [],
        [(low(half, width), own_tile), (low(half, width), got_tile)],
        [],
        grid=(tiles,),
        cost=2 * rows * width * 3 * width,
        stay=(3, 4) + tuple(range(5, 11)),
    )
    grad_got, grad_own, arrived, arrived_up, arrived_down = together(
        grad_got, grad_own, arrived, arrived_up, arrived_down
    )
    arrived = qkv_sum.send(arrived)
    arrived, grad_got = together(arrived, grad_got)
    grad_back = lax.ppermute(grad_got, "seq", swap_x)
    arrived_up, arrived, arrived_down, out_first, out_second = together(
        arrived_up, arrived, arrived_down, out_first, out_second
    )
    arrived = qkv_sum.send(arrived)
    left, right = owned(down_sum.send(arrived_down))
    owned_down = jnp.concatenate([left, right], axis=1)
    left, right = owned(up_sum.send(arrived_up))
    owned_up = jnp.concatenate([left[:, : ff // 2], right[:, : ff // 2]], axis=1)
    owned_out = jnp.concatenate([left[:, ff // 2 :], right[:, ff // 2 :]], axis=1)
    output_tokens = joined(outputs[:half], jnp.concatenate([out_first, out_second], axis=0))
    left, right = owned(qkv_sum.send(arrived))
    owned_qkv = jnp.concatenate([left, right], axis=1)
    grad_tokens = joined(grad_own, grad_back)

    scale = norm_gains.astype(F32)
    first_gain = jnp.sum(w_qkv.astype(F32) * owned_qkv, axis=1) / scale[:, 0]
    second_gain = jnp.sum(w_up.astype(F32) * owned_up, axis=1) / scale[:, 1]
    owned_gains = jnp.stack([first_gain, second_gain], axis=1)
    return (output_tokens, grad_tokens, owned_qkv, owned_out, owned_up, owned_down, owned_gains)


def solution(mesh):
    grid = Grid(mesh.shape["seq"], mesh.shape["clips"])
    shard = P(AXES, None)
    return jax.shard_map(
        functools.partial(body, grid),
        mesh=mesh,
        in_specs=(P("seq", "clips", None), P("clips"), shard, shard, shard, shard, shard, P("seq", "clips", None)),
        out_specs=(P("seq", "clips", None), P("seq", "clips", None), shard, shard, shard, shard, shard),
        check_vma=False,
    )
```

```python
import functools
import math

import jax
import jax.numpy as jnp
from jax import lax
from jax.experimental import pallas as pl
from jax.experimental.pallas import tpu as pltpu
from jax.sharding import PartitionSpec as P

HEAD_DIM = 64
CLIP = 512
EPSILON = 1e-05
AXES = ("seq", "clips")
LOG2E = 1.4426950408889634
SCORE_SCALE = HEAD_DIM ** (-0.5)
BF16 = jnp.bfloat16
F32 = jnp.float32
VMEM_BYTES = 58 * 1024 * 1024
SPARE_BYTES = 10 * 1024 * 1024


class Grid:
    def __init__(self, seq, clips):
        self.nx = seq
        self.clips = clips
        pairs = clips // 2
        bits = pairs.bit_length() - 1
        self.ny = 2 ** (bits // 3)
        self.nz = pairs // self.ny
        self.sizes = {"x": self.nx, "y": self.ny, "z": self.nz}
        self.chips = self.nx * self.ny * self.nz

    def index(self, x, z, y, c):
        return x * self.clips + (z * self.ny + y) * 2 + c

    def shift(self, axis, k):
        pairs = []
        for x in range(self.nx):
            for z in range(self.nz):
                for y in range(self.ny):
                    for c in range(2):
                        t = {"x": x, "y": y, "z": z}
                        t[axis] = (t[axis] + k) % self.sizes[axis]
                        pairs.append((self.index(x, z, y, c), self.index(t["x"], t["z"], t["y"], c)))
        return pairs

    def core_swap(self):
        return [(i, i ^ 1) for i in range(self.nx * self.clips)]

    def here(self):
        x = lax.axis_index("seq")
        rest = lax.axis_index("clips")
        return {"x": x, "z": rest // (2 * self.ny), "y": (rest // 2) % self.ny, "c": rest % 2}


def rel_of(grid, coords):
    return (coords["x"] * grid.ny + coords["y"]) * grid.nz + coords["z"]


def together(*values):
    return lax.optimization_barrier(values)


def exchange(grid, parts, axis):
    moved = []
    for k in range(1, grid.sizes[axis]):
        for array, spots in parts:
            moved.append((lax.ppermute(array, AXES, grid.shift(axis, k)), [{**s, axis: k} for s in spots]))
    return moved


def joined_parts(parts):
    if len(parts) == 1:
        return parts[0]
    return (jnp.concatenate([a for a, _ in parts], axis=0), [s for _, spots in parts for s in spots])


def gather_along_z(grid, piece):
    parts = [(piece[None], [{"x": 0, "y": 0, "z": 0}])]
    return parts + exchange(grid, parts, "z")


def lots_of(parts, cut):
    cut = min(cut, len(parts))
    return [joined_parts(p) for p in (parts[:cut], parts[cut:]) if p]


def arrays_of(parts):
    return [a for a, _ in parts]


def with_arrays(parts, arrays):
    return [(a, s) for a, (_, s) in zip(arrays, parts)]


def scatter_steps(grid, mine, other, cut):
    got = lax.ppermute(other, AXES, grid.core_swap())
    back = yield [got]
    (got,), held = (back[0], tuple(back[1:])) if isinstance(back, tuple) else (back, ())
    shape = (grid.ny, grid.nx, grid.nz) + mine.shape[1:]
    mine, got = mine.reshape(shape), got.reshape(shape)
    cut = min(cut, grid.nz)
    lots = [(lo, hi, axes) for lo, hi, axes in ((0, cut, "yx"), (cut, grid.nz, "xy")) if hi > lo]
    current = [[mine[:, :, lo:hi], got[:, :, lo:hi]] for lo, hi, _ in lots]
    for step in range(2):
        waiting = []
        for n, (_, _, axes) in enumerate(lots):
            axis = axes[step]
            dim = 1 if axis == "x" and step == 0 else 0
            pieces = [
                [lax.index_in_dim(c, k, dim, keepdims=False) for c in current[n]] for k in range(grid.sizes[axis])
            ]
            waiting.append([add_all(pieces[k]).astype(BF16) for k in range(1, grid.sizes[axis])])
            current[n] = pieces[0]
        if held:
            waiting, held = together(waiting, held)
        for n, (_, _, axes) in enumerate(lots):
            waiting[n] = [
                lax.ppermute(total, AXES, grid.shift(axes[step], k + 1)) for k, total in enumerate(waiting[n])
            ]
        flat = [a for received in waiting for a in received]
        back = yield (flat, *held) if held else flat
        flat, held = (back[0], tuple(back[1:])) if isinstance(back, tuple) else (list(back), ())
        for n, received in enumerate(waiting):
            current[n] = current[n] + flat[: len(received)]
            flat = flat[len(received) :]
    final = []
    for k in range(grid.nz):
        n = 0 if k < lots[0][1] else 1
        final.append(add_all([c[k - lots[n][0]] for c in current[n]]))
    leaving = [total.astype(BF16) for total in final[1:]]
    if held:
        leaving, held = together(leaving, held)
    flat = [lax.ppermute(total, AXES, grid.shift("z", k + 1)) for k, total in enumerate(leaving)]
    back = yield (flat, *held) if held else flat
    final[1:] = back[0] if isinstance(back, tuple) else back
    yield add_all(final)


def add_all(items):
    total = items[0].astype(F32)
    for item in items[1:]:
        total = total + item.astype(F32)
    return total


def nn(a, b):
    return lax.dot_general(a, b, (((1,), (0,)), ((), ())), preferred_element_type=F32)


def nt(a, b):
    return lax.dot_general(a, b, (((1,), (1,)), ((), ())), preferred_element_type=F32)


def tn(a, b):
    return lax.dot_general(a, b, (((0,), (0,)), ((), ())), preferred_element_type=F32)


def normalized(values):
    centered = values - jnp.mean(values, axis=-1, keepdims=True)
    spread = jnp.mean(centered * centered, axis=-1, keepdims=True)
    root = lax.rsqrt(spread + EPSILON)
    return centered * root, root


def norm_back(z, root, scaled):
    return root * (
        scaled
        - jnp.mean(scaled, axis=-1, keepdims=True)
        - z * jnp.mean(scaled * z, axis=-1, keepdims=True)
    )


class Pieces:
    def __init__(self, chips, mine, theirs, fields):
        self.chips = chips
        self.arrays = [a for a, _ in mine] + [a for a, _ in theirs]
        self.spots = [s for _, s in mine] + [s for _, s in theirs]
        self.count_mine = len(mine)
        self.rows = self.arrays[0].shape[1]
        self.fields = fields

    def copies(self, wanted):
        total = 0
        for n, spots in enumerate(self.spots):
            for name, column, width, gain in self.fields:
                if name in wanted and not (gain and n >= self.count_mine):
                    total += len(spots)
        return total

    def start(self, refs, tab, wanted, sems, first):
        core = tab[2 * self.chips]
        started = {name: [] for name in wanted}
        n_sem = first
        for n, spots in enumerate(self.spots):
            for name, column, width, gain in self.fields:
                if name not in wanted or (gain and n >= self.count_mine):
                    continue
                for k, r in enumerate(spots):
                    row = pl.multiple_of(tab[r] * self.rows, 16)
                    if gain:
                        place = wanted[name].at[pl.ds(row, self.rows), :]
                    else:
                        side = core if n < self.count_mine else 1 - core
                        col = pl.multiple_of(side * width, 128)
                        place = wanted[name].at[pl.ds(row, self.rows), pl.ds(col, width)]
                    copy = pltpu.make_async_copy(
                        refs[n].at[k, :, column : column + width], place, sems.at[n_sem]
                    )
                    copy.start()
                    started[name].append(copy)
                    n_sem += 1
        return started


def hand_on(scratch, target, sem, step, steps):
    copy = pltpu.make_async_copy(scratch, target, sem.at[0])

    @pl.when(step == 0)
    def _():
        copy.start()

    @pl.when(step == steps - 1)
    def _():
        copy.wait()


def wait_all(copies):
    for copy in copies:
        copy.wait()


def emit(value, first_chip, rows, ref, columns, tab, chips):
    height = value.shape[0]
    low = value.astype(BF16)
    if rows >= height:
        ref[0, pl.ds(first_chip, height), columns] = low
    else:
        for a in range(height // rows):
            ref[tab[chips + first_chip + a], :, columns] = low[a * rows : (a + 1) * rows]


def by_side(core, mine, other, run):
    @pl.when(core == 0)
    def _():
        run(mine, other)

    @pl.when(core != 0)
    def _():
        run(other, mine)


def place_of(row, rows, chips):
    return row if chips == 1 else row // rows


def input_kernel(pieces, n_refs, chips, tab, own, got, *refs):
    sources, refs = refs[:n_refs], refs[n_refs:]
    packed, normed, gains, w_whole, w_qkv, gain_cols, sems, w_sem = refs
    i = pl.program_id(0)
    steps = pl.num_programs(0)
    width = own.shape[1]

    @pl.when(i == 0)
    def _():
        started = pieces.start(sources, tab, {"gain": gain_cols, "qkv": w_qkv}, sems, 0)
        wait_all(started["gain"])
        pick = (
            lax.broadcasted_iota(jnp.int32, (8, 128), 0) == lax.broadcasted_iota(jnp.int32, (8, 128), 1)
        ).astype(BF16)
        gains[...] = nt(pick, gain_cols[...])
        wait_all(started["qkv"])

    x = jnp.where(i < steps // 2, own[...], got[...]).astype(F32)
    z, _ = normalized(x)
    low = (z * gains[0:1, :]).astype(BF16)
    normed[...] = low
    for c in range(3):
        cols = slice(c * width, (c + 1) * width)
        packed[:, cols] = nn(low, w_qkv[:, cols]).astype(BF16)
    hand_on(w_qkv, w_whole, w_sem, i, steps)


def pair_of(ref, n):
    return ref[:, 0, :, 128 * n : 128 * (n + 1)].reshape(512, 128)


def fill_bias(bias, short):
    row_clip = (lax.broadcasted_iota(jnp.int32, (512, 512), 0) // 128) % 2
    col_clip = (lax.broadcasted_iota(jnp.int32, (512, 512), 1) // 128) % 2
    apart = jnp.logical_and(row_clip != col_clip, short != 0)
    bias[...] = jnp.where(apart, -1e30, 0.0)


def by_class(short, run):
    @pl.when(short == 0)
    def _():
        run(False)

    @pl.when(short != 0)
    def _():
        run(True)


def attend_kernel(chips, tab, q_ref, k_ref, v_ref, *refs):
    attended, log_totals, bias = refs[-3:]
    short = tab[2 * chips + 1]

    @pl.when(jnp.logical_and(pl.program_id(0) == 0, pl.program_id(1) == 0))
    def _():
        fill_bias(bias, short)

    def run(masked):
        lane = lax.broadcasted_iota(jnp.int32, (512, 128), 1)
        q, k, v = [[pair_of(ref, n) for n in range(2)] for ref in (q_ref, k_ref, v_ref)]

        def head_of(value, h):
            return jnp.where((lane // 64) == h, value, jnp.zeros_like(value))

        def scores(i):
            s = nt(head_of(q[i // 2], i % 2), k[i // 2])
            return s + bias[...] if masked else s

        logs = jnp.zeros((512, 128), F32)
        mixed = [0.0, 0.0]
        ahead = scores(0)
        for i in range(4):
            s, ahead = ahead, scores(i + 1) if i < 3 else None
            top_score = jnp.max(s, axis=1, keepdims=True) * (SCORE_SCALE * LOG2E)
            p = jnp.exp2(s * (SCORE_SCALE * LOG2E) - top_score)
            total = jnp.sum(p, axis=1, keepdims=True)
            logs = jnp.where(lane == i, top_score + jnp.log2(total), logs)
            mixed[i // 2] = mixed[i // 2] + nn(p.astype(BF16), head_of(v[i // 2], i % 2)) * (1.0 / total)
        for n in range(2):
            attended[:, 0, :, 128 * n : 128 * (n + 1)] = mixed[n].astype(BF16).reshape(2, 256, 128)
        turned = logs.T
        for i in range(4):
            log_totals[i] = turned[i : i + 1, :]

    by_class(short, run)


def gelu_both(u):
    below = 0.5 + 0.5 * lax.erf(u * (0.5**0.5))
    bell = jnp.exp2(u * u * (-0.5 * LOG2E)) * 0.3989422804014327
    return u * below, below + u * bell


def middle_kernel(pieces, n_refs, chips, tab, attended, own, got, gains, *refs):
    sources, refs = refs[:n_refs], refs[n_refs:]
    hidden, normed, w_whole, w_out, sems, w_sem = refs
    i = pl.program_id(0)

    @pl.when(i == 0)
    def _():
        wait_all(pieces.start(sources, tab, {"out": w_out}, sems, 0)["out"])

    x = jnp.where(i < pl.num_programs(0) // 2, own[...], got[...]).astype(F32)
    h = x + nn(attended[...], w_out[...])
    hidden[...] = h
    z, _ = normalized(h)
    normed[...] = (z * gains[1:2, :]).astype(BF16)
    hand_on(w_out, w_whole, w_sem, i, pl.num_programs(0))


def up_tiles(normed, weight, active, slope):
    for i in range(normed.shape[0] // 256):
        rows = slice(256 * i, 256 * (i + 1))
        a, s = gelu_both(nn(normed[rows, :], weight))
        active[rows, :] = a.astype(BF16)
        slope[rows, :] = s.astype(BF16)


def up_kernel(pieces, n_refs, chips, tab, normed, *refs):
    sources, refs = refs[:n_refs], refs[n_refs:]
    active, slope, w_whole, w_up, sems, w_sem = refs
    width = normed.shape[1]
    j = pl.program_id(0)

    @pl.when(j == 0)
    def _():
        wait_all(pieces.start(sources, tab, {"up": w_up}, sems, 0)["up"])

    up_tiles(normed, w_up[:, pl.ds(pl.multiple_of(j * width, 128), width)], active, slope)
    hand_on(w_up, w_whole, w_sem, j, pl.num_programs(0))


def up_rest_kernel(tab, normed, w_up, _active, _slope, active, slope):
    up_tiles(normed, w_up[...], active, slope)


def down_grad_kernel(chips, rows_down, tab, active, cot_own, cot_got, down_mine, down_other):
    half, width = cot_own.shape
    j = pl.program_id(0)

    def run(left, right):
        for m in range(2):
            piece = slice(384 * m, 384 * (m + 1))
            grad = tn(active[:half, piece], cot_own[...]) + tn(active[half:, piece], cot_got[...])
            start = place_of(width * j + 384 * m, rows_down, chips)
            emit(grad[:, : width // 2], start, rows_down, left, slice(None), tab, chips)
            emit(grad[:, width // 2 :], start, rows_down, right, slice(None), tab, chips)

    by_side(tab[2 * chips], down_mine, down_other, run)


def down_back_kernel(chips, rows_up, tab, cot_own, cot_got, normed, slope, w_down, grad_up, up_mine, up_other):
    half, width = cot_own.shape
    j = pl.program_id(0)
    steps = pl.num_programs(0)

    offset = pl.multiple_of(lax.rem(j, steps // 2) * width, 128)

    def run(target):
        for part, cot in enumerate((cot_own, cot_got)):
            for i in range(half // 256):
                inner = slice(256 * i, 256 * (i + 1))
                rows = slice(part * half + 256 * i, part * half + 256 * (i + 1))
                grad_up[rows, :] = (nt(cot[inner, :], w_down[...]) * slope[rows, :].astype(F32)).astype(BF16)
        for m in range(2):
            grad = tn(normed[:, 384 * m : 384 * (m + 1)], grad_up[...])
            emit(grad, place_of(384 * m, rows_up, chips), rows_up, target, pl.ds(offset, width), tab, chips)

    rel = (j // (steps // 2)) ^ tab[2 * chips]

    @pl.when(rel == 0)
    def _():
        run(up_mine)

    @pl.when(rel != 0)
    def _():
        run(up_other)


def up_back_kernel(
    chips, rows_up, tab, grad_up, attended, gains, cot_own, cot_got, hidden, _mine, _other, w_up, w_out, *refs
):
    grad_hidden, grad_att, out_mine, out_other, total_out = refs
    i = pl.program_id(0)
    steps = pl.num_programs(0)
    width = hidden.shape[1]

    @pl.when(i == 0)
    def _():
        total_out[...] = jnp.zeros_like(total_out)

    cot = jnp.where(i < steps // 2, cot_own[...], cot_got[...]).astype(F32)
    e = nt(grad_up[...], w_up[...])
    z, root = normalized(hidden[...])
    total = cot + norm_back(z, root, e * gains[1:2, :])
    grad_hidden[...] = total
    low = total.astype(BF16)
    grad_att[...] = nt(low, w_out[...]).astype(BF16)
    total_out[...] += tn(attended[...], low)

    @pl.when(i == steps - 1)
    def _():
        def run(left, right):
            for m in range(2):
                start = place_of(384 * m, rows_up, chips)
                for side, ref in enumerate((left, right)):
                    value = total_out[384 * m : 384 * (m + 1), side * (width // 2) : (side + 1) * (width // 2)]
                    emit(value, start, rows_up, ref, slice(None), tab, chips)

        by_side(tab[2 * chips], out_mine, out_other, run)


def output_kernel(pieces, n_refs, chips, tab, active, hidden, *refs):
    sources, refs = refs[:n_refs], refs[n_refs:]
    out, w_whole, w_down, sems, w_sem = refs

    @pl.when(pl.program_id(0) == 0)
    def _():
        wait_all(pieces.start(sources, tab, {"down": w_down}, sems, 0)["down"])

    out[...] = (hidden[...] + nn(active[...], w_down[...])).astype(BF16)
    hand_on(w_down, w_whole, w_sem, pl.program_id(0), pl.num_programs(0))


def attend_back_kernel(chips, tab, q_ref, k_ref, v_ref, o_ref, d_ref, log_totals, grad_q_ref, grad_k_ref, grad_v_ref, bias):
    short = tab[2 * chips + 1]

    @pl.when(jnp.logical_and(pl.program_id(0) == 0, pl.program_id(1) == 0))
    def _():
        fill_bias(bias, short)

    def put(ref, n, value):
        ref[:, 0, :, 128 * n : 128 * (n + 1)] = value.astype(BF16).reshape(2, 256, 128)

    def run(masked):
        lane = lax.broadcasted_iota(jnp.int32, (512, 128), 1)
        q, k, v, o, d = [[pair_of(r, n) for n in range(2)] for r in (q_ref, k_ref, v_ref, o_ref, d_ref)]
        k_t = [value.T for value in k]
        dots = [(a.astype(F32) * b.astype(F32)).T for a, b in zip(o, d)]

        def head_of(value, h):
            return jnp.where((lane // 64) == h, value, jnp.zeros_like(value))

        def first(i):
            n, h = i // 2, i % 2
            s = nt(head_of(k[n], h), q[n])
            return (s + bias[...] if masked else s), nt(head_of(v[n], h), d[n])

        ready = [first(0), first(1)]
        grad_q, grad_k, grad_v = [[], []], [0.0, 0.0], [0.0, 0.0]
        for i in range(4):
            if i < 2:
                ready.append(first(i + 2))
            s, grad_p = ready[i]
            ready[i] = None
            n, h = i // 2, i % 2
            delta = jnp.sum(dots[n][64 * h : 64 * h + 64, :], axis=0, keepdims=True)
            p = jnp.exp2(s * (SCORE_SCALE * LOG2E) - log_totals[i])
            grad_s = (p * (grad_p - delta)).astype(BF16)
            grad_v[n] = grad_v[n] + nn(p.astype(BF16), head_of(d[n], h))
            grad_k[n] = grad_k[n] + nn(grad_s, head_of(q[n], h))
            grad_q[n].append(nn(k_t[n][64 * h : 64 * h + 64, :], grad_s))
        for n in range(2):
            put(grad_q_ref, n, jnp.concatenate(grad_q[n], axis=0).T * SCORE_SCALE)
            put(grad_k_ref, n, grad_k[n] * SCORE_SCALE)
            put(grad_v_ref, n, grad_v[n])

    by_class(short, run)


def qkv_grad_kernel(chips, rows_qkv, cuts, tab, normed, *refs):
    grads, mine, other = refs[:-2], refs[-2], refs[-1]
    width = normed.shape[1]
    wide = 3 * width // 2

    def run(*sides):
        for n, ref in enumerate(grads):
            base = (n % 3) * width + cuts[n // 3]
            size = ref.shape[1]
            for m in range(2):
                grad = tn(normed[:, 384 * m : 384 * (m + 1)], ref[...])
                start = place_of(384 * m, rows_qkv, chips)
                at = base
                while at < base + size:
                    side = at // wide
                    end = min(base + size, (side + 1) * wide)
                    columns = slice(at - side * wide, end - side * wide)
                    emit(grad[:, at - base : end - base], start, rows_qkv, sides[side], columns, tab, chips)
                    at = end

    by_side(tab[2 * chips], mine, other, run)


def first_kernel(cuts, tab, own, got, gains, grad_hidden, w_qkv, *refs):
    grads, (out_own, out_got) = refs[:-2], refs[-2:]
    width = own.shape[1]
    here = pl.program_id(0) < pl.num_programs(0) // 2
    e = 0.0
    for n, grad in enumerate(grads):
        base, lot = (n % 3) * width, n // 3
        e = e + nt(grad[...], w_qkv[:, base + cuts[lot] : base + cuts[lot + 1]])
    z, root = normalized(jnp.where(here, own[...], got[...]).astype(F32))
    value = (grad_hidden[...] + norm_back(z, root, e * gains[0:1, :])).astype(BF16)

    @pl.when(here)
    def _():
        out_own[...] = value

    @pl.when(jnp.logical_not(here))
    def _():
        out_got[...] = value


def whole(shape):
    return pl.BlockSpec(shape, lambda *_: (0,) * len(shape))


anywhere = pl.BlockSpec(memory_space=pl.ANY)


def call(kernel, tab, inputs, piece_arrays, outs, scratch, grid=(1,), cost=0, aliases=None, stay=()):
    specs = [spec or whole(a.shape) for a, spec in inputs]
    specs = specs + [pl.BlockSpec(memory_space=pltpu.HBM) for _ in piece_arrays]
    blocks = [(a, spec) for a, spec in inputs] + [(o, spec) for o, spec in outs]
    need = SPARE_BYTES
    for array, spec in blocks:
        if spec is anywhere:
            continue
        size = jnp.dtype(array.dtype).itemsize
        for extent in spec.block_shape if spec else array.shape:
            size *= extent
        need += 2 * size
    for buffer in scratch:
        if hasattr(buffer, "shape") and buffer.dtype in (BF16, F32):
            size = buffer.dtype.itemsize if hasattr(buffer.dtype, "itemsize") else jnp.dtype(buffer.dtype).itemsize
            for extent in buffer.shape:
                size *= extent
            need += size
    moved = sum(a.size * a.dtype.itemsize for a, _ in inputs) + sum(a.size * a.dtype.itemsize for a in piece_arrays)
    moved += sum(math.prod(o.shape) * jnp.dtype(o.dtype).itemsize for o, _ in outs)
    inputs = [
        (pltpu.with_memory_space_constraint(a, pltpu.HBM) if n in stay or a.size > 2**21 and spec is not None else a, spec)
        for n, (a, spec) in enumerate(inputs)
    ]
    return pl.pallas_call(
        kernel,
        out_shape=[o for o, _ in outs],
        input_output_aliases=aliases or {},
        grid_spec=pltpu.PrefetchScalarGridSpec(
            num_scalar_prefetch=1,
            grid=grid,
            in_specs=specs,
            out_specs=[spec or whole(o.shape) for o, spec in outs],
            scratch_shapes=scratch,
        ),
        compiler_params=pltpu.CompilerParams(
            dimension_semantics=("arbitrary",) * len(grid), vmem_limit_bytes=min(need, VMEM_BYTES)
        ),
        cost_estimate=pl.CostEstimate(flops=cost, bytes_accessed=moved, transcendentals=0),
    )(tab, *[a for a, _ in inputs], *piece_arrays)


def body(grid, tokens, clip_class, w_qkv, w_out, w_up, w_down, norm_gains, cotangent):
    rows, width = tokens.shape[1:]
    half = rows // 2
    ff = w_up.shape[1]
    here = grid.here()
    mx = here["x"]
    fast = (2 * w_qkv.shape[0]) % 16 == 0 and (2 * w_down.shape[0]) % 16 == 0
    chips = grid.chips if fast else 1

    def split(array):
        own = lax.dynamic_slice(array[0], (mx * half, 0), (half, width))
        away = lax.dynamic_slice(array[0], ((1 - mx) * half, 0), (half, width))
        return own, away

    swap_x = [(0, 1), (1, 0)]
    tok_own, tok_away = split(tokens)
    cot_own, cot_away = split(cotangent)

    if fast:
        spots = [(x, y, z) for x in range(grid.nx) for y in range(grid.ny) for z in range(grid.nz)]
        chip_at = [
            (((mx - x) % grid.nx) * grid.nz + ((here["z"] - z) % grid.nz)) * grid.ny + ((here["y"] - y) % grid.ny)
            for x, y, z in spots
        ]
        place_at = []
        for a in range(chips):
            x, z, y = a // (grid.nz * grid.ny), (a // grid.ny) % grid.nz, a % grid.ny
            rx, rz, ry = (x - mx) % grid.nx, (z - here["z"]) % grid.nz, (y - here["y"]) % grid.ny
            place_at.append((ry * grid.nx + rx) * grid.nz + rz)
        core = here["c"]
    else:
        chip_at, place_at, core = [jnp.int32(0)], [jnp.int32(0)], jnp.int32(0)
    tab = jnp.stack([jnp.asarray(v, jnp.int32) for v in chip_at + place_at + [core, clip_class[0]]])

    def side_of(weight, side):
        wide = weight.shape[1] // 2
        return lax.dynamic_slice(weight, (0, side * wide), (weight.shape[0], wide))

    gain_block = jnp.pad(norm_gains, ((0, 0), (0, 126)))
    fields_a = [("qkv", 0, 3 * width // 2, False), ("gain", 3 * width // 2, 128, True)]
    fields_b = [("up", 0, ff // 2, False), ("out", ff // 2, width // 2, False)]
    fields_c = [("down", 0, width // 2, False)]
    swap_core = functools.partial(lax.ppermute, axis_name=AXES, perm=grid.core_swap())
    if fast:
        def sides(side, group):
            if group == 0:
                return jnp.concatenate([side_of(w_qkv, side), gain_block], axis=1)
            if group == 1:
                return jnp.concatenate([side_of(w_up, side), side_of(w_out, side)], axis=1)
            return side_of(w_down, side)

        def with_partner(group):
            keep, other = sides(core, group), swap_core(sides(1 - core, group))
            return jnp.concatenate(
                [jnp.where(core == 0, keep, other), jnp.where(core == 0, other, keep)], axis=0
            )

        tok_away, w_qkv = together(tok_away, w_qkv)
        tok_got = lax.ppermute(tok_away, "seq", swap_x)
        piece_a = with_partner(0)
        piece_a, w_up, w_out, w_down = together(piece_a, w_up, w_out, w_down)
        piece_b, piece_c = with_partner(1), with_partner(2)

        def near_of(lots):
            return [exchange(grid, [lot], axis) for lot, axis in zip(lots, "xy")]

        def widened(lots, near):
            return [joined_parts([lot] + moved) for lot, moved in zip(lots, near)]

        def far_of(wide):
            far = []
            for lot, axis in zip(wide, "yx"):
                far += exchange(grid, [lot], axis)
            return far

        def flat(groups):
            return [part for group in groups for part in group]

        def swapped(parts):
            return [(swap_core(a), s) for a, s in parts]

        def pieces_from(mine, theirs, fields):
            named = lambda parts: [(a, [rel_of(grid, s) for s in spots]) for a, spots in parts]
            return Pieces(chips, named(mine), named(theirs), fields)

        def finish(mine, fields):
            mine = [(a, [rel_of(grid, s) for s in spots]) for a, spots in mine]
            theirs = [(swap_core(a), s) for a, s in mine]
            return Pieces(chips, mine, theirs, fields)

        z_a = gather_along_z(grid, piece_a)
        arrays, tok_got, piece_b = together(arrays_of(z_a), tok_got, piece_b)
        z_a = lots_of(with_arrays(z_a, arrays), 2)
        near_a = near_of(z_a)
        z_b = gather_along_z(grid, piece_b)
        arrays = lax.optimization_barrier(arrays_of(flat(near_a)))
        wide_a = widened(z_a, [[part] for part in with_arrays(flat(near_a), arrays)])
        far_a = far_of(wide_a)
        all_a = wide_a + far_a
        arrays_a, z_own, piece_c, cot_away, cot_own = together(
            arrays_of(all_a), z_b[0][0], piece_c, cot_away, cot_own
        )
        z_b = with_arrays(z_b, [z_own] + arrays_of(z_b[1:]))
        group_a = finish(with_arrays(all_a, arrays_a), fields_a)
        z_b = lots_of(with_arrays(z_b, lax.optimization_barrier(arrays_of(z_b))), grid.nz)
        near_b = exchange(grid, z_b, "x")
        straight_b = exchange(grid, z_b, "y")
        z_c = gather_along_z(grid, piece_c)
    else:
        full = [lax.all_gather(w, AXES, axis=0, tiled=True) for w in (w_qkv, w_out, w_up, w_down, gain_block)]

        def natural(parts, fields):
            sides = []
            for side in range(2):
                cut = [p if p.shape[1] == 128 else p[:, side * (p.shape[1] // 2) : (side + 1) * (p.shape[1] // 2)] for p in parts]
                sides.append([(jnp.concatenate(cut, axis=1)[None], [0])])
            return Pieces(1, sides[0], sides[1], fields)

        group_a = natural([full[0], full[4]], fields_a)
        group_b = natural([full[2], full[1]], fields_b)
        group_c = natural([full[3]], fields_c)
        tok_got = lax.ppermute(tok_away, "seq", swap_x)
        cot_got = lax.ppermute(cot_away, "seq", swap_x)

    sds = jax.ShapeDtypeStruct
    heads = width // HEAD_DIM
    rows_a, rows_c = (2 * w_qkv.shape[0], 2 * w_down.shape[0]) if fast else (width, ff)
    dma = pltpu.SemaphoreType.DMA
    vmem = pltpu.VMEM
    tiles = rows // 256
    tile = lambda columns: pl.BlockSpec((256, columns), lambda i, t: (i, 0))
    own_tile = pl.BlockSpec((256, width), lambda i, t: (jnp.minimum(i, tiles // 2 - 1), 0))
    got_tile = pl.BlockSpec((256, width), lambda i, t: (jnp.maximum(i - tiles // 2, 0), 0))
    chunk = pl.BlockSpec((rows, width), lambda j, t: (0, j))
    low = lambda *shape: sds(shape, BF16)

    packed, normed_first, gains, whole_qkv = call(
        functools.partial(input_kernel, group_a, len(group_a.arrays), chips),
        tab,
        [(tok_own, own_tile), (tok_got, got_tile)],
        group_a.arrays,
        [(pltpu.HBM((rows, 3 * width), BF16), tile(3 * width)), (low(rows, width), tile(width)), (sds((8, width), F32), None),
         (pltpu.HBM((width, 3 * width), BF16), anywhere)],
        [vmem((width, 3 * width), BF16), vmem((width, 128), BF16), dma((group_a.copies(("qkv", "gain")),)), dma((1,))],
        grid=(tiles,),
        cost=2 * rows * width * 3 * width,
    )

    if fast:
        packed, arrays_b, arrays_s, arrays_c, cot_away = together(
            packed, arrays_of(near_b), arrays_of(straight_b), arrays_of(z_c), cot_away
        )
        near_b, straight_b = with_arrays(near_b, arrays_b), with_arrays(straight_b, arrays_s)
        z_c = with_arrays(z_c, arrays_c)
        early_b = z_b + near_b + straight_b
        far_b = exchange(grid, near_b, "y")
        cot_got = lax.ppermute(cot_away, "seq", swap_x)
        their_early_b = swapped(early_b)

    clip_blocks = half // 256
    by_clip = lambda a: a.reshape(2, clip_blocks, 256, a.shape[1])
    clip_shape = low(2, clip_blocks, 256, width)
    step = width // 256
    totals_shape = sds((clip_blocks * heads, 1, 512), F32)

    def attend(first, last, packed, earlier):
        at = lambda base: pl.BlockSpec((2, 1, 256, 256), lambda b, g, t: (0, first + b, 0, base + g))
        totals = pl.BlockSpec((4, 1, 512), lambda b, g, t: ((first + b) * (heads // 4) + g, 0, 0))
        return call(
            functools.partial(attend_kernel, chips),
            tab,
            [(by_clip(packed), at(0)), (by_clip(packed), at(step)), (by_clip(packed), at(2 * step))]
            + [(a, anywhere) for a in earlier],
            [],
            [(clip_shape, at(0)), (totals_shape, totals)],
            [vmem((512, 512), F32)],
            grid=(last - first, heads // 4),
            cost=8 * rows * 512 * width * (last - first) // clip_blocks,
            aliases={4: 0, 5: 1} if earlier else None,
        )

    attended, log_totals = attend(0, clip_blocks, packed, [])
    attended = attended.reshape(rows, width)

    if fast:
        attended, arrays_b, arrays_w, arrays_c, cot_got = together(
            attended, arrays_of(far_b), arrays_of(their_early_b), arrays_of(z_c), cot_got
        )
        far_b, their_early_b = with_arrays(far_b, arrays_b), with_arrays(their_early_b, arrays_w)
        group_b = pieces_from(early_b + far_b, their_early_b + swapped(far_b), fields_b)
        z_c = [joined_parts(with_arrays(z_c, arrays_c))]
        near_c = exchange(grid, z_c, "x")
        straight_c = exchange(grid, z_c, "y")

    hidden, normed_second, whole_out = call(
        functools.partial(middle_kernel, group_b, len(group_b.arrays), chips),
        tab,
        [(attended, tile(width)), (tok_own, own_tile), (tok_got, got_tile), (gains, None)],
        group_b.arrays,
        [
            (sds((rows, width), F32), tile(width)), (low(rows, width), tile(width)),
            (pltpu.HBM((width, width), BF16), anywhere),
        ],
        [vmem((width, width), BF16), dma((group_b.copies(("out",)),)), dma((1,))],
        grid=(tiles,),
        cost=2 * rows * width * width,
    )

    steps = ff // width

    split_up = steps // 2
    wide_hbm = pltpu.HBM((rows, ff), BF16)
    active, slope, whole_up = call(
        functools.partial(up_kernel, group_b, len(group_b.arrays), chips),
        tab,
        [(normed_second, None)],
        group_b.arrays,
        [(wide_hbm, chunk), (wide_hbm, chunk), (pltpu.HBM((width, ff), BF16), anywhere)],
        [vmem((width, ff), BF16), dma((group_b.copies(("up",)),)), dma((1,))],
        grid=(split_up,),
        cost=2 * rows * width * width * split_up,
    )
    if fast:
        active, slope, normed_second, arrays_c, arrays_s = together(
            active, slope, normed_second, arrays_of(near_c), arrays_of(straight_c)
        )
        near_c, straight_c = with_arrays(near_c, arrays_c), with_arrays(straight_c, arrays_s)
        far_c = exchange(grid, near_c, "y")
    rest = pl.BlockSpec((rows, width), lambda j, t: (0, split_up + j))
    active, slope = call(
        up_rest_kernel,
        tab,
        [
            (normed_second, None), (whole_up, pl.BlockSpec((width, width), lambda j, t: (0, split_up + j))),
            (active, anywhere), (slope, anywhere),
        ],
        [],
        [(wide_hbm, rest), (wide_hbm, rest)],
        [],
        grid=(steps - split_up,),
        cost=2 * rows * width * width * (steps - split_up),
        aliases={3: 0, 4: 1},
    )
    if fast:
        early_c = z_c + near_c + straight_c
        active, slope, arrays_c = together(active, slope, arrays_of(early_c))
        early_c = with_arrays(early_c, arrays_c)
        their_early_c = swapped(early_c)
    down_out = low(chips, rows_c, width // 2)
    down_mine, down_other = call(
        functools.partial(down_grad_kernel, chips, rows_c),
        tab,
        [(active, chunk), (cot_own, None), (cot_got, None)],
        [],
        [(down_out, None), (down_out, None)],
        [],
        grid=(steps,),
        cost=2 * rows * width * ff,
    )

    def steps_of(mine, other, cut):
        if fast:
            return scatter_steps(grid, mine, other, cut)

        def plain():
            whole_sum = jnp.concatenate([mine[0], other[0]], axis=1)
            back = yield []
            for _ in range(3):
                back = yield back
            yield lax.psum_scatter(whole_sum, AXES, scatter_dimension=0, tiled=True).astype(F32)

        return plain()

    def owned(total):
        if not fast:
            return total[:, : total.shape[1] // 2], total[:, total.shape[1] // 2 :]
        height = total.shape[0] // 2
        keep = lax.dynamic_slice(total, (core * height, 0), (height, total.shape[1]))
        away = lax.dynamic_slice(total, ((1 - core) * height, 0), (height, total.shape[1]))
        got = swap_core(away.astype(BF16)).astype(F32)
        return jnp.where(core == 0, keep, got), jnp.where(core == 0, got, keep)

    if fast:
        down_mine, down_other, active, arrays_c, arrays_w = together(
            down_mine, down_other, active, arrays_of(far_c), arrays_of(their_early_c)
        )
        far_c, their_early_c = with_arrays(far_c, arrays_c), with_arrays(their_early_c, arrays_w)
        their_far_c = swapped(far_c)
        down_mine, down_other, arrays_w = together(down_mine, down_other, arrays_of(their_far_c))
        group_c = pieces_from(early_c + far_c, their_early_c + with_arrays(their_far_c, arrays_w), fields_c)
    outputs, whole_down = call(
        functools.partial(output_kernel, group_c, len(group_c.arrays), chips),
        tab,
        [(active, tile(ff)), (hidden, tile(width))],
        group_c.arrays,
        [(low(rows, width), tile(width)), (pltpu.HBM((ff, width), BF16), anywhere)],
        [vmem((ff, width), BF16), dma((group_c.copies(("down",)),)), dma((1,))],
        grid=(tiles,),
        cost=2 * rows * width * ff,
    )
    down_sum = steps_of(down_mine, down_other, 2)
    arrived = next(down_sum)
    outputs, arrived, slope = together(outputs, arrived, slope)
    arrived = down_sum.send(arrived)
    def joined(own, back):
        first = mx == 0
        return jnp.concatenate([jnp.where(first, own, back), jnp.where(first, back, own)], axis=0)[None]

    up_part = pl.BlockSpec((chips, rows_a, ff // 2), lambda *_: (0, 0, 0))
    out_part = pl.BlockSpec((chips, rows_a, width // 2), lambda *_: (0, 0, ff // width))
    up_out = low(chips, rows_a, ff // 2 + width // 2)
    grad_up, up_mine, up_other = call(
        functools.partial(down_back_kernel, chips, rows_a),
        tab,
        [
            (cot_own, None), (cot_got, None), (normed_second, None), (slope, chunk),
            (whole_down, pl.BlockSpec((width, width), lambda j, t: (j, 0))),
        ],
        [],
        [(pltpu.HBM((rows, ff), BF16), chunk), (up_out, up_part), (up_out, up_part)],
        [],
        grid=(steps,),
        cost=4 * rows * width * ff,
    )
    grad_up, up_mine, up_other, arrived = together(grad_up, up_mine, up_other, arrived)
    arrived = down_sum.send(arrived)
    quarter = half // 2
    out_first = lax.ppermute(outputs[half : half + quarter], "seq", swap_x)
    grad_hidden, grad_att, up_mine, up_other = call(
        functools.partial(up_back_kernel, chips, rows_a),
        tab,
        [
            (grad_up, tile(ff)), (attended, tile(width)), (gains, None), (cot_own, own_tile), (cot_got, got_tile),
            (hidden, tile(width)), (up_mine, anywhere), (up_other, anywhere),
            (whole_up, None), (whole_out, None),
        ],
        [],
        [(pltpu.HBM((rows, width), F32), tile(width)), (low(rows, width), tile(width)), (up_out, out_part), (up_out, out_part)],
        [vmem((width, width), F32)],
        grid=(tiles,),
        cost=2 * rows * width * ff + 4 * rows * width * width,
        aliases={7: 2, 8: 3},
    )
    grad_att, grad_hidden, up_mine, up_other, arrived, out_first, out_next = together(
        grad_att, grad_hidden, up_mine, up_other, arrived, out_first, outputs[half + quarter :]
    )
    out_second = lax.ppermute(out_next, "seq", swap_x)
    arrived = down_sum.send(arrived)
    up_sum = steps_of(up_mine, up_other, 2)
    arrived_up = next(up_sum)

    groups = heads // 4
    group_cut = max(1, groups // 3)
    cuts = [0, 256 * group_cut, width]

    def attend_back(first, last, grad_att):
        at = lambda base: pl.BlockSpec((2, 1, 256, 256), lambda b, g, t: (0, b, 0, base + first + g))
        to = pl.BlockSpec((2, 1, 256, 256), lambda b, g, t: (0, b, 0, g))
        totals = pl.BlockSpec((4, 1, 512), lambda b, g, t: (b * groups + first + g, 0, 0))
        shape = pltpu.HBM((2, clip_blocks, 256, 256 * (last - first)), BF16)
        grads = call(
            functools.partial(attend_back_kernel, chips),
            tab,
            [
                (by_clip(packed), at(0)), (by_clip(packed), at(step)), (by_clip(packed), at(2 * step)),
                (by_clip(attended), at(0)), (by_clip(grad_att), at(0)), (log_totals, totals),
            ],
            [],
            [(shape, to)] * 3,
            [vmem((512, 512), F32)],
            grid=(clip_blocks, last - first),
            cost=30 * rows * 512 * 256 * (last - first),
        )
        return [g.reshape(rows, 256 * (last - first)) for g in grads]

    grads_a = attend_back(0, group_cut, grad_att)
    grads_a, grad_att, arrived_up, out_second = together(grads_a, grad_att, arrived_up, out_second)
    arrived_up = up_sum.send(arrived_up)
    grads_b = attend_back(group_cut, groups, grad_att)
    grads_b, arrived_up, arrived = together(grads_b, arrived_up, arrived)
    arrived_down = arrived
    arrived_up, grads_b, normed_first = up_sum.send((arrived_up, grads_b, normed_first))
    qkv_out = low(chips, rows_a, 3 * width // 2)
    qkv_mine, qkv_other = call(
        functools.partial(qkv_grad_kernel, chips, rows_a, cuts),
        tab,
        [(normed_first, None)] + [(g, None) for g in grads_a + grads_b],
        [],
        [(qkv_out, None), (qkv_out, None)],
        [],
        cost=2 * rows * width * 3 * width,
        stay=tuple(range(1, 7)),
    )
    qkv_mine, qkv_other, grads_a, grads_b, tok_own, arrived_up = together(
        qkv_mine, qkv_other, grads_a, grads_b, tok_own, arrived_up
    )
    arrived_up, tok_got, qkv_mine, qkv_other = up_sum.send((arrived_up, tok_got, qkv_mine, qkv_other))
    qkv_sum = steps_of(qkv_mine, qkv_other, 2)
    arrived = next(qkv_sum)
    arrived, tok_own = qkv_sum.send((arrived, tok_own))

    grad_own, grad_got = call(
        functools.partial(first_kernel, cuts),
        tab,
        [
            (tok_own, own_tile), (tok_got, got_tile), (gains, None), (grad_hidden, tile(width)), (whole_qkv, None),
        ]
        + [(g, tile(g.shape[1])) for g in grads_a + grads_b],
        [],
        [(low(half, width), own_tile), (low(half, width), got_tile)],
        [],
        grid=(tiles,),
        cost=2 * rows * width * 3 * width,
        stay=(3, 4) + tuple(range(5, 11)),
    )
    grad_got, grad_own, arrived, arrived_up, arrived_down = together(
        grad_got, grad_own, arrived, arrived_up, arrived_down
    )
    arrived = qkv_sum.send(arrived)
    arrived, grad_got = together(arrived, grad_got)
    grad_back = lax.ppermute(grad_got, "seq", swap_x)
    arrived_up, arrived, arrived_down, out_first, out_second = together(
        arrived_up, arrived, arrived_down, out_first, out_second
    )
    arrived = qkv_sum.send(arrived)
    left, right = owned(down_sum.send(arrived_down))
    owned_down = jnp.concatenate([left, right], axis=1)
    left, right = owned(up_sum.send(arrived_up))
    owned_up = jnp.concatenate([left[:, : ff // 2], right[:, : ff // 2]], axis=1)
    owned_out = jnp.concatenate([left[:, ff // 2 :], right[:, ff // 2 :]], axis=1)
    output_tokens = joined(outputs[:half], jnp.concatenate([out_first, out_second], axis=0))
    left, right = owned(qkv_sum.send(arrived))
    owned_qkv = jnp.concatenate([left, right], axis=1)
    grad_tokens = joined(grad_own, grad_back)

    scale = norm_gains.astype(F32)
    first_gain = jnp.sum(w_qkv.astype(F32) * owned_qkv, axis=1) / scale[:, 0]
    second_gain = jnp.sum(w_up.astype(F32) * owned_up, axis=1) / scale[:, 1]
    owned_gains = jnp.stack([first_gain, second_gain], axis=1)
    return (output_tokens, grad_tokens, owned_qkv, owned_out, owned_up, owned_down, owned_gains)


def solution(mesh):
    grid = Grid(mesh.shape["seq"], mesh.shape["clips"])
    shard = P(AXES, None)
    return jax.shard_map(
        functools.partial(body, grid),
        mesh=mesh,
        in_specs=(P("seq", "clips", None), P("clips"), shard, shard, shard, shard, shard, P("seq", "clips", None)),
        out_specs=(P("seq", "clips", None), P("seq", "clips", None), shard, shard, shard, shard, shard),
        check_vma=False,
    )
```

```python
import functools
import math

import jax
import jax.numpy as jnp
from jax import lax
from jax.experimental import pallas as pl
from jax.experimental.pallas import tpu as pltpu
from jax.sharding import PartitionSpec as P

HEAD_DIM = 64
CLIP = 512
EPSILON = 1e-05
AXES = ("seq", "clips")
LOG2E = 1.4426950408889634
SCORE_SCALE = HEAD_DIM ** (-0.5)
BF16 = jnp.bfloat16
F32 = jnp.float32
VMEM_BYTES = 58 * 1024 * 1024
SPARE_BYTES = 8 * 1024 * 1024


class Grid:
    def __init__(self, seq, clips):
        self.nx = seq
        self.clips = clips
        pairs = clips // 2
        bits = pairs.bit_length() - 1
        self.ny = 2 ** (bits // 3)
        self.nz = pairs // self.ny
        self.sizes = {"x": self.nx, "y": self.ny, "z": self.nz}
        self.chips = self.nx * self.ny * self.nz

    def index(self, x, z, y, c):
        return x * self.clips + (z * self.ny + y) * 2 + c

    def shift(self, axis, k):
        pairs = []
        for x in range(self.nx):
            for z in range(self.nz):
                for y in range(self.ny):
                    for c in range(2):
                        t = {"x": x, "y": y, "z": z}
                        t[axis] = (t[axis] + k) % self.sizes[axis]
                        pairs.append((self.index(x, z, y, c), self.index(t["x"], t["z"], t["y"], c)))
        return pairs

    def core_swap(self):
        return [(i, i ^ 1) for i in range(self.nx * self.clips)]

    def here(self):
        x = lax.axis_index("seq")
        rest = lax.axis_index("clips")
        return {"x": x, "z": rest // (2 * self.ny), "y": (rest // 2) % self.ny, "c": rest % 2}


def rel_of(grid, coords):
    return (coords["x"] * grid.ny + coords["y"]) * grid.nz + coords["z"]


def together(*values):
    return lax.optimization_barrier(values)


def exchange(grid, parts, axis):
    moved = []
    for k in range(1, grid.sizes[axis]):
        for array, spots in parts:
            moved.append((lax.ppermute(array, AXES, grid.shift(axis, k)), [{**s, axis: k} for s in spots]))
    return moved


def joined_parts(parts):
    if len(parts) == 1:
        return parts[0]
    return (jnp.concatenate([a for a, _ in parts], axis=0), [s for _, spots in parts for s in spots])


def gather_along_z(grid, piece):
    parts = [(piece[None], [{"x": 0, "y": 0, "z": 0}])]
    return parts + exchange(grid, parts, "z")


def lots_of(parts, cut):
    cut = min(cut, len(parts))
    return [joined_parts(p) for p in (parts[:cut], parts[cut:]) if p]


def arrays_of(parts):
    return [a for a, _ in parts]


def with_arrays(parts, arrays):
    return [(a, s) for a, (_, s) in zip(arrays, parts)]


def scatter_steps(grid, mine, other, cut):
    got = lax.ppermute(other, AXES, grid.core_swap())
    back = yield [got]
    (got,), held = (back[0], tuple(back[1:])) if isinstance(back, tuple) else (back, ())
    shape = (grid.ny, grid.nx, grid.nz) + mine.shape[1:]
    mine, got = mine.reshape(shape), got.reshape(shape)
    cut = min(cut, grid.nz)
    lots = [(lo, hi, axes) for lo, hi, axes in ((0, cut, "yx"), (cut, grid.nz, "xy")) if hi > lo]
    current = [[mine[:, :, lo:hi], got[:, :, lo:hi]] for lo, hi, _ in lots]
    for step in range(2):
        waiting = []
        for n, (_, _, axes) in enumerate(lots):
            axis = axes[step]
            dim = 1 if axis == "x" and step == 0 else 0
            pieces = [
                [lax.index_in_dim(c, k, dim, keepdims=False) for c in current[n]] for k in range(grid.sizes[axis])
            ]
            waiting.append([add_all(pieces[k]).astype(BF16) for k in range(1, grid.sizes[axis])])
            current[n] = pieces[0]
        if held:
            waiting, held = together(waiting, held)
        for n, (_, _, axes) in enumerate(lots):
            waiting[n] = [
                lax.ppermute(total, AXES, grid.shift(axes[step], k + 1)) for k, total in enumerate(waiting[n])
            ]
        flat = [a for received in waiting for a in received]
        back = yield (flat, *held) if held else flat
        flat, held = (back[0], tuple(back[1:])) if isinstance(back, tuple) else (list(back), ())
        for n, received in enumerate(waiting):
            current[n] = current[n] + flat[: len(received)]
            flat = flat[len(received) :]
    final = []
    for k in range(grid.nz):
        n = 0 if k < lots[0][1] else 1
        final.append(add_all([c[k - lots[n][0]] for c in current[n]]))
    leaving = [total.astype(BF16) for total in final[1:]]
    if held:
        leaving, held = together(leaving, held)
    flat = [lax.ppermute(total, AXES, grid.shift("z", k + 1)) for k, total in enumerate(leaving)]
    back = yield (flat, *held) if held else flat
    final[1:] = back[0] if isinstance(back, tuple) else back
    yield add_all(final)


def add_all(items):
    total = items[0].astype(F32)
    for item in items[1:]:
        total = total + item.astype(F32)
    return total


def nn(a, b):
    return lax.dot_general(a, b, (((1,), (0,)), ((), ())), preferred_element_type=F32)


def nt(a, b):
    return lax.dot_general(a, b, (((1,), (1,)), ((), ())), preferred_element_type=F32)


def tn(a, b):
    return lax.dot_general(a, b, (((0,), (0,)), ((), ())), preferred_element_type=F32)


def normalized(values):
    centered = values - jnp.mean(values, axis=-1, keepdims=True)
    spread = jnp.mean(centered * centered, axis=-1, keepdims=True)
    root = lax.rsqrt(spread + EPSILON)
    return centered * root, root


def norm_back(z, root, scaled):
    return root * (
        scaled
        - jnp.mean(scaled, axis=-1, keepdims=True)
        - z * jnp.mean(scaled * z, axis=-1, keepdims=True)
    )


class Pieces:
    def __init__(self, chips, mine, theirs, fields):
        self.chips = chips
        self.arrays = [a for a, _ in mine] + [a for a, _ in theirs]
        self.spots = [s for _, s in mine] + [s for _, s in theirs]
        self.count_mine = len(mine)
        self.rows = self.arrays[0].shape[1]
        self.fields = fields

    def copies(self, wanted):
        total = 0
        for n, spots in enumerate(self.spots):
            for name, column, width, gain in self.fields:
                if name in wanted and not (gain and n >= self.count_mine):
                    total += len(spots)
        return total

    def start(self, refs, tab, wanted, sems, first):
        core = tab[2 * self.chips]
        started = {name: [] for name in wanted}
        n_sem = first
        for n, spots in enumerate(self.spots):
            for name, column, width, gain in self.fields:
                if name not in wanted or (gain and n >= self.count_mine):
                    continue
                for k, r in enumerate(spots):
                    row = pl.multiple_of(tab[r] * self.rows, 16)
                    if gain:
                        place = wanted[name].at[pl.ds(row, self.rows), :]
                    else:
                        side = core if n < self.count_mine else 1 - core
                        col = pl.multiple_of(side * width, 128)
                        place = wanted[name].at[pl.ds(row, self.rows), pl.ds(col, width)]
                    copy = pltpu.make_async_copy(
                        refs[n].at[k, :, column : column + width], place, sems.at[n_sem]
                    )
                    copy.start()
                    started[name].append(copy)
                    n_sem += 1
        return started


def hand_on(scratch, target, sem, step, steps):
    copy = pltpu.make_async_copy(scratch, target, sem.at[0])

    @pl.when(step == 0)
    def _():
        copy.start()

    @pl.when(step == steps - 1)
    def _():
        copy.wait()


def wait_all(copies):
    for copy in copies:
        copy.wait()


def emit(value, first_chip, rows, ref, columns, tab, chips):
    height = value.shape[0]
    low = value.astype(BF16)
    if rows >= height:
        ref[0, pl.ds(first_chip, height), columns] = low
    else:
        for a in range(height // rows):
            ref[tab[chips + first_chip + a], :, columns] = low[a * rows : (a + 1) * rows]


def by_side(core, mine, other, run):
    @pl.when(core == 0)
    def _():
        run(mine, other)

    @pl.when(core != 0)
    def _():
        run(other, mine)


def place_of(row, rows, chips):
    return row if chips == 1 else row // rows


def input_kernel(pieces, n_refs, chips, tab, own, got, *refs):
    sources, refs = refs[:n_refs], refs[n_refs:]
    packed, normed, gains, w_whole, w_qkv, gain_cols, sems, w_sem = refs
    i = pl.program_id(0)
    steps = pl.num_programs(0)
    width = own.shape[1]

    @pl.when(i == 0)
    def _():
        started = pieces.start(sources, tab, {"gain": gain_cols, "qkv": w_qkv}, sems, 0)
        wait_all(started["gain"])
        pick = (
            lax.broadcasted_iota(jnp.int32, (8, 128), 0) == lax.broadcasted_iota(jnp.int32, (8, 128), 1)
        ).astype(BF16)
        gains[...] = nt(pick, gain_cols[...])
        wait_all(started["qkv"])

    x = jnp.where(i < steps // 2, own[...], got[...]).astype(F32)
    z, _ = normalized(x)
    low = (z * gains[0:1, :]).astype(BF16)
    normed[...] = low
    for c in range(3):
        cols = slice(c * width, (c + 1) * width)
        packed[:, cols] = nn(low, w_qkv[:, cols]).astype(BF16)
    hand_on(w_qkv, w_whole, w_sem, i, steps)


def pair_of(ref, n):
    return ref[:, 0, :, 128 * n : 128 * (n + 1)].reshape(512, 128)


def fill_bias(bias, short):
    row_clip = (lax.broadcasted_iota(jnp.int32, (512, 512), 0) // 128) % 2
    col_clip = (lax.broadcasted_iota(jnp.int32, (512, 512), 1) // 128) % 2
    apart = jnp.logical_and(row_clip != col_clip, short != 0)
    bias[...] = jnp.where(apart, -1e30, 0.0)


def by_class(short, run):
    @pl.when(short == 0)
    def _():
        run(False)

    @pl.when(short != 0)
    def _():
        run(True)


def attend_kernel(chips, tab, q_ref, k_ref, v_ref, *refs):
    attended, log_totals, bias = refs[-3:]
    short = tab[2 * chips + 1]

    @pl.when(jnp.logical_and(pl.program_id(0) == 0, pl.program_id(1) == 0))
    def _():
        fill_bias(bias, short)

    def run(masked):
        lane = lax.broadcasted_iota(jnp.int32, (512, 128), 1)
        q, k, v = [[pair_of(ref, n) for n in range(2)] for ref in (q_ref, k_ref, v_ref)]

        def head_of(value, h):
            return jnp.where((lane // 64) == h, value, jnp.zeros_like(value))

        def scores(i):
            s = nt(head_of(q[i // 2], i % 2), k[i // 2])
            return s + bias[...] if masked else s

        logs = jnp.zeros((512, 128), F32)
        mixed = [0.0, 0.0]
        ahead = scores(0)
        for i in range(4):
            s, ahead = ahead, scores(i + 1) if i < 3 else None
            top_score = jnp.max(s, axis=1, keepdims=True) * (SCORE_SCALE * LOG2E)
            p = jnp.exp2(s * (SCORE_SCALE * LOG2E) - top_score)
            total = jnp.sum(p, axis=1, keepdims=True)
            logs = jnp.where(lane == i, top_score + jnp.log2(total), logs)
            mixed[i // 2] = mixed[i // 2] + nn(p.astype(BF16), head_of(v[i // 2], i % 2)) * (1.0 / total)
        for n in range(2):
            attended[:, 0, :, 128 * n : 128 * (n + 1)] = mixed[n].astype(BF16).reshape(2, 256, 128)
        turned = logs.T
        for i in range(4):
            log_totals[i] = turned[i : i + 1, :]

    by_class(short, run)


def gelu_both(u):
    below = 0.5 + 0.5 * lax.erf(u * (0.5**0.5))
    bell = jnp.exp2(u * u * (-0.5 * LOG2E)) * 0.3989422804014327
    return u * below, below + u * bell


def middle_kernel(pieces, n_refs, chips, tab, attended, own, got, gains, *refs):
    sources, refs = refs[:n_refs], refs[n_refs:]
    hidden, normed, w_whole, w_out, sems, w_sem = refs
    i = pl.program_id(0)

    @pl.when(i == 0)
    def _():
        wait_all(pieces.start(sources, tab, {"out": w_out}, sems, 0)["out"])

    x = jnp.where(i < pl.num_programs(0) // 2, own[...], got[...]).astype(F32)
    h = x + nn(attended[...], w_out[...])
    hidden[...] = h
    z, _ = normalized(h)
    normed[...] = (z * gains[1:2, :]).astype(BF16)
    hand_on(w_out, w_whole, w_sem, i, pl.num_programs(0))


def up_tiles(normed, weight, active, slope):
    for i in range(normed.shape[0] // 256):
        rows = slice(256 * i, 256 * (i + 1))
        a, s = gelu_both(nn(normed[rows, :], weight))
        active[rows, :] = a.astype(BF16)
        slope[rows, :] = s.astype(BF16)


def up_kernel(pieces, n_refs, chips, tab, normed, *refs):
    sources, refs = refs[:n_refs], refs[n_refs:]
    active, slope, w_whole, w_up, sems, w_sem = refs
    width = normed.shape[1]
    j = pl.program_id(0)

    @pl.when(j == 0)
    def _():
        wait_all(pieces.start(sources, tab, {"up": w_up}, sems, 0)["up"])

    up_tiles(normed, w_up[:, pl.ds(pl.multiple_of(j * width, 128), width)], active, slope)
    hand_on(w_up, w_whole, w_sem, j, pl.num_programs(0))


def up_rest_kernel(tab, normed, w_up, _active, _slope, active, slope):
    up_tiles(normed, w_up[...], active, slope)


def down_grad_kernel(chips, rows_down, tab, active, cot_own, cot_got, down_mine, down_other):
    half, width = cot_own.shape
    j = pl.program_id(0)

    def run(left, right):
        for m in range(2):
            piece = slice(384 * m, 384 * (m + 1))
            grad = tn(active[:half, piece], cot_own[...]) + tn(active[half:, piece], cot_got[...])
            start = place_of(width * j + 384 * m, rows_down, chips)
            emit(grad[:, : width // 2], start, rows_down, left, slice(None), tab, chips)
            emit(grad[:, width // 2 :], start, rows_down, right, slice(None), tab, chips)

    by_side(tab[2 * chips], down_mine, down_other, run)


def down_back_kernel(chips, rows_up, tab, cot_own, cot_got, normed, slope, w_down, grad_up, up_mine, up_other):
    half, width = cot_own.shape
    j = pl.program_id(0)
    steps = pl.num_programs(0)

    offset = pl.multiple_of(lax.rem(j, steps // 2) * width, 128)

    def run(target):
        for part, cot in enumerate((cot_own, cot_got)):
            for i in range(half // 256):
                inner = slice(256 * i, 256 * (i + 1))
                rows = slice(part * half + 256 * i, part * half + 256 * (i + 1))
                grad_up[rows, :] = (nt(cot[inner, :], w_down[...]) * slope[rows, :].astype(F32)).astype(BF16)
        for m in range(2):
            grad = tn(normed[:, 384 * m : 384 * (m + 1)], grad_up[...])
            emit(grad, place_of(384 * m, rows_up, chips), rows_up, target, pl.ds(offset, width), tab, chips)

    rel = (j // (steps // 2)) ^ tab[2 * chips]

    @pl.when(rel == 0)
    def _():
        run(up_mine)

    @pl.when(rel != 0)
    def _():
        run(up_other)


def up_back_kernel(
    chips, rows_up, tab, grad_up, attended, gains, cot_own, cot_got, hidden, _mine, _other, w_up, w_out, *refs
):
    grad_hidden, grad_att, out_mine, out_other, total_out = refs
    i = pl.program_id(0)
    steps = pl.num_programs(0)
    width = hidden.shape[1]

    @pl.when(i == 0)
    def _():
        total_out[...] = jnp.zeros_like(total_out)

    cot = jnp.where(i < steps // 2, cot_own[...], cot_got[...]).astype(F32)
    e = nt(grad_up[...], w_up[...])
    z, root = normalized(hidden[...])
    total = cot + norm_back(z, root, e * gains[1:2, :])
    grad_hidden[...] = total
    low = total.astype(BF16)
    grad_att[...] = nt(low, w_out[...]).astype(BF16)
    total_out[...] += tn(attended[...], low)

    @pl.when(i == steps - 1)
    def _():
        def run(left, right):
            for m in range(2):
                start = place_of(384 * m, rows_up, chips)
                for side, ref in enumerate((left, right)):
                    value = total_out[384 * m : 384 * (m + 1), side * (width // 2) : (side + 1) * (width // 2)]
                    emit(value, start, rows_up, ref, slice(None), tab, chips)

        by_side(tab[2 * chips], out_mine, out_other, run)


def output_kernel(pieces, n_refs, chips, tab, active, hidden, *refs):
    sources, refs = refs[:n_refs], refs[n_refs:]
    out, w_whole, w_down, sems, w_sem = refs

    @pl.when(pl.program_id(0) == 0)
    def _():
        wait_all(pieces.start(sources, tab, {"down": w_down}, sems, 0)["down"])

    out[...] = (hidden[...] + nn(active[...], w_down[...])).astype(BF16)
    hand_on(w_down, w_whole, w_sem, pl.program_id(0), pl.num_programs(0))


def attend_back_kernel(chips, tab, q_ref, k_ref, v_ref, o_ref, d_ref, log_totals, grad_q_ref, grad_k_ref, grad_v_ref, bias):
    short = tab[2 * chips + 1]

    @pl.when(jnp.logical_and(pl.program_id(0) == 0, pl.program_id(1) == 0))
    def _():
        fill_bias(bias, short)

    def put(ref, n, value):
        ref[:, 0, :, 128 * n : 128 * (n + 1)] = value.astype(BF16).reshape(2, 256, 128)

    def run(masked):
        lane = lax.broadcasted_iota(jnp.int32, (512, 128), 1)
        q, k, v, o, d = [[pair_of(r, n) for n in range(2)] for r in (q_ref, k_ref, v_ref, o_ref, d_ref)]
        k_t = [value.T for value in k]
        dots = [(a.astype(F32) * b.astype(F32)).T for a, b in zip(o, d)]

        def head_of(value, h):
            return jnp.where((lane // 64) == h, value, jnp.zeros_like(value))

        def first(i):
            n, h = i // 2, i % 2
            s = nt(head_of(k[n], h), q[n])
            return (s + bias[...] if masked else s), nt(head_of(v[n], h), d[n])

        ready = [first(0), first(1)]
        grad_q, grad_k, grad_v = [[], []], [0.0, 0.0], [0.0, 0.0]
        for i in range(4):
            if i < 2:
                ready.append(first(i + 2))
            s, grad_p = ready[i]
            ready[i] = None
            n, h = i // 2, i % 2
            delta = jnp.sum(dots[n][64 * h : 64 * h + 64, :], axis=0, keepdims=True)
            p = jnp.exp2(s * (SCORE_SCALE * LOG2E) - log_totals[i])
            grad_s = (p * (grad_p - delta)).astype(BF16)
            grad_v[n] = grad_v[n] + nn(p.astype(BF16), head_of(d[n], h))
            grad_k[n] = grad_k[n] + nn(grad_s, head_of(q[n], h))
            grad_q[n].append(nn(k_t[n][64 * h : 64 * h + 64, :], grad_s))
        for n in range(2):
            put(grad_q_ref, n, jnp.concatenate(grad_q[n], axis=0).T * SCORE_SCALE)
            put(grad_k_ref, n, grad_k[n] * SCORE_SCALE)
            put(grad_v_ref, n, grad_v[n])

    by_class(short, run)


def qkv_grad_kernel(chips, rows_qkv, cuts, tab, normed, *refs):
    grads, mine, other = refs[:-2], refs[-2], refs[-1]
    width = normed.shape[1]
    wide = 3 * width // 2

    def run(*sides):
        for n, ref in enumerate(grads):
            base = (n % 3) * width + cuts[n // 3]
            size = ref.shape[1]
            for m in range(2):
                grad = tn(normed[:, 384 * m : 384 * (m + 1)], ref[...])
                start = place_of(384 * m, rows_qkv, chips)
                at = base
                while at < base + size:
                    side = at // wide
                    end = min(base + size, (side + 1) * wide)
                    columns = slice(at - side * wide, end - side * wide)
                    emit(grad[:, at - base : end - base], start, rows_qkv, sides[side], columns, tab, chips)
                    at = end

    by_side(tab[2 * chips], mine, other, run)


def first_kernel(cuts, tab, own, got, gains, grad_hidden, w_qkv, *refs):
    grads, (out_own, out_got) = refs[:-2], refs[-2:]
    width = own.shape[1]
    here = pl.program_id(0) < pl.num_programs(0) // 2
    e = 0.0
    for n, grad in enumerate(grads):
        base, lot = (n % 3) * width, n // 3
        e = e + nt(grad[...], w_qkv[:, base + cuts[lot] : base + cuts[lot + 1]])
    z, root = normalized(jnp.where(here, own[...], got[...]).astype(F32))
    value = (grad_hidden[...] + norm_back(z, root, e * gains[0:1, :])).astype(BF16)

    @pl.when(here)
    def _():
        out_own[...] = value

    @pl.when(jnp.logical_not(here))
    def _():
        out_got[...] = value


def whole(shape):
    return pl.BlockSpec(shape, lambda *_: (0,) * len(shape))


anywhere = pl.BlockSpec(memory_space=pl.ANY)


def call(kernel, tab, inputs, piece_arrays, outs, scratch, grid=(1,), cost=0, aliases=None, stay=()):
    specs = [spec or whole(a.shape) for a, spec in inputs]
    specs = specs + [pl.BlockSpec(memory_space=pltpu.HBM) for _ in piece_arrays]
    blocks = [(a, spec) for a, spec in inputs] + [(o, spec) for o, spec in outs]
    need = SPARE_BYTES
    for array, spec in blocks:
        if spec is anywhere:
            continue
        size = jnp.dtype(array.dtype).itemsize
        for extent in spec.block_shape if spec else array.shape:
            size *= extent
        need += 2 * size
    for buffer in scratch:
        if hasattr(buffer, "shape") and buffer.dtype in (BF16, F32):
            size = buffer.dtype.itemsize if hasattr(buffer.dtype, "itemsize") else jnp.dtype(buffer.dtype).itemsize
            for extent in buffer.shape:
                size *= extent
            need += size
    moved = sum(a.size * a.dtype.itemsize for a, _ in inputs) + sum(a.size * a.dtype.itemsize for a in piece_arrays)
    moved += sum(math.prod(o.shape) * jnp.dtype(o.dtype).itemsize for o, _ in outs)
    inputs = [
        (pltpu.with_memory_space_constraint(a, pltpu.HBM) if n in stay or a.size > 2**21 and spec is not None else a, spec)
        for n, (a, spec) in enumerate(inputs)
    ]
    return pl.pallas_call(
        kernel,
        out_shape=[o for o, _ in outs],
        input_output_aliases=aliases or {},
        grid_spec=pltpu.PrefetchScalarGridSpec(
            num_scalar_prefetch=1,
            grid=grid,
            in_specs=specs,
            out_specs=[spec or whole(o.shape) for o, spec in outs],
            scratch_shapes=scratch,
        ),
        compiler_params=pltpu.CompilerParams(
            dimension_semantics=("arbitrary",) * len(grid), vmem_limit_bytes=min(need, VMEM_BYTES)
        ),
        cost_estimate=pl.CostEstimate(flops=cost, bytes_accessed=moved, transcendentals=0),
    )(tab, *[a for a, _ in inputs], *piece_arrays)


def body(grid, tokens, clip_class, w_qkv, w_out, w_up, w_down, norm_gains, cotangent):
    rows, width = tokens.shape[1:]
    half = rows // 2
    ff = w_up.shape[1]
    here = grid.here()
    mx = here["x"]
    fast = (2 * w_qkv.shape[0]) % 16 == 0 and (2 * w_down.shape[0]) % 16 == 0
    chips = grid.chips if fast else 1

    def split(array):
        own = lax.dynamic_slice(array[0], (mx * half, 0), (half, width))
        away = lax.dynamic_slice(array[0], ((1 - mx) * half, 0), (half, width))
        return own, away

    swap_x = [(0, 1), (1, 0)]
    tok_own, tok_away = split(tokens)
    cot_own, cot_away = split(cotangent)

    if fast:
        spots = [(x, y, z) for x in range(grid.nx) for y in range(grid.ny) for z in range(grid.nz)]
        chip_at = [
            (((mx - x) % grid.nx) * grid.nz + ((here["z"] - z) % grid.nz)) * grid.ny + ((here["y"] - y) % grid.ny)
            for x, y, z in spots
        ]
        place_at = []
        for a in range(chips):
            x, z, y = a // (grid.nz * grid.ny), (a // grid.ny) % grid.nz, a % grid.ny
            rx, rz, ry = (x - mx) % grid.nx, (z - here["z"]) % grid.nz, (y - here["y"]) % grid.ny
            place_at.append((ry * grid.nx + rx) * grid.nz + rz)
        core = here["c"]
    else:
        chip_at, place_at, core = [jnp.int32(0)], [jnp.int32(0)], jnp.int32(0)
    tab = jnp.stack([jnp.asarray(v, jnp.int32) for v in chip_at + place_at + [core, clip_class[0]]])

    def side_of(weight, side):
        wide = weight.shape[1] // 2
        return lax.dynamic_slice(weight, (0, side * wide), (weight.shape[0], wide))

    gain_block = jnp.pad(norm_gains, ((0, 0), (0, 126)))
    fields_a = [("qkv", 0, 3 * width // 2, False), ("gain", 3 * width // 2, 128, True)]
    fields_b = [("up", 0, ff // 2, False), ("out", ff // 2, width // 2, False)]
    fields_c = [("down", 0, width // 2, False)]
    swap_core = functools.partial(lax.ppermute, axis_name=AXES, perm=grid.core_swap())
    if fast:
        def sides(side, group):
            if group == 0:
                return jnp.concatenate([side_of(w_qkv, side), gain_block], axis=1)
            if group == 1:
                return jnp.concatenate([side_of(w_up, side), side_of(w_out, side)], axis=1)
            return side_of(w_down, side)

        def with_partner(group):
            keep, other = sides(core, group), swap_core(sides(1 - core, group))
            return jnp.concatenate(
                [jnp.where(core == 0, keep, other), jnp.where(core == 0, other, keep)], axis=0
            )

        tok_away, w_qkv = together(tok_away, w_qkv)
        tok_got = lax.ppermute(tok_away, "seq", swap_x)
        piece_a = with_partner(0)
        piece_a, w_up, w_out, w_down = together(piece_a, w_up, w_out, w_down)
        piece_b, piece_c = with_partner(1), with_partner(2)

        def near_of(lots):
            return [exchange(grid, [lot], axis) for lot, axis in zip(lots, "xy")]

        def widened(lots, near):
            return [joined_parts([lot] + moved) for lot, moved in zip(lots, near)]

        def far_of(wide):
            far = []
            for lot, axis in zip(wide, "yx"):
                far += exchange(grid, [lot], axis)
            return far

        def flat(groups):
            return [part for group in groups for part in group]

        def swapped(parts):
            return [(swap_core(a), s) for a, s in parts]

        def pieces_from(mine, theirs, fields):
            named = lambda parts: [(a, [rel_of(grid, s) for s in spots]) for a, spots in parts]
            return Pieces(chips, named(mine), named(theirs), fields)

        def finish(mine, fields):
            mine = [(a, [rel_of(grid, s) for s in spots]) for a, spots in mine]
            theirs = [(swap_core(a), s) for a, s in mine]
            return Pieces(chips, mine, theirs, fields)

        z_a = gather_along_z(grid, piece_a)
        arrays, tok_got, piece_b = together(arrays_of(z_a), tok_got, piece_b)
        z_a = lots_of(with_arrays(z_a, arrays), 2)
        near_a = near_of(z_a)
        z_b = gather_along_z(grid, piece_b)
        arrays = lax.optimization_barrier(arrays_of(flat(near_a)))
        wide_a = widened(z_a, [[part] for part in with_arrays(flat(near_a), arrays)])
        far_a = far_of(wide_a)
        all_a = wide_a + far_a
        arrays_a, z_own, piece_c, cot_away, cot_own = together(
            arrays_of(all_a), z_b[0][0], piece_c, cot_away, cot_own
        )
        z_b = with_arrays(z_b, [z_own] + arrays_of(z_b[1:]))
        group_a = finish(with_arrays(all_a, arrays_a), fields_a)
        z_b = lots_of(with_arrays(z_b, lax.optimization_barrier(arrays_of(z_b))), grid.nz)
        near_b = exchange(grid, z_b, "x")
        straight_b = exchange(grid, z_b, "y")
        z_c = gather_along_z(grid, piece_c)
    else:
        full = [lax.all_gather(w, AXES, axis=0, tiled=True) for w in (w_qkv, w_out, w_up, w_down, gain_block)]

        def natural(parts, fields):
            sides = []
            for side in range(2):
                cut = [p if p.shape[1] == 128 else p[:, side * (p.shape[1] // 2) : (side + 1) * (p.shape[1] // 2)] for p in parts]
                sides.append([(jnp.concatenate(cut, axis=1)[None], [0])])
            return Pieces(1, sides[0], sides[1], fields)

        group_a = natural([full[0], full[4]], fields_a)
        group_b = natural([full[2], full[1]], fields_b)
        group_c = natural([full[3]], fields_c)
        tok_got = lax.ppermute(tok_away, "seq", swap_x)
        cot_got = lax.ppermute(cot_away, "seq", swap_x)

    sds = jax.ShapeDtypeStruct
    heads = width // HEAD_DIM
    rows_a, rows_c = (2 * w_qkv.shape[0], 2 * w_down.shape[0]) if fast else (width, ff)
    dma = pltpu.SemaphoreType.DMA
    vmem = pltpu.VMEM
    tiles = rows // 256
    tile = lambda columns: pl.BlockSpec((256, columns), lambda i, t: (i, 0))
    own_tile = pl.BlockSpec((256, width), lambda i, t: (jnp.minimum(i, tiles // 2 - 1), 0))
    got_tile = pl.BlockSpec((256, width), lambda i, t: (jnp.maximum(i - tiles // 2, 0), 0))
    chunk = pl.BlockSpec((rows, width), lambda j, t: (0, j))
    low = lambda *shape: sds(shape, BF16)

    packed, normed_first, gains, whole_qkv = call(
        functools.partial(input_kernel, group_a, len(group_a.arrays), chips),
        tab,
        [(tok_own, own_tile), (tok_got, got_tile)],
        group_a.arrays,
        [(pltpu.HBM((rows, 3 * width), BF16), tile(3 * width)), (low(rows, width), tile(width)), (sds((8, width), F32), None),
         (pltpu.HBM((width, 3 * width), BF16), anywhere)],
        [vmem((width, 3 * width), BF16), vmem((width, 128), BF16), dma((group_a.copies(("qkv", "gain")),)), dma((1,))],
        grid=(tiles,),
        cost=2 * rows * width * 3 * width,
    )

    if fast:
        packed, arrays_b, arrays_s, arrays_c, cot_away = together(
            packed, arrays_of(near_b), arrays_of(straight_b), arrays_of(z_c), cot_away
        )
        near_b, straight_b = with_arrays(near_b, arrays_b), with_arrays(straight_b, arrays_s)
        z_c = with_arrays(z_c, arrays_c)
        early_b = z_b + near_b + straight_b
        far_b = exchange(grid, near_b, "y")
        cot_got = lax.ppermute(cot_away, "seq", swap_x)
        their_early_b = swapped(early_b)

    clip_blocks = half // 256
    by_clip = lambda a: a.reshape(2, clip_blocks, 256, a.shape[1])
    clip_shape = low(2, clip_blocks, 256, width)
    step = width // 256
    totals_shape = sds((clip_blocks * heads, 1, 512), F32)

    def attend(first, last, packed, earlier):
        at = lambda base: pl.BlockSpec((2, 1, 256, 256), lambda b, g, t: (0, first + b, 0, base + g))
        totals = pl.BlockSpec((4, 1, 512), lambda b, g, t: ((first + b) * (heads // 4) + g, 0, 0))
        return call(
            functools.partial(attend_kernel, chips),
            tab,
            [(by_clip(packed), at(0)), (by_clip(packed), at(step)), (by_clip(packed), at(2 * step))]
            + [(a, anywhere) for a in earlier],
            [],
            [(clip_shape, at(0)), (totals_shape, totals)],
            [vmem((512, 512), F32)],
            grid=(last - first, heads // 4),
            cost=8 * rows * 512 * width * (last - first) // clip_blocks,
            aliases={4: 0, 5: 1} if earlier else None,
        )

    attended, log_totals = attend(0, clip_blocks, packed, [])
    attended = attended.reshape(rows, width)

    if fast:
        attended, arrays_b, arrays_w, arrays_c, cot_got = together(
            attended, arrays_of(far_b), arrays_of(their_early_b), arrays_of(z_c), cot_got
        )
        far_b, their_early_b = with_arrays(far_b, arrays_b), with_arrays(their_early_b, arrays_w)
        group_b = pieces_from(early_b + far_b, their_early_b + swapped(far_b), fields_b)
        z_c = [joined_parts(with_arrays(z_c, arrays_c))]
        near_c = exchange(grid, z_c, "x")
        straight_c = exchange(grid, z_c, "y")

    hidden, normed_second, whole_out = call(
        functools.partial(middle_kernel, group_b, len(group_b.arrays), chips),
        tab,
        [(attended, tile(width)), (tok_own, own_tile), (tok_got, got_tile), (gains, None)],
        group_b.arrays,
        [
            (sds((rows, width), F32), tile(width)), (low(rows, width), tile(width)),
            (pltpu.HBM((width, width), BF16), anywhere),
        ],
        [vmem((width, width), BF16), dma((group_b.copies(("out",)),)), dma((1,))],
        grid=(tiles,),
        cost=2 * rows * width * width,
    )

    steps = ff // width

    split_up = steps // 2
    wide_hbm = pltpu.HBM((rows, ff), BF16)
    active, slope, whole_up = call(
        functools.partial(up_kernel, group_b, len(group_b.arrays), chips),
        tab,
        [(normed_second, None)],
        group_b.arrays,
        [(wide_hbm, chunk), (wide_hbm, chunk), (pltpu.HBM((width, ff), BF16), anywhere)],
        [vmem((width, ff), BF16), dma((group_b.copies(("up",)),)), dma((1,))],
        grid=(split_up,),
        cost=2 * rows * width * width * split_up,
    )
    if fast:
        active, slope, normed_second, arrays_c, arrays_s = together(
            active, slope, normed_second, arrays_of(near_c), arrays_of(straight_c)
        )
        near_c, straight_c = with_arrays(near_c, arrays_c), with_arrays(straight_c, arrays_s)
        far_c = exchange(grid, near_c, "y")
    rest = pl.BlockSpec((rows, width), lambda j, t: (0, split_up + j))
    active, slope = call(
        up_rest_kernel,
        tab,
        [
            (normed_second, None), (whole_up, pl.BlockSpec((width, width), lambda j, t: (0, split_up + j))),
            (active, anywhere), (slope, anywhere),
        ],
        [],
        [(wide_hbm, rest), (wide_hbm, rest)],
        [],
        grid=(steps - split_up,),
        cost=2 * rows * width * width * (steps - split_up),
        aliases={3: 0, 4: 1},
    )
    if fast:
        early_c = z_c + near_c + straight_c
        active, slope, arrays_c = together(active, slope, arrays_of(early_c))
        early_c = with_arrays(early_c, arrays_c)
        their_early_c = swapped(early_c)
    down_out = low(chips, rows_c, width // 2)
    down_mine, down_other = call(
        functools.partial(down_grad_kernel, chips, rows_c),
        tab,
        [(active, chunk), (cot_own, None), (cot_got, None)],
        [],
        [(down_out, None), (down_out, None)],
        [],
        grid=(steps,),
        cost=2 * rows * width * ff,
    )

    def steps_of(mine, other, cut):
        if fast:
            return scatter_steps(grid, mine, other, cut)

        def plain():
            whole_sum = jnp.concatenate([mine[0], other[0]], axis=1)
            back = yield []
            for _ in range(3):
                back = yield back
            yield lax.psum_scatter(whole_sum, AXES, scatter_dimension=0, tiled=True).astype(F32)

        return plain()

    def owned(total):
        if not fast:
            return total[:, : total.shape[1] // 2], total[:, total.shape[1] // 2 :]
        height = total.shape[0] // 2
        keep = lax.dynamic_slice(total, (core * height, 0), (height, total.shape[1]))
        away = lax.dynamic_slice(total, ((1 - core) * height, 0), (height, total.shape[1]))
        got = swap_core(away.astype(BF16)).astype(F32)
        return jnp.where(core == 0, keep, got), jnp.where(core == 0, got, keep)

    if fast:
        down_mine, down_other, active, arrays_c, arrays_w = together(
            down_mine, down_other, active, arrays_of(far_c), arrays_of(their_early_c)
        )
        far_c, their_early_c = with_arrays(far_c, arrays_c), with_arrays(their_early_c, arrays_w)
        their_far_c = swapped(far_c)
        down_mine, down_other, arrays_w = together(down_mine, down_other, arrays_of(their_far_c))
        group_c = pieces_from(early_c + far_c, their_early_c + with_arrays(their_far_c, arrays_w), fields_c)
    outputs, whole_down = call(
        functools.partial(output_kernel, group_c, len(group_c.arrays), chips),
        tab,
        [(active, tile(ff)), (hidden, tile(width))],
        group_c.arrays,
        [(low(rows, width), tile(width)), (pltpu.HBM((ff, width), BF16), anywhere)],
        [vmem((ff, width), BF16), dma((group_c.copies(("down",)),)), dma((1,))],
        grid=(tiles,),
        cost=2 * rows * width * ff,
    )
    down_sum = steps_of(down_mine, down_other, 2)
    arrived = next(down_sum)
    outputs, arrived, slope = together(outputs, arrived, slope)
    arrived = down_sum.send(arrived)
    def joined(own, back):
        first = mx == 0
        return jnp.concatenate([jnp.where(first, own, back), jnp.where(first, back, own)], axis=0)[None]

    up_part = pl.BlockSpec((chips, rows_a, ff // 2), lambda *_: (0, 0, 0))
    out_part = pl.BlockSpec((chips, rows_a, width // 2), lambda *_: (0, 0, ff // width))
    up_out = low(chips, rows_a, ff // 2 + width // 2)
    grad_up, up_mine, up_other = call(
        functools.partial(down_back_kernel, chips, rows_a),
        tab,
        [
            (cot_own, None), (cot_got, None), (normed_second, None), (slope, chunk),
            (whole_down, pl.BlockSpec((width, width), lambda j, t: (j, 0))),
        ],
        [],
        [(pltpu.HBM((rows, ff), BF16), chunk), (up_out, up_part), (up_out, up_part)],
        [],
        grid=(steps,),
        cost=4 * rows * width * ff,
    )
    grad_up, up_mine, up_other, arrived = together(grad_up, up_mine, up_other, arrived)
    arrived = down_sum.send(arrived)
    quarter = half // 2
    out_first = lax.ppermute(outputs[half : half + quarter], "seq", swap_x)
    grad_hidden, grad_att, up_mine, up_other = call(
        functools.partial(up_back_kernel, chips, rows_a),
        tab,
        [
            (grad_up, tile(ff)), (attended, tile(width)), (gains, None), (cot_own, own_tile), (cot_got, got_tile),
            (hidden, tile(width)), (up_mine, anywhere), (up_other, anywhere),
            (whole_up, None), (whole_out, None),
        ],
        [],
        [(pltpu.HBM((rows, width), F32), tile(width)), (low(rows, width), tile(width)), (up_out, out_part), (up_out, out_part)],
        [vmem((width, width), F32)],
        grid=(tiles,),
        cost=2 * rows * width * ff + 4 * rows * width * width,
        aliases={7: 2, 8: 3},
    )
    grad_att, grad_hidden, up_mine, up_other, arrived, out_first, out_next = together(
        grad_att, grad_hidden, up_mine, up_other, arrived, out_first, outputs[half + quarter :]
    )
    out_second = lax.ppermute(out_next, "seq", swap_x)
    arrived = down_sum.send(arrived)
    up_sum = steps_of(up_mine, up_other, 2)
    arrived_up = next(up_sum)

    groups = heads // 4
    group_cut = max(1, groups // 3)
    cuts = [0, 256 * group_cut, width]

    def attend_back(first, last, grad_att):
        at = lambda base: pl.BlockSpec((2, 1, 256, 256), lambda b, g, t: (0, b, 0, base + first + g))
        to = pl.BlockSpec((2, 1, 256, 256), lambda b, g, t: (0, b, 0, g))
        totals = pl.BlockSpec((4, 1, 512), lambda b, g, t: (b * groups + first + g, 0, 0))
        shape = pltpu.HBM((2, clip_blocks, 256, 256 * (last - first)), BF16)
        grads = call(
            functools.partial(attend_back_kernel, chips),
            tab,
            [
                (by_clip(packed), at(0)), (by_clip(packed), at(step)), (by_clip(packed), at(2 * step)),
                (by_clip(attended), at(0)), (by_clip(grad_att), at(0)), (log_totals, totals),
            ],
            [],
            [(shape, to)] * 3,
            [vmem((512, 512), F32)],
            grid=(clip_blocks, last - first),
            cost=30 * rows * 512 * 256 * (last - first),
        )
        return [g.reshape(rows, 256 * (last - first)) for g in grads]

    grads_a = attend_back(0, group_cut, grad_att)
    grads_a, grad_att, arrived_up, out_second = together(grads_a, grad_att, arrived_up, out_second)
    arrived_up = up_sum.send(arrived_up)
    grads_b = attend_back(group_cut, groups, grad_att)
    grads_b, arrived_up, arrived = together(grads_b, arrived_up, arrived)
    arrived_down = arrived
    arrived_up, grads_b, normed_first = up_sum.send((arrived_up, grads_b, normed_first))
    qkv_out = low(chips, rows_a, 3 * width // 2)
    qkv_mine, qkv_other = call(
        functools.partial(qkv_grad_kernel, chips, rows_a, cuts),
        tab,
        [(normed_first, None)] + [(g, None) for g in grads_a + grads_b],
        [],
        [(qkv_out, None), (qkv_out, None)],
        [],
        cost=2 * rows * width * 3 * width,
        stay=tuple(range(1, 7)),
    )
    qkv_mine, qkv_other, grads_a, grads_b, tok_own, arrived_up = together(
        qkv_mine, qkv_other, grads_a, grads_b, tok_own, arrived_up
    )
    arrived_up, tok_got, qkv_mine, qkv_other = up_sum.send((arrived_up, tok_got, qkv_mine, qkv_other))
    qkv_sum = steps_of(qkv_mine, qkv_other, 2)
    arrived = next(qkv_sum)
    arrived, tok_own = qkv_sum.send((arrived, tok_own))

    grad_own, grad_got = call(
        functools.partial(first_kernel, cuts),
        tab,
        [
            (tok_own, own_tile), (tok_got, got_tile), (gains, None), (grad_hidden, tile(width)), (whole_qkv, None),
        ]
        + [(g, tile(g.shape[1])) for g in grads_a + grads_b],
        [],
        [(low(half, width), own_tile), (low(half, width), got_tile)],
        [],
        grid=(tiles,),
        cost=2 * rows * width * 3 * width,
        stay=(3, 4) + tuple(range(5, 11)),
    )
    grad_got, grad_own, arrived, arrived_up, arrived_down = together(
        grad_got, grad_own, arrived, arrived_up, arrived_down
    )
    arrived = qkv_sum.send(arrived)
    arrived, grad_got = together(arrived, grad_got)
    grad_back = lax.ppermute(grad_got, "seq", swap_x)
    arrived_up, arrived, arrived_down, out_first, out_second = together(
        arrived_up, arrived, arrived_down, out_first, out_second
    )
    arrived = qkv_sum.send(arrived)
    left, right = owned(down_sum.send(arrived_down))
    owned_down = jnp.concatenate([left, right], axis=1)
    left, right = owned(up_sum.send(arrived_up))
    owned_up = jnp.concatenate([left[:, : ff // 2], right[:, : ff // 2]], axis=1)
    owned_out = jnp.concatenate([left[:, ff // 2 :], right[:, ff // 2 :]], axis=1)
    output_tokens = joined(outputs[:half], jnp.concatenate([out_first, out_second], axis=0))
    left, right = owned(qkv_sum.send(arrived))
    owned_qkv = jnp.concatenate([left, right], axis=1)
    grad_tokens = joined(grad_own, grad_back)

    scale = norm_gains.astype(F32)
    first_gain = jnp.sum(w_qkv.astype(F32) * owned_qkv, axis=1) / scale[:, 0]
    second_gain = jnp.sum(w_up.astype(F32) * owned_up, axis=1) / scale[:, 1]
    owned_gains = jnp.stack([first_gain, second_gain], axis=1)
    return (output_tokens, grad_tokens, owned_qkv, owned_out, owned_up, owned_down, owned_gains)


def solution(mesh):
    grid = Grid(mesh.shape["seq"], mesh.shape["clips"])
    shard = P(AXES, None)
    return jax.shard_map(
        functools.partial(body, grid),
        mesh=mesh,
        in_specs=(P("seq", "clips", None), P("clips"), shard, shard, shard, shard, shard, P("seq", "clips", None)),
        out_specs=(P("seq", "clips", None), P("seq", "clips", None), shard, shard, shard, shard, shard),
        check_vma=False,
    )
```
